32 devices in a mesh: section: 2 (over core), dp: 4 (over z), ctx: 4 (over y, x).
Axes of the slice: x: 2, y: 2, z: 4, core: 2. Of those that a mesh axis runs over, the one named last changes fastest.
Arguments:
- tokens: bfloat16 [2, 2048, 768], P(None, ('dp', 'ctx')), may hold values from -6 to 6
- cotangent: bfloat16 [2, 2048, 768], P(None, ('dp', 'ctx')), may hold values from -6 to 6
- seq_bound: int32 [4, 2], P('dp'), may hold values from 0 to 448, as said below
- ln1_gain: float32 [2, 768], P('section'), may hold values from 0.5 to 1.5
- ln1_shift: float32 [2, 768], P('section'), may hold values from -1.5 to 1.5
- w_qkv: bfloat16 [2, 768, 2304], P('section'), may hold values from -0.21875 to 0.21875
- w_out: bfloat16 [2, 768, 768], P('section'), may hold values from -3.5 to 3.5
- ln2_gain: float32 [2, 768], P('section'), may hold values from 0.5 to 1.5
- ln2_shift: float32 [2, 768], P('section'), may hold values from -1.5 to 1.5
- w_up: bfloat16 [2, 768, 3072], P('section'), may hold values from -0.21875 to 0.21875
- w_down: bfloat16 [2, 3072, 768], P('section'), may hold values from -0.3125 to 0.3125
Outputs:
- section_outputs: bfloat16 [2, 2, 2048, 768], P('section', None, ('dp', 'ctx'))
- input_grads: float32 [2, 2, 2048, 768], P('section', None, ('dp', 'ctx'))
- grad_qkv: float32 [2, 1769472], P('section', ('dp', 'ctx'))
- grad_out: float32 [2, 589824], P('section', ('dp', 'ctx'))
- grad_up: float32 [2, 2359296], P('section', ('dp', 'ctx'))
- grad_down: float32 [2, 2359296], P('section', ('dp', 'ctx'))
- grad_norms: float32 [2, 3072], P('section', ('dp', 'ctx'))
The draws below stay inside these ranges and needn't reach their ends.
Inputs may be any that keep to these rules, and one draw needn't show every extreme that they name: `seq_bound`: in every row of slot groups one micro-batch, drawn at random, holds 0, so that its slot is one sequence of 512 positions; every other entry lies between half of 128 and 512 minus half of 128, and some entry equals the latter.
All inputs are finite; a program needn't handle non-finite values.
Results may differ from the reference program's by a relative error of at most 0.023.
Values may be sent and summed in bfloat16 or wider, within the bound.
No kernel may reach another device: no remote copies, remote signals or barrier semaphores. Data moves between devices by JAX's collectives and lax.ppermute only.
A program may use at most 192 MiB of HBM per device.

```python
import math
import jax
import jax.numpy as jnp
from jax import lax

D = 768
HEADS = 12
HEAD_DIM = 64
FF = 3072
S_DEV = 128
MB = 2
SLOT = 512
GROUPS = 4
TOKENS = 2048


def draw_seq_bound(key, part):
    key = jax.random.fold_in(key, 7)
    key_whole, key_cuts, key_row = jax.random.split(key, 3)
    whole_col = jax.random.randint(key_whole, (GROUPS,), 0, MB)
    cuts = jax.random.randint(key_cuts, (GROUPS, MB), S_DEV // 2, SLOT - S_DEV // 2 + 1)
    widest_row = jax.random.randint(key_row, (), 0, GROUPS)
    row_ids = jnp.arange(GROUPS)[:, None]
    col_ids = jnp.arange(MB)[None, :]
    cuts = jnp.where(row_ids == widest_row, SLOT - S_DEV // 2, cuts)
    return jnp.where(col_ids == whole_col[:, None], 0, cuts).astype(jnp.int32)


def steps_of(own_key, extent, cuts, low, largest):
    factor_of = 1.0
    for dim, blocks in cuts:
        draws = jax.random.uniform(jax.random.fold_in(jax.random.fold_in(own_key, 6), dim), (blocks,), jnp.float32, low / len(cuts), largest / len(cuts))
        factor_of = factor_of * jnp.repeat(jnp.exp(draws), extent[dim] // blocks).reshape((-1,) + (1,) * (len(extent) - 1 - dim))
    return factor_of


def normal_values(rng, dims, width, bound, shards=(), kind=jnp.bfloat16):
    drawn = width * jax.random.normal(rng, dims, jnp.float32)
    if shards:
        drawn = drawn * steps_of(rng, dims, shards, -0.22, 0.18)
    return jnp.clip(drawn, -bound, bound).astype(kind)


def setup_inputs(seed: int = 0) -> dict:
    splits = jax.random.split(jax.random.key(seed), 12)
    return {
        "tokens": normal_values(splits[0], (MB, TOKENS, D), 1.0, 6.0, ((1, 16),)),
        "cotangent": normal_values(splits[1], (MB, TOKENS, D), 1.0, 6.0, ((1, 16),)),
        "seq_bound": draw_seq_bound(jax.random.fold_in(splits[11], 71), 0),
        "ln1_gain": jnp.clip(1.0 + 0.1 * jax.random.normal(splits[3], (2, D), jnp.float32), 0.5, 1.5),
        "ln1_shift": normal_values(splits[4], (2, D), 0.3, 1.5, ((0, 2),), jnp.float32),
        "w_qkv": normal_values(splits[5], (2, D, 3 * D), D ** -0.5, 0.21875, ((0, 2),)),
        "w_out": normal_values(splits[6], (2, D, D), (max(D // 256, 1)) ** -0.5, 3.5, ((0, 2),)),
        "ln2_gain": jnp.clip(1.0 + 0.1 * jax.random.normal(splits[7], (2, D), jnp.float32), 0.5, 1.5),
        "ln2_shift": normal_values(splits[8], (2, D), 0.3, 1.5, ((0, 2),), jnp.float32),
        "w_up": normal_values(splits[9], (2, D, FF), D ** -0.5, 0.21875, ((0, 2),)),
        "w_down": normal_values(splits[10], (2, FF, D), (max(FF // 9, 1)) ** -0.5, 0.3125, ((0, 2),)),
    }


@jax.custom_vjp
def low(v):
    return lax.optimization_barrier(v.astype(jnp.bfloat16)).astype(jnp.float32)

@jax.custom_vjp
def low_back(v):
    return v

def low_keep(v):
    return (low(v), None)

def low_pass(kept, grad):
    return (grad,)

def back_keep(v):
    return (v, None)

def back_low(kept, grad):
    return (low(grad),)
low.defvjp(low_keep, low_pass)
low_back.defvjp(back_keep, back_low)
epsilon = 1e-05
rotary_base = 10000.0
masked_score = -1e+30
exact_precision = lax.Precision.HIGHEST

def norm_apply(values, norm_gain, norm_shift):
    centred = values - lax.optimization_barrier(jnp.mean(values, axis=-1, keepdims=True))
    spread = lax.optimization_barrier(jnp.mean(centred * centred, axis=-1, keepdims=True))
    return centred * lax.rsqrt(spread + epsilon) * norm_gain + norm_shift

def rotate(values, angles):
    half_dim = values.shape[-1] // 2
    cosine = jnp.cos(angles)[:, None, :]
    sine = jnp.sin(angles)[:, None, :]
    first_half = values[..., :half_dim]
    second_half = values[..., half_dim:]
    return jnp.concatenate([first_half * cosine - second_half * sine, second_half * cosine + first_half * sine], axis=-1)

def layer_block(values, layer_params, seq_ids, angles):
    gain_one, shift_one, qkv_weight, out_weight, gain_two, shift_two, up_weight, down_weight = layer_params
    length = values.shape[0]
    normed = low(norm_apply(values, gain_one, shift_one))
    mixed = low_back(jnp.dot(normed, qkv_weight, precision=exact_precision))
    queries = low(rotate(mixed[:, :D].reshape(length, HEADS, HEAD_DIM), angles))
    keys_all = low(rotate(mixed[:, D:2 * D].reshape(length, HEADS, HEAD_DIM), angles))
    values_all = low(mixed[:, 2 * D:].reshape(length, HEADS, HEAD_DIM))
    scores = low_back(jnp.einsum('qhd,khd->hqk', queries, keys_all, precision=exact_precision) * HEAD_DIM ** (-0.5))
    same_seq = (seq_ids[:, None] == seq_ids[None, :])[None]
    scores = jnp.where(same_seq, scores, masked_score)
    probs = low(jax.nn.softmax(scores, axis=-1))
    attended = jnp.einsum('hqk,khd->qhd', probs, values_all, precision=exact_precision).reshape(length, D)
    attended = low(low_back(attended))
    hidden = values + low_back(jnp.dot(attended, out_weight, precision=exact_precision))
    normed_two = low(norm_apply(hidden, gain_two, shift_two))
    upward = low_back(jnp.dot(normed_two, up_weight, precision=exact_precision))
    active = low(jax.nn.gelu(upward, approximate=False))
    return hidden + low_back(jnp.dot(active, down_weight, precision=exact_precision))

def reference(tokens, cotangent, seq_bound, ln1_gain, ln1_shift, w_qkv, w_out, ln2_gain, ln2_shift, w_up, w_down):
    stacked = tuple((array.astype(jnp.float32) for array in (ln1_gain, ln1_shift, w_qkv, w_out, ln2_gain, ln2_shift, w_up, w_down)))
    layer_zero = tuple((array[0] for array in stacked))
    layer_one = tuple((array[1] for array in stacked))
    slot_inputs = tokens.reshape(MB * GROUPS, SLOT, D)
    slot_cots = cotangent.reshape(MB * GROUPS, SLOT, D)
    bounds = jnp.transpose(seq_bound).reshape(MB * GROUPS).astype(jnp.int32)
    positions = jnp.arange(SLOT, dtype=jnp.int32)
    freq_steps = jnp.arange(HEAD_DIM // 2, dtype=jnp.float32)
    freqs = jnp.exp(-math.log(rotary_base) * 2.0 * freq_steps / HEAD_DIM)

    def one_slot(totals, inputs):
        slot_x, slot_cot, bound_now = inputs
        seq_ids = (positions >= bound_now).astype(jnp.int32)
        relative = (positions - seq_ids * bound_now).astype(jnp.float32)
        angles = relative[:, None] * freqs[None, :]

        def forward(params_zero, params_one, start_values, offset):
            sent = low(layer_block(start_values, params_zero, seq_ids, angles))
            final = layer_block(low_back(sent) + offset, params_one, seq_ids, angles)
            return (sent, final)
        start_values = slot_x.astype(jnp.float32)
        offset = jnp.zeros_like(start_values)
        (sent, final), pullback = jax.vjp(forward, layer_zero, layer_one, start_values, offset)
        grads_zero, grads_one, grad_start, grad_offset = pullback((jnp.zeros_like(sent), slot_cot.astype(jnp.float32)))
        totals = tuple((total + jnp.stack([first, second]) for total, first, second in zip(totals, grads_zero, grads_one)))
        return (totals, (sent.astype(jnp.bfloat16), final.astype(jnp.bfloat16), grad_start, grad_offset))
    init = tuple((jnp.zeros(array.shape, jnp.float32) for array in stacked))
    totals, (sent_all, final_all, grad_starts, grad_offsets) = lax.scan(one_slot, init, (slot_inputs, slot_cots, bounds))
    section_outputs = jnp.stack([sent_all.reshape(MB, TOKENS, D), final_all.reshape(MB, TOKENS, D)])
    input_grads = jnp.stack([grad_starts.reshape(MB, TOKENS, D), grad_offsets.reshape(MB, TOKENS, D)])
    grad_norms = jnp.concatenate([totals[0], totals[1], totals[4], totals[5]], axis=1)
    return (section_outputs, input_grads, totals[2].reshape(2, -1), totals[3].reshape(2, -1), totals[6].reshape(2, -1), totals[7].reshape(2, -1), grad_norms)
```

```python
import functools
import math

import jax
import jax.numpy as jnp
from jax import lax
from jax.experimental import pallas as pl
from jax.experimental.pallas import tpu as pltpu
from jax.sharding import PartitionSpec as P

HEAD_DIM = 64
HALF = HEAD_DIM // 2
GROUP = 4
LANES = 128
WIDE = 2 * LANES

epsilon = 1e-05
rotary_base = 10000.0
masked_score = -1e30
low = jnp.bfloat16
full = jnp.float32

NT = (((1,), (1,)), ((), ()))
TN = (((0,), (0,)), ((), ()))


def mm(a, b):
    return jnp.dot(a, b, preferred_element_type=full)


def mm_nt(a, b):
    return lax.dot_general(a, b, NT, preferred_element_type=full)


def mm_tn(a, b):
    return lax.dot_general(a, b, TN, preferred_element_type=full)


def norm_stats(values):
    mean = jnp.mean(values, axis=-1, keepdims=True)
    centred = values - mean
    spread = jnp.mean(centred * centred, axis=-1, keepdims=True)
    scale = lax.rsqrt(spread + epsilon)
    return centred * scale, scale


def norm_backward(values, gain, grad):
    hat, scale = norm_stats(values)
    grad_gain = jnp.sum(grad * hat, axis=0, keepdims=True)
    grad_shift = jnp.sum(grad, axis=0, keepdims=True)
    inner = grad * gain
    first = jnp.mean(inner, axis=-1, keepdims=True)
    second = jnp.mean(inner * hat, axis=-1, keepdims=True)
    return scale * (inner - first - hat * second), grad_gain, grad_shift


def gelu_both(u):
    bell = jnp.exp(-0.5 * u * u)
    z = jnp.abs(u) * (0.5**0.5)
    t = 1.0 / (1.0 + 0.3275911 * z)
    poly = t * (
        0.254829592 + t * (-0.284496736 + t * (1.421413741 + t * (-1.453152027 + t * 1.061405429)))
    )
    tail = 0.5 * poly * bell
    cdf = jnp.where(u >= 0, 1.0 - tail, tail)
    return u * cdf, cdf + u * bell * (1.0 / math.sqrt(2.0 * math.pi))


class Fetch:
    def __init__(self, own, other, use_own, place, target, sem):
        self.parts = (own, other, use_own, place, target, sem)

    def start(self):
        own, other, use_own, place, target, sem = self.parts

        @pl.when(use_own)
        def _():
            pltpu.make_async_copy(own.at[place], target, sem).start()

        @pl.when(jnp.logical_not(use_own))
        def _():
            pltpu.make_async_copy(other.at[place], target, sem).start()

    def wait(self):
        own, other, use_own, place, target, sem = self.parts
        pltpu.make_async_copy(own.at[place], target, sem).wait()


def lane_index(shape):
    return lax.broadcasted_iota(jnp.int32, shape, 1)


def half_mask(head):
    return ((lane_index((1, WIDE)) & (LANES - 1)) // HALF) == head


def value_mask(head):
    return (lane_index((1, WIDE)) // HEAD_DIM) == head


def keep(values, mask):
    return jnp.where(mask, values, jnp.zeros_like(values))


def attend_kernel(layer, heads, sc, x0, x1, x2, x3, norms, cos, sin, w_own, w_oth, n1, qkv, probs, a0, a1, a2, a3, w, sem):
    rows = x0.shape[0]
    fetch = Fetch(w_own, w_oth, sc[0] == layer, (slice(None), slice(None)), w, sem.at[0])
    fetch.start()
    gain, shift = norms[0:1, :], norms[1:2, :]
    for k, x in enumerate((x0, x1, x2, x3)):
        hat, _ = norm_stats(x[...].astype(full))
        n1[k * rows : (k + 1) * rows, :] = (hat * gain + shift).astype(low)
    fetch.wait()
    for k in range(GROUP):
        here = slice(k * rows, (k + 1) * rows)
        mixed = mm(n1[here, :], w[...])
        c, s = cos[here, :], sin[here, :]
        for part in range(2):
            base = part * WIDE
            v1, v2 = mixed[:, base : base + LANES], mixed[:, base + LANES : base + WIDE]
            qkv[here, base : base + LANES] = (v1 * c - v2 * s).astype(low)
            qkv[here, base + LANES : base + WIDE] = (v2 * c + v1 * s).astype(low)
        qkv[here, 2 * WIDE :] = mixed[:, 2 * WIDE :].astype(low)
    me, bound = sc[1], sc[2]
    length = GROUP * rows
    spot = lax.broadcasted_iota(jnp.int32, (1, length), 1)
    place = jnp.zeros((1, length), jnp.int32)
    for k in range(GROUP):
        place = jnp.where(spot // rows == k, (me ^ k) * rows + spot - k * rows, place)
    seq_col = (place >= bound).astype(jnp.int32)
    for k, out in enumerate((a0, a1, a2, a3)):
        here = slice(k * rows, (k + 1) * rows)
        own = (me ^ k) * rows + lax.broadcasted_iota(jnp.int32, (rows, 1), 0)
        same = (own >= bound).astype(jnp.int32) == seq_col
        total = jnp.zeros((rows, WIDE), full)
        for h in range(heads):
            q = keep(qkv[here, 0:WIDE], half_mask(h))
            scores = mm_nt(q, qkv[:, WIDE : 2 * WIDE]) * (HEAD_DIM**-0.5)
            scores = jnp.where(same, scores, masked_score)
            top = jnp.max(scores, axis=-1, keepdims=True)
            expo = jnp.where(same, jnp.exp(scores - top), 0.0)
            p = (expo * (1.0 / jnp.sum(expo, axis=-1, keepdims=True))).astype(low)
            probs[h, here, :] = p
            total = total + mm(p, keep(qkv[:, 2 * WIDE :], value_mask(h)))
        out[...] = total[:, : heads * HEAD_DIM].astype(low)


def attend_back_kernel(layer, heads, sc, g0, g1, g2, g3, qkv, probs, cos, sin, wo_own, wo_oth, w_own, w_oth, gmixed, p0, p1, p2, p3, wo, w, go, gs, qm, gom, sem):
    rows = g0.shape[0]
    width = heads * HEAD_DIM
    me = sc[1]
    mine = sc[0] == layer
    span = pl.ds(pl.multiple_of(me * width, HEAD_DIM), width)
    fetch_o = Fetch(wo_own, wo_oth, mine, (span, slice(None)), wo, sem.at[0])
    fetch_w = Fetch(w_own, w_oth, mine, (slice(None), slice(None)), w, sem.at[1])
    fetch_o.start()
    fetch_w.start()
    fetch_o.wait()
    length = GROUP * rows
    go[:, LANES:] = jnp.zeros((length, WIDE - LANES), low)
    for k, g in enumerate((g0, g1, g2, g3)):
        go[k * rows : (k + 1) * rows, :width] = mm_nt(g[...], wo[...]).astype(low)
    for k in range(GROUP):
        here = slice(k * rows, (k + 1) * rows)
        total = jnp.zeros((rows, WIDE), full)
        for h in range(heads):
            there = slice(h * length + k * rows, h * length + (k + 1) * rows)
            g = keep(go[here, :], value_mask(h))
            gom[there, :] = g
            qm[there, :] = keep(qkv[here, 0:WIDE], half_mask(h))
            gp = mm_nt(g, qkv[:, 2 * WIDE :])
            p = probs[h, here, :].astype(full)
            inner = jnp.sum(p * gp, axis=-1, keepdims=True)
            grad = (p * (gp - inner)).astype(low)
            gs[there, :] = grad
            total = total + mm(grad, keep(qkv[:, WIDE : 2 * WIDE], half_mask(h)))
        total = total * (HEAD_DIM**-0.5)
        c, s = cos[here, :], sin[here, :]
        v1, v2 = total[:, :LANES], total[:, LANES:]
        gmixed[here, 0:LANES] = (v1 * c + v2 * s).astype(low)
        gmixed[here, LANES:WIDE] = (v2 * c - v1 * s).astype(low)
    for k in range(GROUP):
        here = slice(k * rows, (k + 1) * rows)
        gk = mm_tn(gs[:, here], qm[...]) * (HEAD_DIM**-0.5)
        c, s = cos[here, :], sin[here, :]
        v1, v2 = gk[:, :LANES], gk[:, LANES:]
        gmixed[here, WIDE : WIDE + LANES] = (v1 * c + v2 * s).astype(low)
        gmixed[here, WIDE + LANES : 2 * WIDE] = (v2 * c - v1 * s).astype(low)
        gv = jnp.zeros((rows, WIDE), full)
        for h in range(heads):
            gv = gv + mm_tn(probs[h, :, here], gom[h * length : (h + 1) * length, :])
        gmixed[here, 2 * WIDE :] = gv.astype(low)
    fetch_w.wait()
    for k, out in enumerate((p0, p1, p2, p3)):
        out[...] = mm_nt(gmixed[k * rows : (k + 1) * rows, :], w[...]).astype(low)


class FeedWeights:
    def __init__(self, mine, up_own, up_oth, dn_own, dn_oth, wu, wd, sem, first):
        width = wu.shape[1]
        self.wu, self.wd = wu, wd
        self.up, self.down = [], []
        for j in range(GROUP):
            cut = slice(j * width, (j + 1) * width)
            self.up.append(Fetch(up_own, up_oth, mine, (slice(None), cut), wu.at[j], sem.at[first + j]))
            self.down.append(Fetch(dn_own, dn_oth, mine, (cut, slice(None)), wd.at[j], sem.at[first + GROUP + j]))


def feed_forward(me, x, atts, norms, fetch_o, wo, feed, shards, y, hidden, slope, messages, parts, cols):
    rows, width = x.shape
    heads_wide = atts[0].shape[1]
    for k in range(GROUP):
        fetch_o[k].wait()
    state = x[...].astype(full)
    for k in range(GROUP):
        state = state + mm(atts[k][...], wo[k])
        cols[me ^ k] = atts[k][...]
    hidden[...] = state
    hat, _ = norm_stats(state)
    n2 = (hat * norms[2:3, :] + norms[3:4, :]).astype(low)
    for message in messages:
        message[:, 0:width] = n2
    step = width // (GROUP * shards)
    for target in range(GROUP):
        pieces = []
        for z in range(shards):
            at = (z * GROUP + target) * step
            pieces.append(cols[at // heads_wide, :, at % heads_wide : at % heads_wide + step])
        pieces.append(jnp.zeros((rows, WIDE - heads_wide), low))
        parts[target, :, width : width + WIDE] = jnp.concatenate(pieces, axis=1)
    out = jnp.zeros((rows, width), full)
    chunk = feed.wu.shape[2]
    for j in range(GROUP):
        feed.up[j].wait()
        act, grad = gelu_both(mm(n2, feed.wu[j]))
        act = act.astype(low)
        slope[:, j * chunk : (j + 1) * chunk] = grad.astype(low)
        feed.down[j].wait()
        out = out + mm(act, feed.wd[j])
        span = chunk * GROUP // (GROUP * shards)
        for b in range(chunk // span):
            z, target = divmod(j * (chunk // span) + b, GROUP)
            parts[target, :, z * span : (z + 1) * span] = act[:, b * span : (b + 1) * span]
    y[...] = (hidden[...] + out).astype(low)
    for k, message in enumerate(messages):
        message[:, width : 2 * width + WIDE] = parts[me ^ k]


def feed_back(me, gf, grad_out, norms, feed, hidden, slope, ga, gh, dnorm, messages, offset, gu, waited):
    rows, width = gf.shape
    chunk = feed.wu.shape[2]
    grad = jnp.zeros((rows, width), full)
    for j in range(GROUP):
        if not waited:
            feed.down[j].wait()
        got = mm_nt(gf, feed.wd[j]) * slope[:, j * chunk : (j + 1) * chunk].astype(full)
        got = got.astype(low)
        gu[j] = got
        if not waited:
            feed.up[j].wait()
        grad = grad + mm_nt(got, feed.wu[j])
    back, d_gain, d_shift = norm_backward(hidden[...], norms[2:3, :], grad)
    total = grad_out + back
    gh[...] = total
    ga[...] = total.astype(low)
    dnorm[0:1, :] = d_gain
    dnorm[1:2, :] = d_shift
    for k, message in enumerate(messages):
        message[:, offset : offset + width] = gf
        message[:, offset + width : offset + 2 * width] = gu[me ^ k]


def start_out(sc, mine, wo_own, wo_oth, wo, sem):
    width = wo.shape[1]
    out = []
    for k in range(GROUP):
        span = pl.ds(pl.multiple_of((sc[1] ^ k) * width, HEAD_DIM), width)
        out.append(Fetch(wo_own, wo_oth, mine, (span, slice(None)), wo.at[k], sem.at[k]))
    return out


def feed_kernel(layer, shards, sc, x, a0, a1, a2, a3, norms, wo_own, wo_oth, up_own, up_oth, dn_own, dn_oth, y, hidden, slope, m0, m1, m2, m3, wo, wu, wd, parts, cols, sem):
    mine = sc[0] == layer
    fetch_o = start_out(sc, mine, wo_own, wo_oth, wo, sem)
    feed = FeedWeights(mine, up_own, up_oth, dn_own, dn_oth, wu, wd, sem, GROUP)
    for f in fetch_o + [f for pair in zip(feed.up, feed.down) for f in pair]:
        f.start()
    feed_forward(sc[1], x, (a0, a1, a2, a3), norms, fetch_o, wo, feed, shards, y, hidden, slope, (m0, m1, m2, m3), parts, cols)


def feed_turn_kernel(layer, shards, sc, x, a0, a1, a2, a3, norms, cot, wo_own, wo_oth, up_own, up_oth, dn_own, dn_oth, y, ga, gh, dnorm, m0, m1, m2, m3, wo, wu, wd, parts, cols, hidden, slope, gu, sem):
    mine = sc[0] == layer
    fetch_o = start_out(sc, mine, wo_own, wo_oth, wo, sem)
    feed = FeedWeights(mine, up_own, up_oth, dn_own, dn_oth, wu, wd, sem, GROUP)
    for f in fetch_o + [f for pair in zip(feed.up, feed.down) for f in pair]:
        f.start()
    messages = (m0, m1, m2, m3)
    feed_forward(sc[1], x, (a0, a1, a2, a3), norms, fetch_o, wo, feed, shards, y, hidden, slope, messages, parts, cols)
    gf = cot[...]
    feed_back(sc[1], gf, gf.astype(full), norms, feed, hidden, slope, ga, gh, dnorm, messages, 2 * gf.shape[1] + WIDE, gu, True)


def turn_kernel(layer, sc, r0, r1, r2, r3, gh_in, x_in, norms_in, hidden, slope, norms, up_own, up_oth, dn_own, dn_oth, gx, dnorm_in, ga, gh, dnorm, m0, m1, m2, m3, wu, wd, gu, sem):
    mine = sc[0] == layer
    feed = FeedWeights(mine, up_own, up_oth, dn_own, dn_oth, wu, wd, sem, 0)
    for f in [f for pair in zip(feed.down, feed.up) for f in pair]:
        f.start()
    top = first_norm_back(r0, r1, r2, r3, gh_in, x_in, norms_in, gx, dnorm_in)
    gf = top.astype(low)
    feed_back(sc[1], gf, gf.astype(full), norms, feed, hidden, slope, ga, gh, dnorm, (m0, m1, m2, m3), 0, gu, False)


def first_norm_back(r0, r1, r2, r3, gh_in, x_in, norms_in, gx, dnorm):
    grad = r0[...].astype(full) + r1[...].astype(full) + r2[...].astype(full) + r3[...].astype(full)
    back, d_gain, d_shift = norm_backward(x_in[...].astype(full), norms_in[0:1, :], grad)
    dnorm[0:1, :] = d_gain
    dnorm[1:2, :] = d_shift
    total = gh_in[...] + back
    gx[...] = total
    return total


def last_kernel(r0, r1, r2, r3, gh_in, x_in, norms_in, gx, dnorm):
    first_norm_back(r0, r1, r2, r3, gh_in, x_in, norms_in, gx, dnorm)


def tall_product(left, right, out, step):
    @pl.loop(0, left.shape[1] // step)
    def _(i):
        cut = pl.ds(pl.multiple_of(i * step, step), step)
        out[cut, :] = mm_tn(left[:, cut], right[...]).astype(out.dtype)


def feed_grads_kernel(split, *refs):
    if split:
        fwd, bwd, (g_up, g_down, a, b) = refs[:GROUP], refs[GROUP : 2 * GROUP], refs[2 * GROUP :]
        base = 0
    else:
        fwd, (g_up, g_down, a, b) = refs[:GROUP], refs[GROUP:]
        bwd, base = fwd, 2 * g_up.shape[0] + WIDE
    rows, width = fwd[0].shape[0], g_up.shape[0]
    for k in range(GROUP):
        here = slice(k * rows, (k + 1) * rows)
        a[here, :] = fwd[k][:, 0:width]
        b[here, :] = bwd[k][:, base + width : base + 2 * width]
    tall_product(a, b, g_up, WIDE)
    for k in range(GROUP):
        here = slice(k * rows, (k + 1) * rows)
        a[here, :] = fwd[k][:, width : 2 * width]
        b[here, :] = bwd[k][:, base : base + width]
    tall_product(a, b, g_down, WIDE)


def attend_grads_kernel(n1, gmixed, m0, m1, m2, m3, g0, g1, g2, g3, g_qkv, g_out, a, b):
    rows, width = g0.shape
    tall_product(n1, gmixed, g_qkv, WIDE)
    for k, (m, g) in enumerate(zip((m0, m1, m2, m3), (g0, g1, g2, g3))):
        here = slice(k * rows, (k + 1) * rows)
        a[here, :] = m[:, 2 * width : 2 * width + WIDE]
        b[here, :] = g[...]
    g_out[...] = mm_tn(a[...], b[...])[: g_out.shape[0], :].astype(low)


def run(kernel, shapes, scratch, operands, spaces, flops=0, moved=0):
    place = {"s": pltpu.SMEM, "v": pltpu.VMEM, "a": pl.ANY}
    return pl.pallas_call(
        kernel,
        out_shape=[jax.ShapeDtypeStruct(shape, kind) for shape, kind in shapes],
        in_specs=[pl.BlockSpec(memory_space=place[space]) for space in spaces],
        out_specs=[pl.BlockSpec(memory_space=pltpu.VMEM) for _ in shapes],
        scratch_shapes=scratch,
        compiler_params=pltpu.CompilerParams(vmem_limit_bytes=56 * 2**20),
        cost_estimate=pl.CostEstimate(flops=flops, bytes_accessed=moved, transcendentals=0),
    )(*operands)


def exchange(value):
    values = value if isinstance(value, (list, tuple)) else [value] * GROUP
    return [values[0]] + [
        lax.ppermute(values[k], "ctx", [(i, i ^ k) for i in range(GROUP)]) for k in range(1, GROUP)
    ]


def swap(value):
    return lax.ppermute(value, "section", [(0, 1), (1, 0)])


def rotary_tables(me, bound, rows):
    spot = jnp.arange(GROUP * rows, dtype=jnp.int32)
    place = (me ^ (spot // rows)) * rows + spot % rows
    relative = (place - jnp.where(place >= bound, bound, 0)).astype(full)
    steps = (jnp.arange(LANES, dtype=jnp.int32) % HALF).astype(full)
    freqs = jnp.exp(-math.log(rotary_base) * 2.0 * steps / HEAD_DIM)
    angles = relative[:, None] * freqs[None, :]
    return jnp.cos(angles), jnp.sin(angles)


def chosen_columns(me, width, heads):
    t = jnp.arange(3 * WIDE, dtype=jnp.int32)
    part, u = t // WIDE, t % WIDE
    half, v = u // LANES, u % LANES
    rotated = part * width + (me * heads + v // HALF) * HEAD_DIM + half * HALF + v % HALF
    plain = 2 * width + me * heads * HEAD_DIM + u
    return jnp.where(
        part < 2,
        jnp.where(v < heads * HALF, rotated, -1),
        jnp.where(u < heads * HEAD_DIM, plain, -1),
    )


def along_dp(layer, own, other):
    count = lax.axis_size("dp")
    z = lax.axis_index("dp")
    total = own.astype(full) + other.astype(full)
    blocks = total.reshape((count, total.shape[0] // count) + total.shape[1:])
    if count > 8:
        return lax.psum_scatter(blocks.astype(low), "dp", scatter_dimension=0, tiled=False).astype(full)
    result = lax.dynamic_index_in_dim(blocks, z, 0, keepdims=False)
    for k in range(1, count):
        block = lax.dynamic_index_in_dim(blocks, lax.rem(z + k, count), 0, keepdims=False).astype(low)
        pairs = [(layer * count + i, layer * count + (i + k) % count) for i in range(count)]
        result = result + lax.ppermute(block, ("section", "dp"), pairs).astype(full)
    return result


def on_device(tokens, cotangent, seq_bound, ln1_gain, ln1_shift, w_qkv, w_out, ln2_gain, ln2_shift, w_up, w_down):
    section = lax.axis_index("section")
    me = lax.axis_index("ctx")
    shards = lax.axis_size("dp")
    z = lax.axis_index("dp")
    rows, width = tokens.shape[1:]
    feed_width = w_up.shape[2]
    chunk = feed_width // GROUP
    heads = width // HEAD_DIM // GROUP
    mine_wide = heads * HEAD_DIM
    length = GROUP * rows
    bound = lax.dynamic_index_in_dim(seq_bound[0], section, 0, keepdims=False)
    sc = jnp.stack([section, me, bound]).astype(jnp.int32)

    x = lax.dynamic_index_in_dim(tokens, section, 0, keepdims=False)
    cot = lax.dynamic_index_in_dim(cotangent, section, 0, keepdims=False)
    gathered = exchange(x)

    norms_own = jnp.concatenate([ln1_gain, ln1_shift, ln2_gain, ln2_shift], axis=0)
    norms_oth = swap(norms_own)
    norms = [jnp.where(section == layer, norms_own, norms_oth) for layer in range(2)]
    pick = chosen_columns(me, width, heads)
    select = (jnp.arange(3 * width, dtype=jnp.int32)[:, None] == pick[None, :]).astype(low)
    wq_own = mm(w_qkv[0], select).astype(low)
    wq_oth = swap(wq_own)
    wo_own, up_own, dn_own = w_out[0], w_up[0], w_down[0]
    wo_oth, up_oth, dn_oth = swap(wo_own), swap(up_own), swap(dn_own)
    cos, sin = rotary_tables(me, bound, rows)

    dma = pltpu.SemaphoreType.DMA
    vm = pltpu.VMEM
    piece = ((rows, width), low)

    def attend(layer, gathered):
        return run(
            functools.partial(attend_kernel, layer, heads),
            [((length, width), low), ((length, 3 * WIDE), low), ((heads, length, length), low)] + [((rows, mine_wide), low)] * GROUP,
            [vm((width, 3 * WIDE), low), dma((1,))],
            (sc, *gathered, norms[layer], cos, sin, wq_own, wq_oth),
            "svvvvvvvaa",
            flops=2 * length * width * 3 * WIDE * 2, moved=8 * 2**20,
        )

    def attend_back(layer, grads, qkv, probs):
        return run(
            functools.partial(attend_back_kernel, layer, heads),
            [((length, 3 * WIDE), low)] + [piece] * GROUP,
            [
                vm((mine_wide, width), low), vm((width, 3 * WIDE), low), vm((length, WIDE), low),
                vm((heads * length, length), low), vm((heads * length, WIDE), low), vm((heads * length, WIDE), low), dma((2,)),
            ],
            (sc, *grads, qkv, probs, cos, sin, wo_own, wo_oth, wq_own, wq_oth),
            "svvvvvvvvaaaa",
            flops=2 * length * width * 3 * WIDE * 3, moved=8 * 2**20,
        )

    feed_scratch = [vm((GROUP, width, chunk), low), vm((GROUP, chunk, width), low)]
    out_scratch = vm((GROUP, mine_wide, width), low)
    split_scratch = [vm((GROUP, rows, width + WIDE), low), vm((GROUP, rows, mine_wide), low)]
    weights = (wo_own, wo_oth, up_own, up_oth, dn_own, dn_oth)

    n1_0, qkv_0, probs_0, *att = attend(0, gathered)
    att = exchange(att)
    y0, hidden_0, slope_0, *fwd_0 = run(
        functools.partial(feed_kernel, 0, shards),
        [piece, ((rows, width), full), ((rows, feed_width), low)] + [((rows, 2 * width + WIDE), low)] * GROUP,
        [out_scratch, *feed_scratch, *split_scratch, dma((3 * GROUP,))],
        (sc, x, *att, norms[0], *weights),
        "svvvvvvaaaaaa",
        flops=4 * rows * width * feed_width, moved=14 * 2**20,
    )
    gathered_1 = exchange(y0)
    fwd_0 = exchange(fwd_0)
    n1_1, qkv_1, probs_1, *att = attend(1, gathered_1)
    att = exchange(att)
    y1, ga, gh_1, dn2_1, *both_1 = run(
        functools.partial(feed_turn_kernel, 1, shards),
        [piece, piece, ((rows, width), full), ((2, width), full)] + [((rows, 4 * width + WIDE), low)] * GROUP,
        [
            out_scratch, *feed_scratch, *split_scratch, vm((rows, width), full), vm((rows, feed_width), low),
            vm((GROUP, rows, chunk), low), dma((3 * GROUP,)),
        ],
        (sc, y0, *att, norms[1], cot, *weights),
        "svvvvvvvaaaaaa",
        flops=8 * rows * width * feed_width, moved=14 * 2**20,
    )
    ga_1 = exchange(ga)
    both_1 = exchange(both_1)
    gmixed_1, *back = attend_back(1, ga_1, qkv_1, probs_1)
    back = exchange(back)
    gx_1, dn1_1, ga, gh_0, dn2_0, *bwd_0 = run(
        functools.partial(turn_kernel, 0),
        [((rows, width), full), ((2, width), full), piece, ((rows, width), full), ((2, width), full)]
        + [((rows, 2 * width), low)] * GROUP,
        [*feed_scratch, vm((GROUP, rows, chunk), low), dma((2 * GROUP,))],
        (sc, *back, gh_1, y0, norms[1], hidden_0, slope_0, norms[0], up_own, up_oth, dn_own, dn_oth),
        "svvvvvvvvvvaaaa",
        flops=4 * rows * width * feed_width, moved=12 * 2**20,
    )
    ga_0 = exchange(ga)
    bwd_0 = exchange(bwd_0)
    gmixed_0, *back = attend_back(0, ga_0, qkv_0, probs_0)
    back = exchange(back)
    gx_0, dn1_0 = run(
        last_kernel,
        [((rows, width), full), ((2, width), full)],
        [],
        (*back, gh_0, x, norms[0]),
        "vvvvvvv",
        moved=2**20,
    )

    def grads_of(layer, messages, n1, gmixed, ga):
        square = ((width, width), low)
        stage = [vm((length, width), low), vm((length, width), low)]
        g_up, g_down = run(
            functools.partial(feed_grads_kernel, len(messages) > GROUP),
            [((width, chunk), low), ((chunk, width), low)], stage, messages, "v" * len(messages),
            flops=4 * length * width * chunk, moved=8 * 2**20,
        )
        g_qkv, g_out = run(
            attend_grads_kernel,
            [((width, 3 * WIDE), low), ((mine_wide, width), low)],
            [vm((length, WIDE), low), vm((length, width), low)],
            (n1, gmixed, *messages[:GROUP], *ga), "v" * (2 + 2 * GROUP),
            flops=2 * length * width * width, moved=8 * 2**20,
        )
        totals = []
        for g in (g_up, g_down, g_out, g_qkv):
            other = lax.ppermute(g, "section", [(1 - layer, layer)])
            totals.append(along_dp(layer, g, other))
        return totals

    totals_1 = grads_of(1, both_1, n1_1, gmixed_1, ga_1)
    totals_0 = grads_of(0, fwd_0 + bwd_0, n1_0, gmixed_0, ga_0)
    t_up, t_down, t_out, t_qkv = (
        jnp.where(section == 0, first, second) for first, second in zip(totals_0, totals_1)
    )
    slim = jnp.concatenate([t_up, t_qkv], axis=1).astype(low)
    slim = slim.reshape(GROUP, slim.shape[0] // GROUP, slim.shape[1])
    sends = [lax.dynamic_index_in_dim(slim, me ^ k, 0, keepdims=False) for k in range(GROUP)]
    gets = jnp.stack(exchange(sends))
    gets = jnp.stack([lax.dynamic_index_in_dim(gets, me ^ k, 0, keepdims=False) for k in range(GROUP)]).astype(full)
    few = gets.shape[1]
    grad_up = jnp.transpose(gets[:, :, :chunk], (1, 0, 2)).reshape(1, -1)
    cols = gets[:, :, chunk:].reshape(GROUP, few, 3, WIDE)
    turned = cols[:, :, :2].reshape(GROUP, few, 2, 2, LANES)[..., : heads * HALF]
    turned = turned.reshape(GROUP, few, 2, 2, heads, HALF).transpose(1, 2, 0, 4, 3, 5).reshape(few, 2 * width)
    plain = cols[:, :, 2, :mine_wide].transpose(1, 0, 2).reshape(few, width)
    grad_qkv = jnp.concatenate([turned, plain], axis=1).reshape(1, -1)
    grad_down = t_down.reshape(1, -1)
    grad_out = t_out.reshape(1, -1)

    small = [jnp.concatenate([dn1_0, dn2_0]), jnp.concatenate([dn1_1, dn2_1])]
    small = jnp.where(section == 0, small[0], small[1]) + swap(jnp.where(section == 0, small[1], small[0]))
    small = small.reshape(shards * GROUP, -1)
    grad_norms = lax.psum_scatter(small, ("dp", "ctx"), scatter_dimension=0, tiled=True)

    def by_section(first, second):
        own = jnp.where(section == 0, first, second)
        got = swap(jnp.where(section == 0, second, first))
        return jnp.where(section == 0, jnp.stack([own, got]), jnp.stack([got, own]))[None]

    return (
        by_section(y0, y1),
        by_section(gx_0, gx_1),
        grad_qkv,
        grad_out,
        grad_up,
        grad_down,
        grad_norms,
    )


def solution(mesh):
    in_specs = (
        P(None, ("dp", "ctx"), None),
        P(None, ("dp", "ctx"), None),
        P("dp", None),
        P("section", None),
        P("section", None),
        P("section", None, None),
        P("section", None, None),
        P("section", None),
        P("section", None),
        P("section", None, None),
        P("section", None, None),
    )
    out_specs = (
        P("section", None, ("dp", "ctx"), None),
        P("section", None, ("dp", "ctx"), None),
        P("section", ("dp", "ctx")),
        P("section", ("dp", "ctx")),
        P("section", ("dp", "ctx")),
        P("section", ("dp", "ctx")),
        P("section", ("dp", "ctx")),
    )
    return jax.shard_map(
        on_device, mesh=mesh, in_specs=in_specs, out_specs=out_specs, check_vma=False
    )
```

```python
import functools
import math

import jax
import jax.numpy as jnp
from jax import lax
from jax.experimental import pallas as pl
from jax.experimental.pallas import tpu as pltpu
from jax.sharding import PartitionSpec as P

HEAD_DIM = 64
HALF = HEAD_DIM // 2
GROUP = 4
LANES = 128
WIDE = 2 * LANES

epsilon = 1e-05
rotary_base = 10000.0
masked_score = -1e30
low = jnp.bfloat16
full = jnp.float32

NT = (((1,), (1,)), ((), ()))
TN = (((0,), (0,)), ((), ()))


def mm(a, b):
    return jnp.dot(a, b, preferred_element_type=full)


def mm_nt(a, b):
    return lax.dot_general(a, b, NT, preferred_element_type=full)


def mm_tn(a, b):
    return lax.dot_general(a, b, TN, preferred_element_type=full)


def norm_stats(values):
    mean = jnp.mean(values, axis=-1, keepdims=True)
    centred = values - mean
    spread = jnp.mean(centred * centred, axis=-1, keepdims=True)
    scale = lax.rsqrt(spread + epsilon)
    return centred * scale, scale


def norm_backward(values, gain, grad):
    hat, scale = norm_stats(values)
    grad_gain = jnp.sum(grad * hat, axis=0, keepdims=True)
    grad_shift = jnp.sum(grad, axis=0, keepdims=True)
    inner = grad * gain
    first = jnp.mean(inner, axis=-1, keepdims=True)
    second = jnp.mean(inner * hat, axis=-1, keepdims=True)
    return scale * (inner - first - hat * second), grad_gain, grad_shift


def gelu_both(u):
    bell = jnp.exp(-0.5 * u * u)
    z = jnp.abs(u) * (0.5**0.5)
    t = 1.0 / (1.0 + 0.3275911 * z)
    poly = t * (
        0.254829592 + t * (-0.284496736 + t * (1.421413741 + t * (-1.453152027 + t * 1.061405429)))
    )
    tail = 0.5 * poly * bell
    cdf = jnp.where(u >= 0, 1.0 - tail, tail)
    return u * cdf, cdf + u * bell * (1.0 / math.sqrt(2.0 * math.pi))


class Fetch:
    def __init__(self, own, other, use_own, place, target, sem):
        self.parts = (own, other, use_own, place, target, sem)

    def start(self):
        own, other, use_own, place, target, sem = self.parts

        @pl.when(use_own)
        def _():
            pltpu.make_async_copy(own.at[place], target, sem).start()

        @pl.when(jnp.logical_not(use_own))
        def _():
            pltpu.make_async_copy(other.at[place], target, sem).start()

    def wait(self):
        own, other, use_own, place, target, sem = self.parts
        pltpu.make_async_copy(own.at[place], target, sem).wait()


def lane_index(shape):
    return lax.broadcasted_iota(jnp.int32, shape, 1)


def half_mask(head):
    return ((lane_index((1, WIDE)) & (LANES - 1)) // HALF) == head


def value_mask(head):
    return (lane_index((1, WIDE)) // HEAD_DIM) == head


def keep(values, mask):
    return jnp.where(mask, values, jnp.zeros_like(values))


class ProjectionWeights:
    def __init__(self, me, heads, mine, own, other, windows, target, sem):
        total = own.shape[0]
        at = me * (heads * HEAD_DIM)
        self.shift = lax.rem(at, LANES)
        start = at - self.shift
        self.windows, self.target, self.heads = windows, target, heads
        self.parts = []
        for part in range(3):
            span = pl.ds(pl.multiple_of(part * total + start, LANES), WIDE)
            self.parts.append(Fetch(own, other, mine, (slice(None), span), windows.at[part], sem.at[part]))

    def start(self):
        for part in self.parts:
            part.start()

    def wait(self):
        shape = (WIDE, WIDE)
        source, u = lax.broadcasted_iota(jnp.int32, shape, 0), lane_index(shape)
        v = u & (LANES - 1)
        turned = jnp.where(v < self.heads * HALF, (v // HALF) * HEAD_DIM + (u // LANES) * HALF + (v & (HALF - 1)) + self.shift, -1)
        plain = jnp.where(u < self.heads * HEAD_DIM, u + self.shift, -1)
        turned = jnp.where(source == turned, 1.0, 0.0).astype(low)
        plain = jnp.where(source == plain, 1.0, 0.0).astype(low)
        for part in range(3):
            self.parts[part].wait()
            chosen = mm(self.windows[part], plain if part == 2 else turned)
            self.target[:, part * WIDE : (part + 1) * WIDE] = chosen.astype(low)


def attend_kernel(layer, heads, sc, x0, x1, x2, x3, norms, cos, sin, w_own, w_oth, n1, qkv, probs, a0, a1, a2, a3, win, w, sem):
    rows = x0.shape[0]
    weights = ProjectionWeights(sc[1], heads, sc[0] == layer, w_own, w_oth, win, w, sem)
    weights.start()
    gain, shift = norms[0:1, :], norms[1:2, :]
    for k, x in enumerate((x0, x1, x2, x3)):
        hat, _ = norm_stats(x[...].astype(full))
        n1[k * rows : (k + 1) * rows, :] = (hat * gain + shift).astype(low)
    weights.wait()
    for k in range(GROUP):
        here = slice(k * rows, (k + 1) * rows)
        mixed = mm(n1[here, :], w[...])
        c, s = cos[here, :], sin[here, :]
        for part in range(2):
            base = part * WIDE
            v1, v2 = mixed[:, base : base + LANES], mixed[:, base + LANES : base + WIDE]
            qkv[here, base : base + LANES] = (v1 * c - v2 * s).astype(low)
            qkv[here, base + LANES : base + WIDE] = (v2 * c + v1 * s).astype(low)
        qkv[here, 2 * WIDE :] = mixed[:, 2 * WIDE :].astype(low)
    me, bound = sc[1], sc[2]
    length = GROUP * rows
    spot = lax.broadcasted_iota(jnp.int32, (1, length), 1)
    place = jnp.zeros((1, length), jnp.int32)
    for k in range(GROUP):
        place = jnp.where(spot // rows == k, (me ^ k) * rows + spot - k * rows, place)
    seq_col = (place >= bound).astype(jnp.int32)
    for k, out in enumerate((a0, a1, a2, a3)):
        here = slice(k * rows, (k + 1) * rows)
        own = (me ^ k) * rows + lax.broadcasted_iota(jnp.int32, (rows, 1), 0)
        same = (own >= bound).astype(jnp.int32) == seq_col
        total = jnp.zeros((rows, WIDE), full)
        for h in range(heads):
            q = keep(qkv[here, 0:WIDE], half_mask(h))
            scores = mm_nt(q, qkv[:, WIDE : 2 * WIDE]) * (HEAD_DIM**-0.5)
            scores = jnp.where(same, scores, masked_score)
            top = jnp.max(scores, axis=-1, keepdims=True)
            expo = jnp.where(same, jnp.exp(scores - top), 0.0)
            p = (expo * (1.0 / jnp.sum(expo, axis=-1, keepdims=True))).astype(low)
            probs[h, here, :] = p
            total = total + mm(p, keep(qkv[:, 2 * WIDE :], value_mask(h)))
        out[...] = total[:, : heads * HEAD_DIM].astype(low)


def attend_back_kernel(layer, heads, sc, g0, g1, g2, g3, qkv, probs, cos, sin, wo_own, wo_oth, w_own, w_oth, gmixed, p0, p1, p2, p3, wo, win, w, go, gs, qm, gom, sem):
    rows = g0.shape[0]
    width = heads * HEAD_DIM
    me = sc[1]
    mine = sc[0] == layer
    span = pl.ds(pl.multiple_of(me * width, HEAD_DIM), width)
    fetch_o = Fetch(wo_own, wo_oth, mine, (span, slice(None)), wo, sem.at[3])
    fetch_w = ProjectionWeights(me, heads, mine, w_own, w_oth, win, w, sem)
    fetch_o.start()
    fetch_w.start()
    fetch_o.wait()
    length = GROUP * rows
    go[:, LANES:] = jnp.zeros((length, WIDE - LANES), low)
    for k, g in enumerate((g0, g1, g2, g3)):
        go[k * rows : (k + 1) * rows, :width] = mm_nt(g[...], wo[...]).astype(low)
    for k in range(GROUP):
        here = slice(k * rows, (k + 1) * rows)
        total = jnp.zeros((rows, WIDE), full)
        for h in range(heads):
            there = slice(h * length + k * rows, h * length + (k + 1) * rows)
            g = keep(go[here, :], value_mask(h))
            gom[there, :] = g
            qm[there, :] = keep(qkv[here, 0:WIDE], half_mask(h))
            gp = mm_nt(g, qkv[:, 2 * WIDE :])
            p = probs[h, here, :].astype(full)
            inner = jnp.sum(p * gp, axis=-1, keepdims=True)
            grad = (p * (gp - inner)).astype(low)
            gs[there, :] = grad
            total = total + mm(grad, keep(qkv[:, WIDE : 2 * WIDE], half_mask(h)))
        total = total * (HEAD_DIM**-0.5)
        c, s = cos[here, :], sin[here, :]
        v1, v2 = total[:, :LANES], total[:, LANES:]
        gmixed[here, 0:LANES] = (v1 * c + v2 * s).astype(low)
        gmixed[here, LANES:WIDE] = (v2 * c - v1 * s).astype(low)
    for k in range(GROUP):
        here = slice(k * rows, (k + 1) * rows)
        gk = mm_tn(gs[:, here], qm[...]) * (HEAD_DIM**-0.5)
        c, s = cos[here, :], sin[here, :]
        v1, v2 = gk[:, :LANES], gk[:, LANES:]
        gmixed[here, WIDE : WIDE + LANES] = (v1 * c + v2 * s).astype(low)
        gmixed[here, WIDE + LANES : 2 * WIDE] = (v2 * c - v1 * s).astype(low)
        gv = jnp.zeros((rows, WIDE), full)
        for h in range(heads):
            gv = gv + mm_tn(probs[h, :, here], gom[h * length : (h + 1) * length, :])
        gmixed[here, 2 * WIDE :] = gv.astype(low)
    fetch_w.wait()
    for k, out in enumerate((p0, p1, p2, p3)):
        out[...] = mm_nt(gmixed[k * rows : (k + 1) * rows, :], w[...]).astype(low)


class FeedWeights:
    def __init__(self, mine, up_own, up_oth, dn_own, dn_oth, wu, wd, sem, first):
        width = wu.shape[1]
        self.wu, self.wd = wu, wd
        self.up, self.down = [], []
        for j in range(GROUP):
            cut = slice(j * width, (j + 1) * width)
            self.up.append(Fetch(up_own, up_oth, mine, (slice(None), cut), wu.at[j], sem.at[first + j]))
            self.down.append(Fetch(dn_own, dn_oth, mine, (cut, slice(None)), wd.at[j], sem.at[first + GROUP + j]))


def feed_forward(me, x, atts, norms, fetch_o, wo, feed, shards, y, hidden, slope, messages, parts, cols):
    rows, width = x.shape
    heads_wide = atts[0].shape[1]
    for k in range(GROUP):
        fetch_o[k].wait()
    state = x[...].astype(full)
    for k in range(GROUP):
        state = state + mm(atts[k][...], wo[k])
        cols[me ^ k] = atts[k][...]
    hidden[...] = state
    hat, _ = norm_stats(state)
    n2 = (hat * norms[2:3, :] + norms[3:4, :]).astype(low)
    for message in messages:
        message[:, 0:width] = n2
    step = width // (GROUP * shards)
    for target in range(GROUP):
        pieces = []
        for z in range(shards):
            at = (z * GROUP + target) * step
            pieces.append(cols[at // heads_wide, :, at % heads_wide : at % heads_wide + step])
        pieces.append(jnp.zeros((rows, WIDE - heads_wide), low))
        parts[target, :, width : width + WIDE] = jnp.concatenate(pieces, axis=1)
    out = jnp.zeros((rows, width), full)
    chunk = feed.wu.shape[2]
    for j in range(GROUP):
        feed.up[j].wait()
        act, grad = gelu_both(mm(n2, feed.wu[j]))
        act = act.astype(low)
        slope[:, j * chunk : (j + 1) * chunk] = grad.astype(low)
        feed.down[j].wait()
        out = out + mm(act, feed.wd[j])
        span = chunk * GROUP // (GROUP * shards)
        for b in range(chunk // span):
            z, target = divmod(j * (chunk // span) + b, GROUP)
            parts[target, :, z * span : (z + 1) * span] = act[:, b * span : (b + 1) * span]
    y[...] = (hidden[...] + out).astype(low)
    for k, message in enumerate(messages):
        message[:, width : 2 * width + WIDE] = parts[me ^ k]


def feed_back(me, gf, grad_out, norms, feed, hidden, slope, ga, gh, dnorm, messages, offset, gu, waited, with_gf):
    rows, width = gf.shape
    chunk = feed.wu.shape[2]
    grad = jnp.zeros((rows, width), full)
    for j in range(GROUP):
        if not waited:
            feed.down[j].wait()
        got = mm_nt(gf, feed.wd[j]) * slope[:, j * chunk : (j + 1) * chunk].astype(full)
        got = got.astype(low)
        gu[j] = got
        if not waited:
            feed.up[j].wait()
        grad = grad + mm_nt(got, feed.wu[j])
    back, d_gain, d_shift = norm_backward(hidden[...], norms[2:3, :], grad)
    total = grad_out + back
    gh[...] = total
    ga[...] = total.astype(low)
    dnorm[0:1, :] = d_gain
    dnorm[1:2, :] = d_shift
    for k, message in enumerate(messages):
        message[:, offset : offset + width] = gu[me ^ k]
        if with_gf:
            message[:, offset + width : offset + 2 * width] = gf


def start_out(sc, mine, wo_own, wo_oth, wo, sem):
    width = wo.shape[1]
    out = []
    for k in range(GROUP):
        span = pl.ds(pl.multiple_of((sc[1] ^ k) * width, HEAD_DIM), width)
        out.append(Fetch(wo_own, wo_oth, mine, (span, slice(None)), wo.at[k], sem.at[k]))
    return out


def feed_kernel(layer, shards, sc, x, a0, a1, a2, a3, norms, wo_own, wo_oth, up_own, up_oth, dn_own, dn_oth, y, hidden, slope, m0, m1, m2, m3, wo, wu, wd, parts, cols, sem):
    mine = sc[0] == layer
    fetch_o = start_out(sc, mine, wo_own, wo_oth, wo, sem)
    feed = FeedWeights(mine, up_own, up_oth, dn_own, dn_oth, wu, wd, sem, GROUP)
    for f in fetch_o + [f for pair in zip(feed.up, feed.down) for f in pair]:
        f.start()
    feed_forward(sc[1], x, (a0, a1, a2, a3), norms, fetch_o, wo, feed, shards, y, hidden, slope, (m0, m1, m2, m3), parts, cols)


def feed_turn_kernel(layer, shards, sc, x, a0, a1, a2, a3, norms, cot, wo_own, wo_oth, up_own, up_oth, dn_own, dn_oth, y, ga, gh, dnorm, m0, m1, m2, m3, wo, wu, wd, parts, cols, hidden, slope, gu, sem):
    mine = sc[0] == layer
    fetch_o = start_out(sc, mine, wo_own, wo_oth, wo, sem)
    feed = FeedWeights(mine, up_own, up_oth, dn_own, dn_oth, wu, wd, sem, GROUP)
    for f in fetch_o + [f for pair in zip(feed.up, feed.down) for f in pair]:
        f.start()
    messages = (m0, m1, m2, m3)
    feed_forward(sc[1], x, (a0, a1, a2, a3), norms, fetch_o, wo, feed, shards, y, hidden, slope, messages, parts, cols)
    gf = cot[...]
    feed_back(sc[1], gf, gf.astype(full), norms, feed, hidden, slope, ga, gh, dnorm, messages, 2 * gf.shape[1] + WIDE, gu, True, False)


def turn_kernel(layer, sc, r0, r1, r2, r3, gh_in, x_in, norms_in, hidden, slope, norms, up_own, up_oth, dn_own, dn_oth, gx, dnorm_in, ga, gh, dnorm, m0, m1, m2, m3, wu, wd, gu, sem):
    mine = sc[0] == layer
    feed = FeedWeights(mine, up_own, up_oth, dn_own, dn_oth, wu, wd, sem, 0)
    for f in [f for pair in zip(feed.down, feed.up) for f in pair]:
        f.start()
    top = first_norm_back(r0, r1, r2, r3, gh_in, x_in, norms_in, gx, dnorm_in)
    gf = top.astype(low)
    feed_back(sc[1], gf, gf.astype(full), norms, feed, hidden, slope, ga, gh, dnorm, (m0, m1, m2, m3), 0, gu, False, True)


def first_norm_back(r0, r1, r2, r3, gh_in, x_in, norms_in, gx, dnorm):
    grad = r0[...].astype(full) + r1[...].astype(full) + r2[...].astype(full) + r3[...].astype(full)
    back, d_gain, d_shift = norm_backward(x_in[...].astype(full), norms_in[0:1, :], grad)
    dnorm[0:1, :] = d_gain
    dnorm[1:2, :] = d_shift
    total = gh_in[...] + back
    gx[...] = total
    return total


def last_kernel(r0, r1, r2, r3, gh_in, x_in, norms_in, gx, dnorm):
    first_norm_back(r0, r1, r2, r3, gh_in, x_in, norms_in, gx, dnorm)


def tall_product(left, right, out, base, step):
    @pl.loop(0, left.shape[1] // step)
    def _(i):
        cut = pl.ds(pl.multiple_of(i * step, step), step)
        put = pl.ds(pl.multiple_of(base + i * step, step), step)
        out[put, :] = mm_tn(left[:, cut], right[...]).astype(out.dtype)


def feed_grads_kernel(at_gu, at_gf, *refs):
    fwd, gus, gfs = refs[:GROUP], refs[GROUP : 2 * GROUP], refs[2 * GROUP : 3 * GROUP]
    grads, a, b = refs[3 * GROUP :]
    rows, width = fwd[0].shape[0], a.shape[1]
    for k in range(GROUP):
        here = slice(k * rows, (k + 1) * rows)
        a[here, :] = fwd[k][:, 0:width]
        b[here, :] = gus[k][:, at_gu : at_gu + width]
    tall_product(a, b, grads, 0, WIDE)
    for k in range(GROUP):
        here = slice(k * rows, (k + 1) * rows)
        a[here, :] = fwd[k][:, width : 2 * width]
        b[here, :] = gfs[k][:, at_gf : at_gf + width]
    tall_product(a, b, grads, width, WIDE)


def attend_grads_kernel(n1, gmixed, m0, m1, m2, m3, g0, g1, g2, g3, grads, a, b):
    rows, width = g0.shape
    tall_product(n1, gmixed, grads, 0, WIDE)
    for k, (m, g) in enumerate(zip((m0, m1, m2, m3), (g0, g1, g2, g3))):
        here = slice(k * rows, (k + 1) * rows)
        a[here, :] = m[:, 2 * width : 2 * width + WIDE]
        b[here, :] = g[...]
    grads[width:, :] = mm_tn(a[...], b[...])[: grads.shape[0] - width, :].astype(low)


def merge_kernel(shards, sizes, sc, *refs):
    count = len(sizes)
    own, other, outs = refs[:count], refs[count : 2 * count], refs[2 * count :]
    for k in range(shards):
        block = lax.rem(sc[3] + k, shards)
        at = 0
        for mine, theirs, parts in zip(own, other, sizes):
            base = 0
            for size in parts:
                step = size // shards
                span = pl.ds(pl.multiple_of(base + block * step, 16), step)
                total = mine[span, :].astype(full) + theirs[span, :].astype(full)
                outs[k][at : at + step, :] = total.astype(outs[k].dtype)
                at += step
                base += size


def block_sum(sc, first, second, at, upto, shift):
    total = 0.0
    for a, b in zip(first, second):
        total = total + jnp.where(sc[0] == 0, a[at:upto, :].astype(full), b[at + shift : upto + shift, :].astype(full))
    return total


def spread_rows(out, values, start, stride):
    for j in range(values.shape[1] // LANES):
        out[pl.ds(start + j, values.shape[0], stride=stride), :] = values[:, j * LANES : (j + 1) * LANES]


def feed_finish_kernel(shards, sc, *refs):
    first, second = refs[:shards], refs[shards : 2 * shards]
    grad_down, u0, u1, u2, u3, held = refs[2 * shards :]
    half = first[0].shape[0] // 2
    width = first[0].shape[1]
    spread_rows(grad_down, block_sum(sc, first, second, half, 2 * half, 0), 0, width // LANES)
    held[...] = block_sum(sc, first, second, 0, half, 0)
    few = half // GROUP
    for k, u in enumerate((u0, u1, u2, u3)):
        u[...] = held[pl.ds(pl.multiple_of((sc[1] ^ k) * few, few), few), :].astype(low)


def attend_finish_kernel(shards, sc, *refs):
    first, second = refs[:shards], refs[shards : 2 * shards]
    grad_out, v0, v1, v2, v3, held = refs[2 * shards :]
    shift = second[0].shape[0] - first[0].shape[0]
    tall = held.shape[0]
    width = first[0].shape[1]
    spread_rows(grad_out, block_sum(sc, first, second, tall, first[0].shape[0], shift), 0, width // LANES)
    held[...] = block_sum(sc, first, second, 0, tall, shift)
    few = tall // GROUP
    for k, v in enumerate((v0, v1, v2, v3)):
        v[...] = held[pl.ds(pl.multiple_of((sc[1] ^ k) * few, few), few), :].astype(low)


def up_place_kernel(sc, u0, u1, u2, u3, grad_up):
    width = u0.shape[1]
    per = width // LANES
    for k, u in enumerate((u0, u1, u2, u3)):
        spread_rows(grad_up, u[...].astype(full), (sc[1] ^ k) * per, GROUP * per)


def qkv_place_kernel(heads, sc, v0, v1, v2, v3, grad_qkv, natural, whole):
    mine_wide = heads * HEAD_DIM
    shape = (WIDE, WIDE)
    u, out = lax.broadcasted_iota(jnp.int32, shape, 0), lane_index(shape)
    v = u & (LANES - 1)
    column = jnp.where(v < heads * HALF, (v // HALF) * HEAD_DIM + (u // LANES) * HALF + (v & (HALF - 1)), -1)
    back = jnp.where(out == column, 1.0, 0.0).astype(low)
    for k, piece in enumerate((v0, v1, v2, v3)):
        for part in range(3):
            values = piece[:, part * WIDE : (part + 1) * WIDE]
            natural[sc[1] ^ k, :, part * WIDE : (part + 1) * WIDE] = values.astype(full) if part == 2 else mm(values, back)
    for part in range(3):
        for c in range(GROUP):
            at = (part * GROUP + c) * mine_wide
            whole[:, at : at + mine_wide] = natural[c, :, part * WIDE : part * WIDE + mine_wide]
    spread_rows(grad_qkv, whole[...], 0, whole.shape[1] // LANES)


def run(kernel, shapes, scratch, operands, spaces, flops=0, moved=0):
    place = {"s": pltpu.SMEM, "v": pltpu.VMEM, "a": pl.ANY}
    return pl.pallas_call(
        kernel,
        out_shape=[jax.ShapeDtypeStruct(shape, kind) for shape, kind in shapes],
        in_specs=[pl.BlockSpec(memory_space=place[space]) for space in spaces],
        out_specs=[pl.BlockSpec(memory_space=pltpu.VMEM) for _ in shapes],
        scratch_shapes=scratch,
        compiler_params=pltpu.CompilerParams(vmem_limit_bytes=56 * 2**20),
        cost_estimate=pl.CostEstimate(flops=flops, bytes_accessed=moved, transcendentals=0),
    )(*operands)


def exchange(value):
    values = value if isinstance(value, (list, tuple)) else [value] * GROUP
    return [values[0]] + [
        lax.ppermute(values[k], "ctx", [(i, i ^ k) for i in range(GROUP)]) for k in range(1, GROUP)
    ]


def swap(value):
    return lax.ppermute(value, "section", [(0, 1), (1, 0)])


def rotary_tables(me, bound, rows):
    spot = jnp.arange(GROUP * rows, dtype=jnp.int32)
    place = (me ^ (spot // rows)) * rows + spot % rows
    relative = (place - jnp.where(place >= bound, bound, 0)).astype(full)
    steps = (jnp.arange(LANES, dtype=jnp.int32) % HALF).astype(full)
    freqs = jnp.exp(-math.log(rotary_base) * 2.0 * steps / HEAD_DIM)
    angles = relative[:, None] * freqs[None, :]
    return jnp.cos(angles), jnp.sin(angles)


def together(*values):
    return lax.optimization_barrier(values)


def along_dp(layer, blocks):
    count = len(blocks)
    got = [blocks[0]]
    for k in range(1, count):
        pairs = [(layer * count + i, layer * count + (i + k) % count) for i in range(count)]
        got.append(lax.ppermute(blocks[k], ("section", "dp"), pairs))
    return got


def on_device(tokens, cotangent, seq_bound, ln1_gain, ln1_shift, w_qkv, w_out, ln2_gain, ln2_shift, w_up, w_down):
    section = lax.axis_index("section")
    me = lax.axis_index("ctx")
    shards = lax.axis_size("dp")
    z = lax.axis_index("dp")
    rows, width = tokens.shape[1:]
    feed_width = w_up.shape[2]
    chunk = feed_width // GROUP
    heads = width // HEAD_DIM // GROUP
    mine_wide = heads * HEAD_DIM
    length = GROUP * rows
    few = width // (GROUP * shards)
    bound = lax.dynamic_index_in_dim(seq_bound[0], section, 0, keepdims=False)
    sc = jnp.stack([section, me, bound, z]).astype(jnp.int32)

    dma = pltpu.SemaphoreType.DMA
    vm = pltpu.VMEM
    piece = ((rows, width), low)
    wide_piece = ((rows, width), full)
    pair = ((2, width), full)

    x = lax.dynamic_index_in_dim(tokens, section, 0, keepdims=False)
    wq_own = w_qkv[0]
    wq_oth = swap(wq_own)
    gathered = exchange(x)
    norms_own = jnp.concatenate([ln1_gain, ln1_shift, ln2_gain, ln2_shift], axis=0)
    norms_oth = swap(norms_own)
    norms = [jnp.where(section == layer, norms_own, norms_oth) for layer in range(2)]
    cos, sin = rotary_tables(me, bound, rows)
    gathered[1], wo_own, up_own, dn_own = together(gathered[1], w_out[0], w_up[0], w_down[0])
    wo_oth, up_oth, dn_oth = swap(wo_own), swap(up_own), swap(dn_own)

    def attend(layer, gathered):
        return run(
            functools.partial(attend_kernel, layer, heads),
            [((length, width), low), ((length, 3 * WIDE), low), ((heads, length, length), low)] + [((rows, mine_wide), low)] * GROUP,
            [vm((3, width, WIDE), low), vm((width, 3 * WIDE), low), dma((3,))],
            (sc, *gathered, norms[layer], cos, sin, wq_own, wq_oth),
            "svvvvvvvaa",
            flops=2 * length * width * 3 * WIDE * 2, moved=8 * 2**20,
        )

    def attend_back(layer, grads, qkv, probs):
        return run(
            functools.partial(attend_back_kernel, layer, heads),
            [((length, 3 * WIDE), low)] + [piece] * GROUP,
            [
                vm((mine_wide, width), low), vm((3, width, WIDE), low), vm((width, 3 * WIDE), low), vm((length, WIDE), low),
                vm((heads * length, length), low), vm((heads * length, WIDE), low), vm((heads * length, WIDE), low), dma((4,)),
            ],
            (sc, *grads, qkv, probs, cos, sin, wo_own, wo_oth, wq_own, wq_oth),
            "svvvvvvvvaaaa",
            flops=2 * length * width * 3 * WIDE * 3, moved=8 * 2**20,
        )

    def feed_grads(fwd, gus, gfs, at_gu, at_gf):
        return run(
            functools.partial(feed_grads_kernel, at_gu, at_gf),
            [((2 * width, chunk), low)], [vm((length, width), low), vm((length, width), low)], (*fwd, *gus, *gfs), "v" * (3 * GROUP),
            flops=4 * length * width * chunk, moved=8 * 2**20,
        )[0]

    def attend_grads(n1, gmixed, fwd, ga):
        return run(
            attend_grads_kernel,
            [((width + mine_wide, width), low)], [vm((length, WIDE), low), vm((length, width), low)],
            (n1, gmixed, *fwd, *ga), "v" * (2 + 2 * GROUP),
            flops=2 * length * width * width, moved=8 * 2**20,
        )[0]

    def across(layer, value):
        return lax.ppermute(value, "section", [(1 - layer, layer)])

    feed_sizes, attend_sizes = (width, chunk), (width, mine_wide)

    def merge(own, other, sizes):
        total = sum(sum(parts) for parts in sizes) // shards
        return run(
            functools.partial(merge_kernel, shards, sizes),
            [((total, width), full)] + [((total, width), low)] * (shards - 1), [],
            (sc, *own, *other), "s" + "v" * (2 * len(own)), moved=2**22,
        )

    feed_scratch = [vm((GROUP, width, chunk), low), vm((GROUP, chunk, width), low)]
    out_scratch = vm((GROUP, mine_wide, width), low)
    split_scratch = [vm((GROUP, rows, width + WIDE), low), vm((GROUP, rows, mine_wide), low)]
    weights = (wo_own, wo_oth, up_own, up_oth, dn_own, dn_oth)

    n1_0, qkv_0, probs_0, *att = attend(0, gathered)
    att = exchange(att)
    y0, hidden_0, slope_0, *fwd_0 = run(
        functools.partial(feed_kernel, 0, shards),
        [piece, wide_piece, ((rows, feed_width), low)] + [((rows, 2 * width + WIDE), low)] * GROUP,
        [out_scratch, *feed_scratch, *split_scratch, dma((3 * GROUP,))],
        (sc, x, *att, norms[0], *weights),
        "svvvvvvaaaaaa",
        flops=4 * rows * width * feed_width, moved=14 * 2**20,
    )
    gathered_1 = exchange(y0)
    cot = lax.dynamic_index_in_dim(cotangent, section, 0, keepdims=False)
    att[3], cot = together(att[3], cot)
    cots = exchange(cot)
    *gathered_1, cots[1], cots[2], cots[3] = together(*gathered_1, *cots[1:])
    gathered_1[3], *fwd_0 = together(gathered_1[3], *fwd_0)
    fwd_0 = exchange(fwd_0)
    n1_1, qkv_1, probs_1, *att = attend(1, gathered_1)
    att = exchange(att)
    y1, ga, gh_1, dn2_1, *both_1 = run(
        functools.partial(feed_turn_kernel, 1, shards),
        [piece, piece, wide_piece, pair] + [((rows, 3 * width + WIDE), low)] * GROUP,
        [
            out_scratch, *feed_scratch, *split_scratch, vm((rows, width), full), vm((rows, feed_width), low),
            vm((GROUP, rows, chunk), low), dma((3 * GROUP,)),
        ],
        (sc, y0, *att, norms[1], cot, *weights),
        "svvvvvvvaaaaaa",
        flops=8 * rows * width * feed_width, moved=14 * 2**20,
    )
    ga_1 = exchange(ga)
    *ga_1, fwd_0[1], fwd_0[2], fwd_0[3] = together(*ga_1, *fwd_0[1:])
    ga_1[3], *both_1 = together(ga_1[3], *both_1)
    both_1 = exchange(both_1)
    gmixed_1, *back = attend_back(1, ga_1, qkv_1, probs_1)
    back = exchange(back)
    gx_1, dn1_1, ga, gh_0, dn2_0, *bwd_0 = run(
        functools.partial(turn_kernel, 0),
        [wide_piece, pair, piece, wide_piece, pair] + [((rows, 2 * width), low)] * GROUP,
        [*feed_scratch, vm((GROUP, rows, chunk), low), dma((2 * GROUP,))],
        (sc, *back, gh_1, y0, norms[1], hidden_0, slope_0, norms[0], up_own, up_oth, dn_own, dn_oth),
        "svvvvvvvvvvaaaa",
        flops=4 * rows * width * feed_width, moved=12 * 2**20,
    )
    ga_0 = exchange(ga)
    g_feed_1 = feed_grads(both_1, both_1, cots, 2 * width + WIDE, 0)
    *ga_0, g_feed_1 = together(*ga_0, g_feed_1)
    ga_0[3], *bwd_0 = together(ga_0[3], *bwd_0)
    bwd_0 = exchange(bwd_0)
    h_feed_1 = across(1, g_feed_1)
    gmixed_0, *back = attend_back(0, ga_0, qkv_0, probs_0)
    back = exchange(back)
    g_att_1 = attend_grads(n1_1, gmixed_1, both_1, ga_1)
    *back, g_att_1 = together(*back, g_att_1)
    h_att_1 = across(1, g_att_1)
    gx_0, dn1_0 = run(
        last_kernel, [wide_piece, pair], [], (*back, gh_0, x, norms[0]), "vvvvvvv", moved=2**20,
    )

    g_att_0 = attend_grads(n1_0, gmixed_0, fwd_0, ga_0)
    h_att_0 = across(0, g_att_0)
    g_feed_0 = feed_grads(fwd_0, bwd_0, bwd_0, 0, width)
    h_feed_0 = across(0, g_feed_0)
    if shards <= 8:
        r_1 = along_dp(1, merge([g_feed_1, g_att_1], [h_feed_1, h_att_1], [feed_sizes, attend_sizes]))
        r_att = along_dp(0, merge([g_att_0], [h_att_0], [attend_sizes]))
        r_feed = along_dp(0, merge([g_feed_0], [h_feed_0], [feed_sizes]))
        tall, lanes = width // shards, width // LANES
        grad_down, *up = run(
            functools.partial(feed_finish_kernel, shards),
            [((tall * lanes, LANES), full)] + [((few, chunk), low)] * GROUP, [vm((tall, chunk), full)],
            (sc, *r_feed, *r_1), "s" + "v" * (2 * shards), moved=2**22,
        )
        up = exchange(up)
        grad_out, *qkv = run(
            functools.partial(attend_finish_kernel, shards),
            [((few * lanes, LANES), full)] + [((few, width), low)] * GROUP, [vm((tall, width), full)],
            (sc, *r_att, *r_1), "s" + "v" * (2 * shards), moved=2**22,
        )
        qkv = exchange(qkv)
        (grad_up,) = run(
            up_place_kernel, [((few * GROUP * lanes, LANES), full)], [], (sc, *up), "s" + "v" * GROUP, moved=2**20,
        )
        (grad_qkv,) = run(
            functools.partial(qkv_place_kernel, heads),
            [((few * 3 * lanes, LANES), full)], [vm((GROUP, few, 3 * WIDE), full), vm((few, 3 * width), full)],
            (sc, *qkv), "s" + "v" * GROUP, moved=2**20,
        )
    else:
        grad_down, grad_up, grad_out, grad_qkv = many_shards(
            me, section, shards, heads, [g_feed_0, g_feed_1], [h_feed_0, h_feed_1], [g_att_0, g_att_1], [h_att_0, h_att_1], chunk
        )

    small = [jnp.concatenate([dn1_0, dn2_0]), jnp.concatenate([dn1_1, dn2_1])]
    small = jnp.where(section == 0, small[0], small[1]) + swap(jnp.where(section == 0, small[1], small[0]))
    small = small.reshape(shards, GROUP, -1)
    if shards <= 8:
        at_z = lax.dynamic_index_in_dim(small, z, 0, keepdims=False)
        for k in range(1, shards):
            block = lax.dynamic_index_in_dim(small, lax.rem(z + k, shards), 0, keepdims=False)
            at_z = at_z + lax.ppermute(block, "dp", [(i, (i + k) % shards) for i in range(shards)])
    else:
        at_z = lax.psum_scatter(small, "dp", scatter_dimension=0, tiled=False)
    grad_norms = sum(exchange([lax.dynamic_index_in_dim(at_z, me ^ k, 0, keepdims=False) for k in range(GROUP)]))

    def by_section(first, second):
        own = jnp.where(section == 0, first, second)
        got = swap(jnp.where(section == 0, second, first))
        return jnp.where(section == 0, jnp.stack([own, got]), jnp.stack([got, own]))[None]

    return (
        by_section(y0, y1),
        by_section(gx_0, gx_1),
        grad_qkv.reshape(1, -1),
        grad_out.reshape(1, -1),
        grad_up.reshape(1, -1),
        grad_down.reshape(1, -1),
        grad_norms.reshape(1, -1),
    )


def many_shards(me, section, shards, heads, g_feed, h_feed, g_att, h_att, chunk):
    width = g_feed[0].shape[1]

    def total(own, other):
        sums = [a.astype(full) + b.astype(full) for a, b in zip(own, other)]
        return jnp.where(section == 0, sums[0], sums[1])

    def scattered(value):
        blocks = value.reshape(shards, value.shape[0] // shards, value.shape[1]).astype(low)
        return lax.psum_scatter(blocks, "dp", scatter_dimension=0, tiled=False)

    feed, att = total(g_feed, h_feed), total(g_att, h_att)
    t_up, t_down = scattered(feed[:width]), scattered(feed[width:])
    t_qkv, t_out = scattered(att[:width]), scattered(att[width:])
    slim = jnp.concatenate([t_up, t_qkv], axis=1)
    slim = slim.reshape(GROUP, slim.shape[0] // GROUP, slim.shape[1])
    gets = jnp.stack(exchange([lax.dynamic_index_in_dim(slim, me ^ k, 0, keepdims=False) for k in range(GROUP)]))
    gets = jnp.stack([lax.dynamic_index_in_dim(gets, me ^ k, 0, keepdims=False) for k in range(GROUP)]).astype(full)
    few = gets.shape[1]
    grad_up = jnp.transpose(gets[:, :, :chunk], (1, 0, 2))
    cols = gets[:, :, chunk:].reshape(GROUP, few, 3, WIDE)
    turned = cols[:, :, :2].reshape(GROUP, few, 2, 2, LANES)[..., : heads * HALF]
    turned = turned.reshape(GROUP, few, 2, 2, heads, HALF).transpose(1, 2, 0, 4, 3, 5).reshape(few, 2 * width)
    plain = cols[:, :, 2, : heads * HEAD_DIM].transpose(1, 0, 2).reshape(few, width)
    return t_down.astype(full), grad_up, t_out.astype(full), jnp.concatenate([turned, plain], axis=1)


def solution(mesh):
    in_specs = (
        P(None, ("dp", "ctx"), None),
        P(None, ("dp", "ctx"), None),
        P("dp", None),
        P("section", None),
        P("section", None),
        P("section", None, None),
        P("section", None, None),
        P("section", None),
        P("section", None),
        P("section", None, None),
        P("section", None, None),
    )
    out_specs = (
        P("section", None, ("dp", "ctx"), None),
        P("section", None, ("dp", "ctx"), None),
        P("section", ("dp", "ctx")),
        P("section", ("dp", "ctx")),
        P("section", ("dp", "ctx")),
        P("section", ("dp", "ctx")),
        P("section", ("dp", "ctx")),
    )
    return jax.shard_map(
        on_device, mesh=mesh, in_specs=in_specs, out_specs=out_specs, check_vma=False
    )
```

```python
import functools
import math

import jax
import jax.numpy as jnp
from jax import lax
from jax.experimental import pallas as pl
from jax.experimental.pallas import tpu as pltpu
from jax.sharding import PartitionSpec as P

HEAD_DIM = 64
HALF = HEAD_DIM // 2
GROUP = 4
LANES = 128
WIDE = 2 * LANES

epsilon = 1e-05
rotary_base = 10000.0
masked_score = -1e30
low = jnp.bfloat16
full = jnp.float32

NT = (((1,), (1,)), ((), ()))
TN = (((0,), (0,)), ((), ()))


def mm(a, b):
    return jnp.dot(a, b, preferred_element_type=full)


def mm_nt(a, b):
    return lax.dot_general(a, b, NT, preferred_element_type=full)


def mm_tn(a, b):
    return lax.dot_general(a, b, TN, preferred_element_type=full)


def layer_norms(layer, sc, own, other):
    return jnp.where(sc[0] == layer, own[...], other[...])


def norm_stats(values):
    mean = jnp.mean(values, axis=-1, keepdims=True)
    centred = values - mean
    spread = jnp.mean(centred * centred, axis=-1, keepdims=True)
    scale = lax.rsqrt(spread + epsilon)
    return centred * scale, scale


def norm_backward(values, gain, grad):
    hat, scale = norm_stats(values)
    grad_gain = jnp.sum(grad * hat, axis=0, keepdims=True)
    grad_shift = jnp.sum(grad, axis=0, keepdims=True)
    inner = grad * gain
    first = jnp.mean(inner, axis=-1, keepdims=True)
    second = jnp.mean(inner * hat, axis=-1, keepdims=True)
    return scale * (inner - first - hat * second), grad_gain, grad_shift


def gelu_both(u):
    bell = jnp.exp(-0.5 * u * u)
    z = jnp.abs(u) * (0.5**0.5)
    t = 1.0 / (1.0 + 0.3275911 * z)
    poly = t * (
        0.254829592 + t * (-0.284496736 + t * (1.421413741 + t * (-1.453152027 + t * 1.061405429)))
    )
    tail = 0.5 * poly * bell
    cdf = jnp.where(u >= 0, 1.0 - tail, tail)
    return u * cdf, cdf + u * bell * (1.0 / math.sqrt(2.0 * math.pi))


class Fetch:
    def __init__(self, own, other, use_own, place, target, sem):
        self.parts = (own, other, use_own, place, target, sem)

    def start(self):
        own, other, use_own, place, target, sem = self.parts

        @pl.when(use_own)
        def _():
            pltpu.make_async_copy(own.at[place], target, sem).start()

        @pl.when(jnp.logical_not(use_own))
        def _():
            pltpu.make_async_copy(other.at[place], target, sem).start()

    def wait(self):
        own, other, use_own, place, target, sem = self.parts
        pltpu.make_async_copy(own.at[place], target, sem).wait()


def lane_index(shape):
    return lax.broadcasted_iota(jnp.int32, shape, 1)


def half_mask(head):
    return ((lane_index((1, WIDE)) & (LANES - 1)) // HALF) == head


def value_mask(head):
    return (lane_index((1, WIDE)) // HEAD_DIM) == head


def keep(values, mask):
    return jnp.where(mask, values, jnp.zeros_like(values))


class ProjectionWeights:
    def __init__(self, me, heads, mine, own, other, windows, target, sem):
        total = own.shape[0]
        at = me * (heads * HEAD_DIM)
        self.shift = lax.rem(at, LANES)
        start = at - self.shift
        self.windows, self.target, self.heads = windows, target, heads
        self.parts = []
        for part in range(3):
            span = pl.ds(pl.multiple_of(part * total + start, LANES), WIDE)
            self.parts.append(Fetch(own, other, mine, (slice(None), span), windows.at[part], sem.at[part]))

    def start(self):
        for part in self.parts:
            part.start()

    def wait(self):
        shape = (WIDE, WIDE)
        source, u = lax.broadcasted_iota(jnp.int32, shape, 0), lane_index(shape)
        v = u & (LANES - 1)
        turned = jnp.where(v < self.heads * HALF, (v // HALF) * HEAD_DIM + (u // LANES) * HALF + (v & (HALF - 1)) + self.shift, -1)
        plain = jnp.where(u < self.heads * HEAD_DIM, u + self.shift, -1)
        turned = jnp.where(source == turned, 1.0, 0.0).astype(low)
        plain = jnp.where(source == plain, 1.0, 0.0).astype(low)
        for part in range(3):
            self.parts[part].wait()
            chosen = mm(self.windows[part], plain if part == 2 else turned)
            self.target[:, part * WIDE : (part + 1) * WIDE] = chosen.astype(low)


def rotary_tables(me, bound, rows, cos, sin):
    for k in range(GROUP):
        here = slice(k * rows, (k + 1) * rows)
        spot = (me ^ k) * rows + lax.broadcasted_iota(jnp.int32, (rows, LANES), 0)
        relative = (spot - jnp.where(spot >= bound, bound, 0)).astype(full)
        steps = (lane_index((rows, LANES)) & (HALF - 1)).astype(full)
        angles = relative * jnp.exp(-math.log(rotary_base) * 2.0 * steps / HEAD_DIM)
        cos[here, :] = jnp.cos(angles)
        sin[here, :] = jnp.sin(angles)


def attend_kernel(layer, heads, sc, x0, x1, x2, x3, norms_own, norms_oth, *refs):
    if layer == 0:
        w_own, w_oth, cos, sin, n1, qkv, probs, a0, a1, a2, a3, win, w, sem = refs
    else:
        cos, sin, w_own, w_oth, n1, qkv, probs, a0, a1, a2, a3, win, w, sem = refs
    rows = x0.shape[0]
    weights = ProjectionWeights(sc[1], heads, sc[0] == layer, w_own, w_oth, win, w, sem)
    weights.start()
    if layer == 0:
        rotary_tables(sc[1], sc[2], rows, cos, sin)
    norms = layer_norms(layer, sc, norms_own, norms_oth)
    gain, shift = norms[0:1, :], norms[1:2, :]
    for k, x in enumerate((x0, x1, x2, x3)):
        hat, _ = norm_stats(x[...].astype(full))
        n1[k * rows : (k + 1) * rows, :] = (hat * gain + shift).astype(low)
    weights.wait()
    for k in range(GROUP):
        here = slice(k * rows, (k + 1) * rows)
        mixed = mm(n1[here, :], w[...])
        c, s = cos[here, :], sin[here, :]
        for part in range(2):
            base = part * WIDE
            v1, v2 = mixed[:, base : base + LANES], mixed[:, base + LANES : base + WIDE]
            qkv[here, base : base + LANES] = (v1 * c - v2 * s).astype(low)
            qkv[here, base + LANES : base + WIDE] = (v2 * c + v1 * s).astype(low)
        qkv[here, 2 * WIDE :] = mixed[:, 2 * WIDE :].astype(low)
    me, bound = sc[1], sc[2]
    length = GROUP * rows
    spot = lax.broadcasted_iota(jnp.int32, (1, length), 1)
    place = jnp.zeros((1, length), jnp.int32)
    for k in range(GROUP):
        place = jnp.where(spot // rows == k, (me ^ k) * rows + spot - k * rows, place)
    seq_col = (place >= bound).astype(jnp.int32)
    for k, out in enumerate((a0, a1, a2, a3)):
        here = slice(k * rows, (k + 1) * rows)
        own = (me ^ k) * rows + lax.broadcasted_iota(jnp.int32, (rows, 1), 0)
        same = (own >= bound).astype(jnp.int32) == seq_col
        total = jnp.zeros((rows, WIDE), full)
        for h in range(heads):
            q = keep(qkv[here, 0:WIDE], half_mask(h))
            scores = mm_nt(q, qkv[:, WIDE : 2 * WIDE]) * (HEAD_DIM**-0.5)
            scores = jnp.where(same, scores, masked_score)
            top = jnp.max(scores, axis=-1, keepdims=True)
            expo = jnp.where(same, jnp.exp(scores - top), 0.0)
            p = (expo * (1.0 / jnp.sum(expo, axis=-1, keepdims=True))).astype(low)
            probs[h, here, :] = p
            total = total + mm(p, keep(qkv[:, 2 * WIDE :], value_mask(h)))
        out[...] = total[:, : heads * HEAD_DIM].astype(low)


def attend_back_kernel(layer, heads, sc, g0, g1, g2, g3, qkv, probs, cos, sin, wo_own, wo_oth, w_own, w_oth, gmixed, p0, p1, p2, p3, wo, win, w, go, gs, qm, gom, sem):
    rows = g0.shape[0]
    width = heads * HEAD_DIM
    me = sc[1]
    mine = sc[0] == layer
    span = pl.ds(pl.multiple_of(me * width, HEAD_DIM), width)
    fetch_o = Fetch(wo_own, wo_oth, mine, (span, slice(None)), wo, sem.at[3])
    fetch_w = ProjectionWeights(me, heads, mine, w_own, w_oth, win, w, sem)
    fetch_o.start()
    fetch_w.start()
    fetch_o.wait()
    length = GROUP * rows
    go[:, LANES:] = jnp.zeros((length, WIDE - LANES), low)
    for k, g in enumerate((g0, g1, g2, g3)):
        go[k * rows : (k + 1) * rows, :width] = mm_nt(g[:, : wo.shape[1]], wo[...]).astype(low)
    for k in range(GROUP):
        here = slice(k * rows, (k + 1) * rows)
        total = jnp.zeros((rows, WIDE), full)
        for h in range(heads):
            there = slice(h * length + k * rows, h * length + (k + 1) * rows)
            g = keep(go[here, :], value_mask(h))
            gom[there, :] = g
            qm[there, :] = keep(qkv[here, 0:WIDE], half_mask(h))
            gp = mm_nt(g, qkv[:, 2 * WIDE :])
            p = probs[h, here, :].astype(full)
            inner = jnp.sum(p * gp, axis=-1, keepdims=True)
            grad = (p * (gp - inner)).astype(low)
            gs[there, :] = grad
            total = total + mm(grad, keep(qkv[:, WIDE : 2 * WIDE], half_mask(h)))
        total = total * (HEAD_DIM**-0.5)
        c, s = cos[here, :], sin[here, :]
        v1, v2 = total[:, :LANES], total[:, LANES:]
        gmixed[here, 0:LANES] = (v1 * c + v2 * s).astype(low)
        gmixed[here, LANES:WIDE] = (v2 * c - v1 * s).astype(low)
    for k in range(GROUP):
        here = slice(k * rows, (k + 1) * rows)
        gk = mm_tn(gs[:, here], qm[...]) * (HEAD_DIM**-0.5)
        c, s = cos[here, :], sin[here, :]
        v1, v2 = gk[:, :LANES], gk[:, LANES:]
        gmixed[here, WIDE : WIDE + LANES] = (v1 * c + v2 * s).astype(low)
        gmixed[here, WIDE + LANES : 2 * WIDE] = (v2 * c - v1 * s).astype(low)
        gv = jnp.zeros((rows, WIDE), full)
        for h in range(heads):
            gv = gv + mm_tn(probs[h, :, here], gom[h * length : (h + 1) * length, :])
        gmixed[here, 2 * WIDE :] = gv.astype(low)
    fetch_w.wait()
    for k, out in enumerate((p0, p1, p2, p3)):
        out[...] = mm_nt(gmixed[k * rows : (k + 1) * rows, :], w[...]).astype(low)


class FeedWeights:
    def __init__(self, mine, up_own, up_oth, dn_own, dn_oth, wu, wd, sem, first):
        width = wu.shape[1]
        self.wu, self.wd = wu, wd
        self.up, self.down = [], []
        for j in range(GROUP):
            cut = slice(j * width, (j + 1) * width)
            self.up.append(Fetch(up_own, up_oth, mine, (slice(None), cut), wu.at[j], sem.at[first + j]))
            self.down.append(Fetch(dn_own, dn_oth, mine, (cut, slice(None)), wd.at[j], sem.at[first + GROUP + j]))


def feed_forward(sc, x, atts, norms, fetch_o, wo, feed, shards, y, hidden, slope, owner, parts, cols):
    rows, width = x.shape
    heads_wide = atts[0].shape[1]
    me = sc[1]
    for k in range(GROUP):
        fetch_o[k].wait()
    state = x[...].astype(full)
    for k in range(GROUP):
        state = state + mm(atts[k][...], wo[k])
        cols[me ^ k, :, :heads_wide] = atts[k][...]
    hidden[...] = state
    hat, _ = norm_stats(state)
    n2 = (hat * norms[2:3, :] + norms[3:4, :]).astype(low)
    step = width // (GROUP * shards)
    shares = []
    for target in range(GROUP):
        pieces = []
        for z in range(shards):
            at = (z * GROUP + target) * step
            pieces.append(cols[at // heads_wide, :, at % heads_wide : at % heads_wide + step])
        pieces.append(jnp.zeros((rows, WIDE - heads_wide), low))
        shares.append(jnp.concatenate(pieces, axis=1))
    for target in range(GROUP):
        cols[target] = shares[target]
    out = jnp.zeros((rows, width), full)
    chunk = feed.wu.shape[2]
    for j in range(GROUP):
        feed.up[j].wait()
        act, grad = gelu_both(mm(n2, feed.wu[j]))
        act = act.astype(low)
        slope[:, j * chunk : (j + 1) * chunk] = grad.astype(low)
        feed.down[j].wait()
        out = out + mm(act, feed.wd[j])
        if owner == 3:
            parts[j] = act
            continue
        span = chunk // shards
        for b in range(chunk // span):
            z, target = divmod(j * (chunk // span) + b, GROUP)
            parts[target, :, z * span : (z + 1) * span] = act[:, b * span : (b + 1) * span]
    y[...] = (hidden[...] + out).astype(low)
    return n2


def feed_back(gf, grad_out, norms, feed, hidden, slope, gas, gh, dnorm, gu, waited):
    rows, width = gf.shape
    chunk = feed.wu.shape[2]
    grad = jnp.zeros((rows, width), full)
    for j in range(GROUP):
        if not waited:
            feed.down[j].wait()
        got = mm_nt(gf, feed.wd[j]) * slope[:, j * chunk : (j + 1) * chunk].astype(full)
        got = got.astype(low)
        gu[j] = got
        if not waited:
            feed.up[j].wait()
        grad = grad + mm_nt(got, feed.wu[j])
    back, d_gain, d_shift = norm_backward(hidden[...], norms[2:3, :], grad)
    total = grad_out + back
    gh[...] = total
    for ga in gas:
        ga[:, 0:width] = total.astype(low)
    dnorm[0:1, :] = d_gain
    dnorm[1:2, :] = d_shift


def start_out(sc, mine, wo_own, wo_oth, wo, sem):
    width = wo.shape[1]
    out = []
    for k in range(GROUP):
        span = pl.ds(pl.multiple_of((sc[1] ^ k) * width, HEAD_DIM), width)
        out.append(Fetch(wo_own, wo_oth, mine, (span, slice(None)), wo.at[k], sem.at[k]))
    return out


def feed_kernel(layer, shards, sc, x, a0, a1, a2, a3, norms_own, norms_oth, wo_own, wo_oth, up_own, up_oth, dn_own, dn_oth, y, hidden, slope, m0, m1, m2, m3, wo, wu, wd, parts, cols, sem):
    mine = sc[0] == layer
    norms = layer_norms(layer, sc, norms_own, norms_oth)
    fetch_o = start_out(sc, mine, wo_own, wo_oth, wo, sem)
    feed = FeedWeights(mine, up_own, up_oth, dn_own, dn_oth, wu, wd, sem, GROUP)
    for f in fetch_o + [f for pair in zip(feed.up, feed.down) for f in pair]:
        f.start()
    n2 = feed_forward(sc, x, (a0, a1, a2, a3), norms, fetch_o, wo, feed, shards, y, hidden, slope, 1, parts, cols)
    width = x.shape[1]
    for k, m in enumerate((m0, m1, m2, m3)):
        m[:, 0:width] = n2
        m[:, width : 2 * width] = parts[sc[1] ^ k]
        m[:, 2 * width :] = cols[sc[1] ^ k]


def feed_turn_kernel(layer, shards, owner, sc, x, a0, a1, a2, a3, norms_own, norms_oth, cot, wo_own, wo_oth, up_own, up_oth, dn_own, dn_oth, y, gh, dnorm, g0, g1, g2, g3, m0, m1, m2, m3, d0, d1, d2, d3, wo, wu, wd, parts, cols, hidden, slope, gu, sem):
    mine = sc[0] == layer
    norms = layer_norms(layer, sc, norms_own, norms_oth)
    fetch_o = start_out(sc, mine, wo_own, wo_oth, wo, sem)
    feed = FeedWeights(mine, up_own, up_oth, dn_own, dn_oth, wu, wd, sem, GROUP)
    for f in fetch_o + [f for pair in zip(feed.up, feed.down) for f in pair]:
        f.start()
    gas = (g0, g1, g2, g3)
    n2 = feed_forward(sc, x, (a0, a1, a2, a3), norms, fetch_o, wo, feed, shards, y, hidden, slope, owner, parts, cols)
    gf = cot[...]
    feed_back(gf, gf.astype(full), norms, feed, hidden, slope, gas, gh, dnorm, gu, True)
    width = x.shape[1]
    for k, (g, m, d) in enumerate(((g0, m0, d0), (g1, m1, d1), (g2, m2, d2), (g3, m3, d3))):
        g[:, width:] = cols[sc[1] ^ k]
        m[:, 0:width] = n2
        m[:, width:] = gu[sc[1] ^ k]
        d[:, 0:width] = parts[sc[owner] ^ k]
        d[:, width:] = gf


def turn_kernel(layer, sc, r0, r1, r2, r3, gh_in, x_in, hidden, slope, norms_own, norms_oth, up_own, up_oth, dn_own, dn_oth, gx, dnorm_in, ga, gh, dnorm, m0, m1, m2, m3, wu, wd, gu, sem):
    mine = sc[0] == layer
    feed = FeedWeights(mine, up_own, up_oth, dn_own, dn_oth, wu, wd, sem, 0)
    for f in [f for pair in zip(feed.down, feed.up) for f in pair]:
        f.start()
    norms_in = layer_norms(layer + 1, sc, norms_own, norms_oth)
    norms = layer_norms(layer, sc, norms_own, norms_oth)
    top = first_norm_back(r0, r1, r2, r3, gh_in, x_in, norms_in, gx, dnorm_in)
    gf = top.astype(low)
    feed_back(gf, gf.astype(full), norms, feed, hidden, slope, (ga,), gh, dnorm, gu, False)
    width = gf.shape[1]
    for k, m in enumerate((m0, m1, m2, m3)):
        m[:, 0:width] = gu[sc[1] ^ k]
        m[:, width:] = gf


def first_norm_back(r0, r1, r2, r3, gh_in, x_in, norms_in, gx, dnorm):
    grad = r0[...].astype(full) + r1[...].astype(full) + r2[...].astype(full) + r3[...].astype(full)
    back, d_gain, d_shift = norm_backward(x_in[...].astype(full), norms_in[0:1, :], grad)
    dnorm[0:1, :] = d_gain
    dnorm[1:2, :] = d_shift
    total = gh_in[...] + back
    gx[...] = total
    return total


def last_kernel(sc, r0, r1, r2, r3, gh_in, x_in, norms_own, norms_oth, above, d1_1, d2_1, d2_0, kept, sent, sums, sums_sent, gx, dnorm):
    first_norm_back(r0, r1, r2, r3, gh_in, x_in, layer_norms(0, sc, norms_own, norms_oth), gx, dnorm)
    first = sc[0] == 0
    kept[...] = jnp.where(first, gx[...], above[...])
    sent[...] = jnp.where(first, above[...], gx[...])
    for at, zero, one in ((0, dnorm, d1_1), (2, d2_0, d2_1)):
        sums[at : at + 2, :] = jnp.where(first, zero[...], one[...])
        sums_sent[at : at + 2, :] = jnp.where(first, one[...], zero[...])


def gather_rows(pieces, at, target, half, section, sems):
    rows, width = pieces[0].shape[0], target.shape[1]
    copies = []
    for k, piece in enumerate(pieces):
        here = pl.ds(k * rows, rows)
        if half is None:
            copies.append(pltpu.make_async_copy(piece.at[:, pl.ds(at, width)], target.at[here, :], sems.at[k]))
            continue
        for i, part in enumerate((section, 1 - section)):
            source = pl.ds(pl.multiple_of(at + part * half, LANES), half)
            copies.append(pltpu.make_async_copy(piece.at[:, source], target.at[here, pl.ds(i * half, half)], sems.at[2 * k + i]))
    for copy in copies:
        copy.start()
    return copies


def tall_product(left, right, stay, go, base, step):
    half = stay.shape[1]
    for i in range(left.shape[1] // step):
        cut, put = slice(i * step, (i + 1) * step), slice(base + i * step, base + (i + 1) * step)
        product = mm_tn(left[:, cut], right[...]).astype(low)
        stay[put, :] = product[:, :half]
        go[put, :] = product[:, half:]


def pair_grads_kernel(places, sc, *refs):
    count = len(places)
    outs, (a, b, sem) = refs[2 * GROUP * count : -3], refs[-3:]
    half = outs[0].shape[1]
    copies = []
    for i, (at_left, at_right) in enumerate(places):
        lefts, rights = refs[2 * GROUP * i :][:GROUP], refs[2 * GROUP * i + GROUP :][:GROUP]
        copies.append(
            gather_rows(lefts, at_left, a.at[i], None, None, sem.at[2 * i]) + gather_rows(rights, at_right, b.at[i], half, sc[0], sem.at[2 * i + 1])
        )
    for i in range(count):
        for copy in copies[i]:
            copy.wait()
        tall_product(a.at[i], b.at[i], outs[2 * i], outs[2 * i + 1], 0, WIDE)


def attend_grads_kernel(at_att, sc, n1, gmixed, m0, m1, m2, m3, g0, g1, g2, g3, stay, go, left, right, a, b, sem):
    width, half = b.shape[1], stay.shape[1]
    first = gather_rows((n1,), 0, left, None, None, sem.at[0]) + gather_rows((gmixed,), 0, right, half, sc[0], sem.at[1])
    second = gather_rows((m0, m1, m2, m3), at_att, a, None, None, sem.at[2]) + gather_rows((g0, g1, g2, g3), 0, b, half, sc[0], sem.at[3])
    for copy in first:
        copy.wait()
    tall_product(left, right, stay, go, 0, WIDE)
    for copy in second:
        copy.wait()
    product = mm_tn(a[...], b[...])[: stay.shape[0] - width, :].astype(low)
    stay[width:, :] = product[:, :half]
    go[width:, :] = product[:, half:]


def add_kernel(sizes, *refs):
    count = len(sizes)
    mine, theirs = refs[:count], refs[count : 2 * count]
    norms = refs[2 * count] if len(refs) > 2 * count + 1 else None
    out = refs[-1]
    blocks, total, half = out.shape
    for b in range(blocks):
        at = 0
        for x, y, size in zip(mine, theirs, sizes):
            base = 0
            for part in size:
                step = part // blocks
                span = slice(base + b * step, base + (b + 1) * step)
                out[b, at : at + step, :] = (x[span, :].astype(full) + y[span, :].astype(full)).astype(low)
                at += step
                base += part
        if norms is not None:
            row = lax.broadcasted_iota(jnp.int32, (total - at, half), 0)
            lower, upper = norms[b : b + 1, :half], norms[b : b + 1, half:]
            out[b, at:, :] = jnp.where(row == 0, lower, jnp.where(row == 1, upper, 0.0)).astype(low)


def split_kernel(sc, mine, theirs, stay, go):
    step = stay.shape[1]
    for out, flip in ((stay, 0), (go, 1)):
        for j in range(2):
            span = pl.ds(pl.multiple_of((2 * j + ((sc[1] & 1) ^ flip)) * step, 16), step)
            out[j] = (mine[span, :].astype(full) + theirs[span, :].astype(full)).astype(low)


def halve_kernel(sc, held, got, stay, go):
    high = sc[1] >> 1
    stay[...] = held[high].astype(full) + got[high].astype(full)
    go[...] = (held[1 - high].astype(full) + got[1 - high].astype(full)).astype(low)


def pack_kernel(sc, att_0, feed_0, att_1, up_1, down_1, down_1_got, stay, go):
    parts = (
        (att_0[...], att_1[...]),
        (feed_0[0 : up_1.shape[0], :], up_1[...]),
        (feed_0[up_1.shape[0] : 2 * up_1.shape[0], :], (down_1[...] + down_1_got[...].astype(full)).astype(low)),
    )
    first = sc[0] == 0
    at = 0
    for zero, one in parts:
        upto = at + zero.shape[0]
        stay[at:upto, :] = jnp.where(first, zero, one)
        go[at:upto, :] = jnp.where(first, one, zero)
        at = upto


def spread_rows(out, values, start, stride):
    for j in range(values.shape[1] // LANES):
        out[pl.ds(start + j, values.shape[0], stride=stride), :] = values[:, j * LANES : (j + 1) * LANES]


def finish_kernel(sc, mine, theirs, feed_0, grad_down, grad_out, v0, v1, v2, v3, whole):
    half = mine.shape[1]
    width = 2 * half
    step = width // GROUP
    few = step // GROUP
    lanes = width // LANES
    whole[:, pl.ds(pl.multiple_of(sc[0] * half, LANES), half)] = mine[...].astype(full)
    whole[:, pl.ds(pl.multiple_of((1 - sc[0]) * half, LANES), half)] = theirs[...].astype(full)
    at_up = step + few
    spread_rows(grad_out, whole[step:at_up, :], 0, lanes)
    spread_rows(grad_down, whole[at_up + step :, :], 0, lanes)
    lower, upper = feed_0[2 * step : 2 * step + 1, :], feed_0[2 * step + 1 : 2 * step + 2, :]
    last = jnp.concatenate([lower, upper], axis=1)
    shares = [last[:, c * step : (c + 1) * step] for c in range(GROUP)]
    for k, v in enumerate((v0, v1, v2, v3)):
        at = (sc[1] ^ k) * few
        v[0:few, :] = whole[pl.ds(pl.multiple_of(at_up + at, few), few), :].astype(low)
        v[few : 2 * few, :] = whole[pl.ds(pl.multiple_of(at, few), few), :].astype(low)
        share = jnp.zeros_like(shares[0])
        for c in range(GROUP):
            share = jnp.where((sc[1] ^ k) == c, shares[c], share)
        v[2 * few :, :] = jnp.zeros((v.shape[0] - 2 * few, width), low)
        v[2 * few : 2 * few + 1, :step] = share


def place_kernel(heads, sc, v0, v1, v2, v3, grad_up, grad_qkv, grad_norms, natural, whole):
    width = v0.shape[1]
    few = natural.shape[1]
    per = width // LANES
    mine_wide = heads * HEAD_DIM
    shape = (WIDE, WIDE)
    source, out = lax.broadcasted_iota(jnp.int32, shape, 0), lane_index(shape)
    v = source & (LANES - 1)
    column = jnp.where(v < heads * HALF, (v // HALF) * HEAD_DIM + (source // LANES) * HALF + (v & (HALF - 1)), -1)
    back = jnp.where(out == column, 1.0, 0.0).astype(low)
    norm = jnp.zeros((1, mine_wide), full)
    for k, piece in enumerate((v0, v1, v2, v3)):
        spread_rows(grad_up, piece[0:few, :].astype(full), (sc[1] ^ k) * per, GROUP * per)
        for part in range(3):
            values = piece[few : 2 * few, part * WIDE : (part + 1) * WIDE]
            natural[sc[1] ^ k, :, part * WIDE : (part + 1) * WIDE] = values.astype(full) if part == 2 else mm(values, back)
        norm = norm + piece[2 * few : 2 * few + 1, :mine_wide].astype(full)
    grad_norms[...] = norm
    for part in range(3):
        for c in range(GROUP):
            to = (part * GROUP + c) * mine_wide
            whole[:, to : to + mine_wide] = natural[c, :, part * WIDE : part * WIDE + mine_wide]
    spread_rows(grad_qkv, whole[...], 0, whole.shape[1] // LANES)


def run(kernel, shapes, scratch, operands, spaces):
    place = {"s": pltpu.SMEM, "v": pltpu.VMEM, "a": pl.ANY}
    return pl.pallas_call(
        kernel,
        out_shape=[jax.ShapeDtypeStruct(shape, kind) for shape, kind in shapes],
        in_specs=[pl.BlockSpec(memory_space=place[space]) for space in spaces],
        out_specs=[pl.BlockSpec(memory_space=pltpu.VMEM) for _ in shapes],
        scratch_shapes=scratch,
        compiler_params=pltpu.CompilerParams(vmem_limit_bytes=52 * 2**20),
        cost_estimate=pl.CostEstimate(flops=1, bytes_accessed=1, transcendentals=0),
    )(*operands)


def exchange(value):
    values = value if isinstance(value, (list, tuple)) else [value] * GROUP
    return [values[0]] + [
        lax.ppermute(values[k], "ctx", [(i, i ^ k) for i in range(GROUP)]) for k in range(1, GROUP)
    ]


def towards(value, k):
    return lax.ppermute(value, "ctx", [(i, i ^ k) for i in range(GROUP)])


def along(value, k):
    count = lax.axis_size("dp")
    return lax.ppermute(value, "dp", [(i, i ^ k) for i in range(count)])


def swap(value):
    return lax.ppermute(value, "section", [(0, 1), (1, 0)])


def together(*values):
    return lax.optimization_barrier(values)


def on_device(tokens, cotangent, seq_bound, ln1_gain, ln1_shift, w_qkv, w_out, ln2_gain, ln2_shift, w_up, w_down):
    section = lax.axis_index("section")
    me = lax.axis_index("ctx")
    shards = lax.axis_size("dp")
    z = lax.axis_index("dp")
    rows, width = tokens.shape[1:]
    feed_width = w_up.shape[2]
    chunk = feed_width // GROUP
    heads = width // HEAD_DIM // GROUP
    mine_wide = heads * HEAD_DIM
    length = GROUP * rows
    few = width // (GROUP * shards)
    bound = lax.dynamic_index_in_dim(seq_bound[0], section, 0, keepdims=False)
    sc = jnp.stack([section, me, bound, z]).astype(jnp.int32)

    dma = pltpu.SemaphoreType.DMA
    vm = pltpu.VMEM
    piece = ((rows, width), low)
    wide_piece = ((rows, width), full)
    pair = ((2, width), full)

    x = lax.dynamic_index_in_dim(tokens, section, 0, keepdims=False)
    gathered = exchange(x)
    wq_own, wo_own, up_own, dn_own = w_qkv[0], w_out[0], w_up[0], w_down[0]
    wq_oth, wo_oth = swap(wq_own), swap(wo_own)
    norms_own = jnp.concatenate([ln1_gain, ln1_shift, ln2_gain, ln2_shift], axis=0)
    wo_oth, later = together(wo_oth, norms_own)
    norms_oth = swap(later)
    wq_oth, norms_oth, later = together(wq_oth, norms_oth, up_own)
    up_oth = swap(later)
    *gathered, later = together(*gathered, dn_own)
    dn_oth = swap(later)

    def attend(layer, gathered, *tables):
        table = ((length, LANES), full)
        given = len(tables)
        return run(
            functools.partial(attend_kernel, layer, heads),
            [table] * (2 - given) + [((length, width), low), ((length, 3 * WIDE), low), ((heads, length, length), low)] + [((rows, mine_wide), low)] * GROUP,
            [vm((3, width, WIDE), low), vm((width, 3 * WIDE), low), dma((3,))],
            (sc, *gathered, norms_own, norms_oth, *tables, wq_own, wq_oth),
            "svvvvvv" + "v" * given + "aa",
        )

    def attend_back(layer, grads, qkv, probs):
        return run(
            functools.partial(attend_back_kernel, layer, heads),
            [((length, 3 * WIDE), low)] + [piece] * GROUP,
            [
                vm((mine_wide, width), low), vm((3, width, WIDE), low), vm((width, 3 * WIDE), low), vm((length, WIDE), low),
                vm((heads * length, length), low), vm((heads * length, WIDE), low), vm((heads * length, WIDE), low), dma((4,)),
            ],
            (sc, *grads, qkv, probs, cos, sin, wo_own, wo_oth, wq_own, wq_oth),
            "svvvvvvvvaaaa",
        )

    half = width // 2

    def pair_grads(*products):
        out = ((width, half), low)
        operands = [piece for lefts, rights, _, _ in products for piece in (*lefts, *rights)]
        places = [(at_left, at_right) for _, _, at_left, at_right in products]
        return run(
            functools.partial(pair_grads_kernel, places),
            [out] * (2 * len(products)),
            [vm((len(products), length, width), low), vm((len(products), length, width), low), dma((2 * len(products), 2 * GROUP))],
            (sc, *operands), "s" + "a" * len(operands),
        )

    def attend_grads(n1, gmixed, fwd, ga, at_att):
        return run(
            functools.partial(attend_grads_kernel, at_att),
            [((width + mine_wide, half), low)] * 2,
            [vm((length, width), low), vm((length, 3 * WIDE), low), vm((length, WIDE), low), vm((length, width), low), dma((4, 2 * GROUP))],
            (sc, n1, gmixed, *fwd, *ga), "s" + "a" * (2 + 2 * GROUP),
        )

    square, attend_size = (width,), (width, mine_wide)

    def over_dp(sizes, mine, theirs, *norms):
        total = sum(sum(size) for size in sizes) // shards + (16 if norms else 0)
        if small:
            (blocks,) = run(
                functools.partial(add_kernel, sizes), [((shards, total, half), low)], [], (*mine, *theirs, *norms),
                "v" * (2 * len(mine) + len(norms)),
            )
        else:
            parts = []
            for x, y, size in zip(mine, theirs, sizes):
                value = (x.astype(full) + y.astype(full)).astype(low)
                base = 0
                for part in size:
                    parts.append(value[base : base + part].reshape(shards, part // shards, half))
                    base += part
            blocks = jnp.concatenate(parts, axis=1)
        return lax.psum_scatter(blocks, "dp", scatter_dimension=0, tiled=False)

    feed_scratch = [vm((GROUP, width, chunk), low), vm((GROUP, chunk, width), low)]
    out_scratch = vm((GROUP, mine_wide, width), low)
    split_scratch = [vm((GROUP, rows, chunk), low), vm((GROUP, rows, WIDE), low)]
    small = shards == GROUP
    owner, other_way = (3, along) if small else (1, towards)

    cos, sin, n1_0, qkv_0, probs_0, *att = attend(0, gathered)
    att = exchange(att)
    weights = (wo_own, wo_oth, up_own, up_oth, dn_own, dn_oth)
    cot = lax.dynamic_index_in_dim(cotangent, section, 0, keepdims=False)
    y0, hidden_0, slope_0, *fwd_0 = run(
        functools.partial(feed_kernel, 0, shards),
        [piece, wide_piece, ((rows, feed_width), low)] + [((rows, 2 * width + WIDE), low)] * GROUP,
        [out_scratch, *feed_scratch, *split_scratch, dma((3 * GROUP,))],
        (sc, x, *att, norms_own, norms_oth, *weights),
        "svvvvvvvaaaaaa",
    )
    gathered_1 = exchange(y0)
    *gathered_1, fwd_0[1], fwd_0[2] = together(*gathered_1, fwd_0[1], fwd_0[2])
    fwd_0[1], fwd_0[2] = towards(fwd_0[1], 1), towards(fwd_0[2], 2)
    n1_1, qkv_1, probs_1, *att = attend(1, gathered_1, cos, sin)
    *att, fwd_0[1], fwd_0[2], fwd_0[3] = together(*att, *fwd_0[1:])
    att = exchange(att)
    fwd_0[3] = towards(fwd_0[3], 3)
    y1, gh_1, dn2_1, *rest = run(
        functools.partial(feed_turn_kernel, 1, shards, owner),
        [piece, wide_piece, pair] + [((rows, width + WIDE), low)] * GROUP + [((rows, 2 * width), low)] * (2 * GROUP),
        [
            out_scratch, *feed_scratch, *split_scratch, vm((rows, width), full), vm((rows, feed_width), low),
            vm((GROUP, rows, chunk), low), dma((3 * GROUP,)),
        ],
        (sc, y0, *att, norms_own, norms_oth, cot, *weights),
        "svvvvvvvvaaaaaa",
    )
    ga, up_1, down_1 = rest[:GROUP], rest[GROUP : 2 * GROUP], rest[2 * GROUP :]
    *ga, fwd_0[3] = together(*ga, fwd_0[3])
    ga_1 = exchange(ga)
    *ga_1, down_1[3], up_1[1], up_1[2] = together(*ga_1, down_1[3], up_1[1], up_1[2])
    up_1[1], up_1[2] = towards(up_1[1], 1), towards(up_1[2], 2)
    down_1[3] = other_way(down_1[3], 3)
    gmixed_1, *back = attend_back(1, ga_1, qkv_1, probs_1)
    *back, up_1[1], up_1[2], up_1[3] = together(*back, *up_1[1:])
    back = exchange(back)
    *back, down_1[3], up_1[3] = together(*back, down_1[3], up_1[3])
    up_1[3] = towards(up_1[3], 3)
    att_1, att_1_go = attend_grads(n1_1, gmixed_1, ga_1, ga_1, width)
    *back, att_1, att_1_go = together(*back, att_1, att_1_go)
    att_1_got = swap(att_1_go)
    gx_1, dn1_1, ga, gh_0, dn2_0, *bwd_0 = run(
        functools.partial(turn_kernel, 0),
        [wide_piece, pair, piece, wide_piece, pair] + [((rows, 2 * width), low)] * GROUP,
        [*feed_scratch, vm((GROUP, rows, chunk), low), dma((2 * GROUP,))],
        (sc, *back, gh_1, y0, hidden_0, slope_0, norms_own, norms_oth, up_own, up_oth, dn_own, dn_oth),
        "svvvvvvvvvvaaaa",
    )
    ga, att_1_got, up_1[3] = together(ga, att_1_got, up_1[3])
    ga_0 = exchange(ga)
    sum_att_1 = over_dp([attend_size], [att_1], [att_1_got])
    up_1_stay, up_1_go = pair_grads((up_1, up_1, 0, width))
    *ga_0, up_1_stay, up_1_go, bwd_0[1], bwd_0[2] = together(*ga_0, up_1_stay, up_1_go, bwd_0[1], bwd_0[2])
    bwd_0[1], bwd_0[2] = towards(bwd_0[1], 1), towards(bwd_0[2], 2)
    up_1_got = swap(up_1_go)
    gmixed_0, *back = attend_back(0, ga_0, qkv_0, probs_0)
    gmixed_0, *back, bwd_0[1], bwd_0[2], bwd_0[3], up_1_got, down_1[2] = together(gmixed_0, *back, *bwd_0[1:], up_1_got, down_1[2])
    sum_up_1 = over_dp([square], [up_1_stay], [up_1_got])
    bwd_0[3] = towards(bwd_0[3], 3)
    back = exchange(back)
    down_1[2] = other_way(down_1[2], 2)
    att_0, att_0_go = attend_grads(n1_0, gmixed_0, fwd_0, ga_0, 2 * width)
    *back, bwd_0[3], att_0, att_0_go, down_1[1] = together(*back, bwd_0[3], att_0, att_0_go, down_1[1])
    att_0_got = swap(att_0_go)
    kept, sent, sums, sums_sent = run(
        last_kernel, [wide_piece, wide_piece, ((4, width), full), ((4, width), full)],
        [vm((rows, width), full), vm((2, width), full)],
        (sc, *back, gh_0, x, norms_own, norms_oth, gx_1, dn1_1, dn2_1, dn2_0), "svvvvvvvvvvvv",
    )
    sums, sums_sent, att_0_got, bwd_0[3] = together(sums, sums_sent, att_0_got, bwd_0[3])
    sum_att_0 = over_dp([attend_size], [att_0], [att_0_got])
    down_1[1] = other_way(down_1[1], 1)
    sums_got = swap(sums_sent)
    up_0, up_0_go, down_0, down_0_go = pair_grads((fwd_0, bwd_0, 0, 0), (fwd_0, bwd_0, width, width))
    up_0, up_0_go, down_0, down_0_go, sums_got = together(up_0, up_0_go, down_0, down_0_go, sums_got)
    up_0_got, down_0_got = swap(up_0_go), swap(down_0_go)
    sums = sums + sums_got
    up_0_got, down_0_got = together(up_0_got, down_0_got)
    if small:
        sum_feed_0 = over_dp([square, square], [up_0, down_0], [up_0_got, down_0_got], sums)
    down_1_stay, down_1_go = pair_grads((down_1, down_1, 0, width))
    down_1_got = swap(down_1_go)
    if small:
        block = ((2, width // GROUP, half), low)
        stay, go = run(split_kernel, [block, block], [], (sc, down_1_stay, down_1_got), "svv")
        block = (width // GROUP, half)
        stay, go = run(halve_kernel, [(block, full), (block, low)], [], (sc, stay, towards(go, 1)), "svv")
        tall = width // shards
        lanes = width // LANES
        everything = ((3 * tall + few, half), low)
        mine, other = run(
            pack_kernel, [everything, everything], [],
            (sc, sum_att_0, sum_feed_0, sum_att_1, sum_up_1, stay, towards(go, 2)), "svvvvvv",
        )
        grad_down, grad_out, *pieces = run(
            finish_kernel,
            [((tall * lanes, LANES), full), ((few * lanes, LANES), full)] + [((2 * few + 16, width), low)] * GROUP,
            [vm((3 * tall + few, width), full)],
            (sc, mine, swap(other), sum_feed_0), "svvv",
        )
        grad_up, grad_qkv, grad_norms = run(
            functools.partial(place_kernel, heads),
            [((few * GROUP * lanes, LANES), full), ((few * 3 * lanes, LANES), full), ((1, mine_wide), full)],
            [vm((GROUP, few, 3 * WIDE), full), vm((few, 3 * width), full)],
            (sc, *exchange(pieces)), "s" + "v" * GROUP,
        )
    else:
        sum_feed_0 = over_dp([square, square], [up_0, down_0], [up_0_got, down_0_got])
        sum_down_1 = over_dp([square], [down_1_stay], [down_1_got])
        grad_up, grad_down, grad_out, grad_qkv = many_shards(
            me, section, heads, few, jnp.concatenate([sum_att_0, sum_feed_0]), jnp.concatenate([sum_att_1, sum_up_1, sum_down_1])
        )
        grad_norms = lax.psum_scatter(sums.reshape(shards * GROUP, -1), ("dp", "ctx"), scatter_dimension=0, tiled=True)

    def by_section(own, got):
        return jnp.where(section == 0, jnp.stack([own, got]), jnp.stack([got, own]))[None]

    y_own, y_sent = jnp.where(section == 0, y0, y1), jnp.where(section == 0, y1, y0)
    return (
        by_section(y_own, swap(y_sent)),
        by_section(kept, swap(sent)),
        grad_qkv.reshape(1, -1),
        grad_out.reshape(1, -1),
        grad_up.reshape(1, -1),
        grad_down.reshape(1, -1),
        grad_norms.reshape(1, -1),
    )


def many_shards(me, section, heads, few, first, second):
    own, other = jnp.where(section == 0, first, second), jnp.where(section == 0, second, first)
    got = swap(other)
    whole = jnp.where(section == 0, jnp.concatenate([own, got], axis=1), jnp.concatenate([got, own], axis=1))
    width = whole.shape[1]
    chunk, tall = width, GROUP * few
    t_qkv, t_out, t_up, t_down = whole[:tall], whole[tall : tall + few], whole[tall + few : 2 * tall + few], whole[2 * tall + few :]
    slim = jnp.concatenate([t_up, t_qkv], axis=1)
    slim = slim.reshape(GROUP, slim.shape[0] // GROUP, slim.shape[1])
    gets = jnp.stack(exchange([lax.dynamic_index_in_dim(slim, me ^ k, 0, keepdims=False) for k in range(GROUP)]))
    gets = jnp.stack([lax.dynamic_index_in_dim(gets, me ^ k, 0, keepdims=False) for k in range(GROUP)]).astype(full)
    few = gets.shape[1]
    grad_up = jnp.transpose(gets[:, :, :chunk], (1, 0, 2))
    cols = gets[:, :, chunk:].reshape(GROUP, few, 3, WIDE)
    turned = cols[:, :, :2].reshape(GROUP, few, 2, 2, LANES)[..., : heads * HALF]
    turned = turned.reshape(GROUP, few, 2, 2, heads, HALF).transpose(1, 2, 0, 4, 3, 5).reshape(few, 2 * width)
    plain = cols[:, :, 2, : heads * HEAD_DIM].transpose(1, 0, 2).reshape(few, width)
    return grad_up, t_down.astype(full), t_out.astype(full), jnp.concatenate([turned, plain], axis=1)


def solution(mesh):
    in_specs = (
        P(None, ("dp", "ctx"), None),
        P(None, ("dp", "ctx"), None),
        P("dp", None),
        P("section", None),
        P("section", None),
        P("section", None, None),
        P("section", None, None),
        P("section", None),
        P("section", None),
        P("section", None, None),
        P("section", None, None),
    )
    out_specs = (
        P("section", None, ("dp", "ctx"), None),
        P("section", None, ("dp", "ctx"), None),
        P("section", ("dp", "ctx")),
        P("section", ("dp", "ctx")),
        P("section", ("dp", "ctx")),
        P("section", ("dp", "ctx")),
        P("section", ("dp", "ctx")),
    )
    return jax.shard_map(
        on_device, mesh=mesh, in_specs=in_specs, out_specs=out_specs, check_vma=False
    )
```

```python
import functools
import math

import jax
import jax.numpy as jnp
from jax import lax
from jax.experimental import pallas as pl
from jax.experimental.pallas import tpu as pltpu
from jax.sharding import PartitionSpec as P

HEAD_DIM = 64
HALF = HEAD_DIM // 2
GROUP = 4
LANES = 128
WIDE = 2 * LANES

epsilon = 1e-05
rotary_base = 10000.0
masked_score = -1e30
low = jnp.bfloat16
full = jnp.float32

NT = (((1,), (1,)), ((), ()))
TN = (((0,), (0,)), ((), ()))


def mm(a, b):
    return jnp.dot(a, b, preferred_element_type=full)


def mm_nt(a, b):
    return lax.dot_general(a, b, NT, preferred_element_type=full)


def mm_tn(a, b):
    return lax.dot_general(a, b, TN, preferred_element_type=full)


def layer_norms(layer, sc, own, other):
    return jnp.where(sc[0] == layer, own[...], other[...])


def norm_stats(values):
    mean = jnp.mean(values, axis=-1, keepdims=True)
    centred = values - mean
    spread = jnp.mean(centred * centred, axis=-1, keepdims=True)
    scale = lax.rsqrt(spread + epsilon)
    return centred * scale, scale


def norm_backward(values, gain, grad):
    hat, scale = norm_stats(values)
    grad_gain = jnp.sum(grad * hat, axis=0, keepdims=True)
    grad_shift = jnp.sum(grad, axis=0, keepdims=True)
    inner = grad * gain
    first = jnp.mean(inner, axis=-1, keepdims=True)
    second = jnp.mean(inner * hat, axis=-1, keepdims=True)
    return scale * (inner - first - hat * second), grad_gain, grad_shift


def gelu_both(u):
    bell = jnp.exp(-0.5 * u * u)
    z = jnp.abs(u) * (0.5**0.5)
    t = 1.0 / (1.0 + 0.3275911 * z)
    poly = t * (
        0.254829592 + t * (-0.284496736 + t * (1.421413741 + t * (-1.453152027 + t * 1.061405429)))
    )
    tail = 0.5 * poly * bell
    cdf = jnp.where(u >= 0, 1.0 - tail, tail)
    return u * cdf, cdf + u * bell * (1.0 / math.sqrt(2.0 * math.pi))


class Fetch:
    def __init__(self, own, other, use_own, place, target, sem):
        self.parts = (own, other, use_own, place, target, sem)

    def start(self):
        own, other, use_own, place, target, sem = self.parts

        @pl.when(use_own)
        def _():
            pltpu.make_async_copy(own.at[place], target, sem).start()

        @pl.when(jnp.logical_not(use_own))
        def _():
            pltpu.make_async_copy(other.at[place], target, sem).start()

    def wait(self):
        own, other, use_own, place, target, sem = self.parts
        pltpu.make_async_copy(own.at[place], target, sem).wait()


def lane_index(shape):
    return lax.broadcasted_iota(jnp.int32, shape, 1)


def half_mask(head):
    return ((lane_index((1, WIDE)) & (LANES - 1)) // HALF) == head


def value_mask(head):
    return (lane_index((1, WIDE)) // HEAD_DIM) == head


def keep(values, mask):
    return jnp.where(mask, values, jnp.zeros_like(values))


class ProjectionWeights:
    def __init__(self, me, heads, mine, own, other, windows, target, sem):
        total = own.shape[0]
        at = me * (heads * HEAD_DIM)
        self.shift = lax.rem(at, LANES)
        start = at - self.shift
        self.windows, self.target, self.heads = windows, target, heads
        self.parts = []
        for part in range(3):
            span = pl.ds(pl.multiple_of(part * total + start, LANES), WIDE)
            self.parts.append(Fetch(own, other, mine, (slice(None), span), windows.at[part], sem.at[part]))

    def start(self):
        for part in self.parts:
            part.start()

    def wait(self):
        shape = (WIDE, WIDE)
        source, u = lax.broadcasted_iota(jnp.int32, shape, 0), lane_index(shape)
        v = u & (LANES - 1)
        turned = jnp.where(v < self.heads * HALF, (v // HALF) * HEAD_DIM + (u // LANES) * HALF + (v & (HALF - 1)) + self.shift, -1)
        plain = jnp.where(u < self.heads * HEAD_DIM, u + self.shift, -1)
        turned = jnp.where(source == turned, 1.0, 0.0).astype(low)
        plain = jnp.where(source == plain, 1.0, 0.0).astype(low)
        for part in range(3):
            self.parts[part].wait()
            chosen = mm(self.windows[part], plain if part == 2 else turned)
            self.target[:, part * WIDE : (part + 1) * WIDE] = chosen.astype(low)


def rotary_tables(me, bound, rows, cos, sin):
    for k in range(GROUP):
        here = slice(k * rows, (k + 1) * rows)
        spot = (me ^ k) * rows + lax.broadcasted_iota(jnp.int32, (rows, LANES), 0)
        relative = (spot - jnp.where(spot >= bound, bound, 0)).astype(full)
        steps = (lane_index((rows, LANES)) & (HALF - 1)).astype(full)
        angles = relative * jnp.exp(-math.log(rotary_base) * 2.0 * steps / HEAD_DIM)
        cos[here, :] = jnp.cos(angles)
        sin[here, :] = jnp.sin(angles)


def attend_kernel(layer, heads, sc, x0, x1, x2, x3, norms_own, norms_oth, *refs):
    if layer == 0:
        w_own, w_oth, cos, sin, n1, qkv, probs, a0, a1, a2, a3, win, w, sem = refs
    else:
        cos, sin, w_own, w_oth, n1, qkv, probs, a0, a1, a2, a3, win, w, sem = refs
    rows = x0.shape[0]
    weights = ProjectionWeights(sc[1], heads, sc[0] == layer, w_own, w_oth, win, w, sem)
    weights.start()
    if layer == 0:
        rotary_tables(sc[1], sc[2], rows, cos, sin)
    norms = layer_norms(layer, sc, norms_own, norms_oth)
    gain, shift = norms[0:1, :], norms[1:2, :]
    for k, x in enumerate((x0, x1, x2, x3)):
        hat, _ = norm_stats(x[...].astype(full))
        n1[k * rows : (k + 1) * rows, :] = (hat * gain + shift).astype(low)
    weights.wait()
    for k in range(GROUP):
        here = slice(k * rows, (k + 1) * rows)
        mixed = mm(n1[here, :], w[...])
        c, s = cos[here, :], sin[here, :]
        for part in range(2):
            base = part * WIDE
            v1, v2 = mixed[:, base : base + LANES], mixed[:, base + LANES : base + WIDE]
            qkv[here, base : base + LANES] = (v1 * c - v2 * s).astype(low)
            qkv[here, base + LANES : base + WIDE] = (v2 * c + v1 * s).astype(low)
        qkv[here, 2 * WIDE :] = mixed[:, 2 * WIDE :].astype(low)
    me, bound = sc[1], sc[2]
    length = GROUP * rows
    spot = lax.broadcasted_iota(jnp.int32, (1, length), 1)
    place = jnp.zeros((1, length), jnp.int32)
    for k in range(GROUP):
        place = jnp.where(spot // rows == k, (me ^ k) * rows + spot - k * rows, place)
    seq_col = (place >= bound).astype(jnp.int32)
    for k, out in enumerate((a0, a1, a2, a3)):
        here = slice(k * rows, (k + 1) * rows)
        own = (me ^ k) * rows + lax.broadcasted_iota(jnp.int32, (rows, 1), 0)
        same = (own >= bound).astype(jnp.int32) == seq_col
        total = jnp.zeros((rows, WIDE), full)
        for h in range(heads):
            q = keep(qkv[here, 0:WIDE], half_mask(h))
            scores = mm_nt(q, qkv[:, WIDE : 2 * WIDE]) * (HEAD_DIM**-0.5)
            scores = jnp.where(same, scores, masked_score)
            top = jnp.max(scores, axis=-1, keepdims=True)
            expo = jnp.where(same, jnp.exp(scores - top), 0.0)
            p = (expo * (1.0 / jnp.sum(expo, axis=-1, keepdims=True))).astype(low)
            probs[h, here, :] = p
            total = total + mm(p, keep(qkv[:, 2 * WIDE :], value_mask(h)))
        out[...] = total[:, : heads * HEAD_DIM].astype(low)


def attend_back_kernel(layer, heads, sc, g0, g1, g2, g3, qkv, probs, cos, sin, wo_own, wo_oth, w_own, w_oth, gmixed, p0, p1, p2, p3, wo, win, w, go, gs, qm, gom, sem):
    rows = g0.shape[0]
    width = heads * HEAD_DIM
    me = sc[1]
    mine = sc[0] == layer
    span = pl.ds(pl.multiple_of(me * width, HEAD_DIM), width)
    fetch_o = Fetch(wo_own, wo_oth, mine, (span, slice(None)), wo, sem.at[3])
    fetch_w = ProjectionWeights(me, heads, mine, w_own, w_oth, win, w, sem)
    fetch_o.start()
    fetch_w.start()
    fetch_o.wait()
    length = GROUP * rows
    go[:, LANES:] = jnp.zeros((length, WIDE - LANES), low)
    for k, g in enumerate((g0, g1, g2, g3)):
        go[k * rows : (k + 1) * rows, :width] = mm_nt(g[:, : wo.shape[1]], wo[...]).astype(low)
    for k in range(GROUP):
        here = slice(k * rows, (k + 1) * rows)
        total = jnp.zeros((rows, WIDE), full)
        for h in range(heads):
            there = slice(h * length + k * rows, h * length + (k + 1) * rows)
            g = keep(go[here, :], value_mask(h))
            gom[there, :] = g
            qm[there, :] = keep(qkv[here, 0:WIDE], half_mask(h))
            gp = mm_nt(g, qkv[:, 2 * WIDE :])
            p = probs[h, here, :].astype(full)
            inner = jnp.sum(p * gp, axis=-1, keepdims=True)
            grad = (p * (gp - inner)).astype(low)
            gs[there, :] = grad
            total = total + mm(grad, keep(qkv[:, WIDE : 2 * WIDE], half_mask(h)))
        total = total * (HEAD_DIM**-0.5)
        c, s = cos[here, :], sin[here, :]
        v1, v2 = total[:, :LANES], total[:, LANES:]
        gmixed[here, 0:LANES] = (v1 * c + v2 * s).astype(low)
        gmixed[here, LANES:WIDE] = (v2 * c - v1 * s).astype(low)
    for k in range(GROUP):
        here = slice(k * rows, (k + 1) * rows)
        gk = mm_tn(gs[:, here], qm[...]) * (HEAD_DIM**-0.5)
        c, s = cos[here, :], sin[here, :]
        v1, v2 = gk[:, :LANES], gk[:, LANES:]
        gmixed[here, WIDE : WIDE + LANES] = (v1 * c + v2 * s).astype(low)
        gmixed[here, WIDE + LANES : 2 * WIDE] = (v2 * c - v1 * s).astype(low)
        gv = jnp.zeros((rows, WIDE), full)
        for h in range(heads):
            gv = gv + mm_tn(probs[h, :, here], gom[h * length : (h + 1) * length, :])
        gmixed[here, 2 * WIDE :] = gv.astype(low)
    fetch_w.wait()
    for k, out in enumerate((p0, p1, p2, p3)):
        out[...] = mm_nt(gmixed[k * rows : (k + 1) * rows, :], w[...]).astype(low)


class FeedWeights:
    def __init__(self, mine, up_own, up_oth, dn_own, dn_oth, wu, wd, sem, first):
        width = wu.shape[1]
        self.wu, self.wd = wu, wd
        self.up, self.down = [], []
        for j in range(GROUP):
            cut = slice(j * width, (j + 1) * width)
            self.up.append(Fetch(up_own, up_oth, mine, (slice(None), cut), wu.at[j], sem.at[first + j]))
            self.down.append(Fetch(dn_own, dn_oth, mine, (cut, slice(None)), wd.at[j], sem.at[first + GROUP + j]))


def feed_forward(sc, x, atts, norms, fetch_o, wo, feed, shards, y, hidden, slope, owner, parts, cols):
    rows, width = x.shape
    heads_wide = atts[0].shape[1]
    me = sc[1]
    for k in range(GROUP):
        fetch_o[k].wait()
    state = x[...].astype(full)
    for k in range(GROUP):
        state = state + mm(atts[k][...], wo[k])
        cols[me ^ k, :, :heads_wide] = atts[k][...]
    hidden[...] = state
    hat, _ = norm_stats(state)
    n2 = (hat * norms[2:3, :] + norms[3:4, :]).astype(low)
    step = width // (GROUP * shards)
    shares = []
    for target in range(GROUP):
        pieces = []
        for z in range(shards):
            at = (z * GROUP + target) * step
            pieces.append(cols[at // heads_wide, :, at % heads_wide : at % heads_wide + step])
        pieces.append(jnp.zeros((rows, WIDE - heads_wide), low))
        shares.append(jnp.concatenate(pieces, axis=1))
    for target in range(GROUP):
        cols[target] = shares[target]
    out = jnp.zeros((rows, width), full)
    chunk = feed.wu.shape[2]
    for j in range(GROUP):
        feed.up[j].wait()
        act, grad = gelu_both(mm(n2, feed.wu[j]))
        act = act.astype(low)
        slope[:, j * chunk : (j + 1) * chunk] = grad.astype(low)
        feed.down[j].wait()
        out = out + mm(act, feed.wd[j])
        if owner == 3:
            parts[j] = act
            continue
        span = chunk // shards
        for b in range(chunk // span):
            z, target = divmod(j * (chunk // span) + b, GROUP)
            parts[target, :, z * span : (z + 1) * span] = act[:, b * span : (b + 1) * span]
    y[...] = (hidden[...] + out).astype(low)
    return n2


def feed_back(gf, grad_out, norms, feed, hidden, slope, gas, gh, dnorm, gu, waited):
    rows, width = gf.shape
    chunk = feed.wu.shape[2]
    grad = jnp.zeros((rows, width), full)
    for j in range(GROUP):
        if not waited:
            feed.down[j].wait()
        got = mm_nt(gf, feed.wd[j]) * slope[:, j * chunk : (j + 1) * chunk].astype(full)
        got = got.astype(low)
        gu[j] = got
        if not waited:
            feed.up[j].wait()
        grad = grad + mm_nt(got, feed.wu[j])
    back, d_gain, d_shift = norm_backward(hidden[...], norms[2:3, :], grad)
    total = grad_out + back
    gh[...] = total
    for ga in gas:
        ga[:, 0:width] = total.astype(low)
    dnorm[0:1, :] = d_gain
    dnorm[1:2, :] = d_shift


def start_out(sc, mine, wo_own, wo_oth, wo, sem):
    width = wo.shape[1]
    out = []
    for k in range(GROUP):
        span = pl.ds(pl.multiple_of((sc[1] ^ k) * width, HEAD_DIM), width)
        out.append(Fetch(wo_own, wo_oth, mine, (span, slice(None)), wo.at[k], sem.at[k]))
    return out


def feed_kernel(layer, shards, sc, x, a0, a1, a2, a3, norms_own, norms_oth, wo_own, wo_oth, up_own, up_oth, dn_own, dn_oth, y, hidden, slope, m0, m1, m2, m3, wo, wu, wd, parts, cols, sem):
    mine = sc[0] == layer
    norms = layer_norms(layer, sc, norms_own, norms_oth)
    fetch_o = start_out(sc, mine, wo_own, wo_oth, wo, sem)
    feed = FeedWeights(mine, up_own, up_oth, dn_own, dn_oth, wu, wd, sem, GROUP)
    for f in fetch_o + [f for pair in zip(feed.up, feed.down) for f in pair]:
        f.start()
    n2 = feed_forward(sc, x, (a0, a1, a2, a3), norms, fetch_o, wo, feed, shards, y, hidden, slope, 1, parts, cols)
    width = x.shape[1]
    for k, m in enumerate((m0, m1, m2, m3)):
        m[:, 0:width] = n2
        m[:, width : 2 * width] = parts[sc[1] ^ k]
        m[:, 2 * width :] = cols[sc[1] ^ k]


def feed_turn_kernel(layer, shards, owner, sc, x, a0, a1, a2, a3, norms_own, norms_oth, cot, wo_own, wo_oth, up_own, up_oth, dn_own, dn_oth, y, gh, dnorm, g0, g1, g2, g3, m0, m1, m2, m3, d0, d1, d2, d3, wo, wu, wd, parts, cols, hidden, slope, gu, sem):
    mine = sc[0] == layer
    norms = layer_norms(layer, sc, norms_own, norms_oth)
    fetch_o = start_out(sc, mine, wo_own, wo_oth, wo, sem)
    feed = FeedWeights(mine, up_own, up_oth, dn_own, dn_oth, wu, wd, sem, GROUP)
    for f in fetch_o + [f for pair in zip(feed.up, feed.down) for f in pair]:
        f.start()
    gas = (g0, g1, g2, g3)
    n2 = feed_forward(sc, x, (a0, a1, a2, a3), norms, fetch_o, wo, feed, shards, y, hidden, slope, owner, parts, cols)
    gf = cot[...]
    feed_back(gf, gf.astype(full), norms, feed, hidden, slope, gas, gh, dnorm, gu, True)
    width = x.shape[1]
    for k, (g, m, d) in enumerate(((g0, m0, d0), (g1, m1, d1), (g2, m2, d2), (g3, m3, d3))):
        g[:, width:] = cols[sc[1] ^ k]
        m[:, 0:width] = n2
        m[:, width:] = gu[sc[1] ^ k]
        d[...] = parts[sc[owner] ^ k]


def turn_kernel(layer, sc, r0, r1, r2, r3, gh_in, x_in, hidden, slope, norms_own, norms_oth, up_own, up_oth, dn_own, dn_oth, gx, dnorm_in, ga, gh, dnorm, m0, m1, m2, m3, wu, wd, gu, sem):
    mine = sc[0] == layer
    feed = FeedWeights(mine, up_own, up_oth, dn_own, dn_oth, wu, wd, sem, 0)
    for f in [f for pair in zip(feed.down, feed.up) for f in pair]:
        f.start()
    norms_in = layer_norms(layer + 1, sc, norms_own, norms_oth)
    norms = layer_norms(layer, sc, norms_own, norms_oth)
    top = first_norm_back(r0, r1, r2, r3, gh_in, x_in, norms_in, gx, dnorm_in)
    gf = top.astype(low)
    feed_back(gf, gf.astype(full), norms, feed, hidden, slope, (ga,), gh, dnorm, gu, False)
    width = gf.shape[1]
    for k, m in enumerate((m0, m1, m2, m3)):
        m[:, 0:width] = gu[sc[1] ^ k]
        m[:, width:] = gf


def first_norm_back(r0, r1, r2, r3, gh_in, x_in, norms_in, gx, dnorm):
    grad = r0[...].astype(full) + r1[...].astype(full) + r2[...].astype(full) + r3[...].astype(full)
    back, d_gain, d_shift = norm_backward(x_in[...].astype(full), norms_in[0:1, :], grad)
    dnorm[0:1, :] = d_gain
    dnorm[1:2, :] = d_shift
    total = gh_in[...] + back
    gx[...] = total
    return total


def last_kernel(sc, r0, r1, r2, r3, gh_in, x_in, norms_own, norms_oth, above, d1_1, d2_1, d2_0, kept, sent, sums, sums_sent, gx, dnorm):
    first_norm_back(r0, r1, r2, r3, gh_in, x_in, layer_norms(0, sc, norms_own, norms_oth), gx, dnorm)
    first = sc[0] == 0
    kept[...] = jnp.where(first, gx[...], above[...])
    sent[...] = jnp.where(first, above[...], gx[...])
    for at, zero, one in ((0, dnorm, d1_1), (2, d2_0, d2_1)):
        sums[at : at + 2, :] = jnp.where(first, zero[...], one[...])
        sums_sent[at : at + 2, :] = jnp.where(first, one[...], zero[...])


def gather_rows(pieces, at, target, half, section, sems):
    rows, width = pieces[0].shape[0], target.shape[1]
    copies = []
    for k, piece in enumerate(pieces):
        here = pl.ds(k * rows, rows)
        if half is None:
            copies.append(pltpu.make_async_copy(piece.at[:, pl.ds(at, width)], target.at[here, :], sems.at[k]))
            continue
        for i, part in enumerate((section, 1 - section)):
            source = pl.ds(pl.multiple_of(at + part * half, LANES), half)
            copies.append(pltpu.make_async_copy(piece.at[:, source], target.at[here, pl.ds(i * half, half)], sems.at[2 * k + i]))
    for copy in copies:
        copy.start()
    return copies


def tall_product(left, right, stay, go, base, step):
    half = stay.shape[1]
    for i in range(left.shape[1] // step):
        cut, put = slice(i * step, (i + 1) * step), slice(base + i * step, base + (i + 1) * step)
        product = mm_tn(left[:, cut], right[...]).astype(low)
        stay[put, :] = product[:, :half]
        go[put, :] = product[:, half:]


def pair_grads_kernel(places, sc, *refs):
    count = len(places)
    outs, (a, b, sem) = refs[2 * GROUP * count : -3], refs[-3:]
    half = outs[0].shape[1]
    copies = []
    for i, (at_left, at_right) in enumerate(places):
        lefts, rights = refs[2 * GROUP * i :][:GROUP], refs[2 * GROUP * i + GROUP :][:GROUP]
        copies.append(
            gather_rows(lefts, at_left, a.at[i], None, None, sem.at[2 * i]) + gather_rows(rights, at_right, b.at[i], half, sc[0], sem.at[2 * i + 1])
        )
    for i in range(count):
        for copy in copies[i]:
            copy.wait()
        tall_product(a.at[i], b.at[i], outs[2 * i], outs[2 * i + 1], 0, WIDE)


def attend_grads_kernel(at_att, sc, n1, gmixed, m0, m1, m2, m3, g0, g1, g2, g3, stay, go, left, right, a, b, sem):
    width, half = b.shape[1], stay.shape[1]
    first = gather_rows((n1,), 0, left, None, None, sem.at[0]) + gather_rows((gmixed,), 0, right, half, sc[0], sem.at[1])
    second = gather_rows((m0, m1, m2, m3), at_att, a, None, None, sem.at[2]) + gather_rows((g0, g1, g2, g3), 0, b, half, sc[0], sem.at[3])
    for copy in first:
        copy.wait()
    tall_product(left, right, stay, go, 0, WIDE)
    for copy in second:
        copy.wait()
    product = mm_tn(a[...], b[...])[: stay.shape[0] - width, :].astype(low)
    stay[width:, :] = product[:, :half]
    go[width:, :] = product[:, half:]


def add_kernel(sizes, *refs):
    count = len(sizes)
    mine, theirs = refs[:count], refs[count : 2 * count]
    norms = refs[2 * count] if len(refs) > 2 * count + 1 else None
    out = refs[-1]
    blocks, total, half = out.shape
    for b in range(blocks):
        at = 0
        for x, y, size in zip(mine, theirs, sizes):
            base = 0
            for part in size:
                step = part // blocks
                span = slice(base + b * step, base + (b + 1) * step)
                out[b, at : at + step, :] = (x[span, :].astype(full) + y[span, :].astype(full)).astype(low)
                at += step
                base += part
        if norms is not None:
            row = lax.broadcasted_iota(jnp.int32, (total - at, half), 0)
            lower, upper = norms[b : b + 1, :half], norms[b : b + 1, half:]
            out[b, at:, :] = jnp.where(row == 0, lower, jnp.where(row == 1, upper, 0.0)).astype(low)


def split_kernel(axis, sizes, sc, mine, theirs, stay, go):
    for out, flip in ((stay, 0), (go, 1)):
        for j in range(2):
            block = 2 * j + ((sc[axis] & 1) ^ flip)
            at, base = 0, 0
            for size in sizes:
                step = size // GROUP
                span = pl.ds(pl.multiple_of(base + block * step, 16), step)
                out[j, at : at + step, :] = (mine[span, :].astype(full) + theirs[span, :].astype(full)).astype(low)
                at += step
                base += size


def halve_kernel(axis, sc, held, got, stay, go):
    high = sc[axis] >> 1
    stay[...] = held[high].astype(full) + got[high].astype(full)
    go[...] = (held[1 - high].astype(full) + got[1 - high].astype(full)).astype(low)


def pack_kernel(sc, att_0, feed_0, grads_1, down_1, down_1_got, stay, go):
    step, split = down_1.shape[0], att_0.shape[0]
    parts = (
        (att_0[...], grads_1[0:split, :]),
        (feed_0[0:step, :], grads_1[split:, :]),
        (feed_0[step : 2 * step, :], (down_1[...] + down_1_got[...].astype(full)).astype(low)),
    )
    first = sc[0] == 0
    at = 0
    for zero, one in parts:
        upto = at + zero.shape[0]
        stay[at:upto, :] = jnp.where(first, zero, one)
        go[at:upto, :] = jnp.where(first, one, zero)
        at = upto


def spread_rows(out, values, start, stride):
    for j in range(values.shape[1] // LANES):
        out[pl.ds(start + j, values.shape[0], stride=stride), :] = values[:, j * LANES : (j + 1) * LANES]


def finish_kernel(sc, mine, theirs, feed_0, grad_down, grad_out, v0, v1, v2, v3, whole):
    half = mine.shape[1]
    width = 2 * half
    step = width // GROUP
    few = step // GROUP
    lanes = width // LANES
    whole[:, pl.ds(pl.multiple_of(sc[0] * half, LANES), half)] = mine[...].astype(full)
    whole[:, pl.ds(pl.multiple_of((1 - sc[0]) * half, LANES), half)] = theirs[...].astype(full)
    at_up = step + few
    spread_rows(grad_out, whole[step:at_up, :], 0, lanes)
    spread_rows(grad_down, whole[at_up + step :, :], 0, lanes)
    lower, upper = feed_0[2 * step : 2 * step + 1, :], feed_0[2 * step + 1 : 2 * step + 2, :]
    last = jnp.concatenate([lower, upper], axis=1)
    shares = [last[:, c * step : (c + 1) * step] for c in range(GROUP)]
    for k, v in enumerate((v0, v1, v2, v3)):
        at = (sc[1] ^ k) * few
        v[0:few, :] = whole[pl.ds(pl.multiple_of(at_up + at, few), few), :].astype(low)
        v[few : 2 * few, :] = whole[pl.ds(pl.multiple_of(at, few), few), :].astype(low)
        share = jnp.zeros_like(shares[0])
        for c in range(GROUP):
            share = jnp.where((sc[1] ^ k) == c, shares[c], share)
        v[2 * few :, :] = jnp.zeros((v.shape[0] - 2 * few, width), low)
        v[2 * few : 2 * few + 1, :step] = share


def place_kernel(heads, sc, v0, v1, v2, v3, grad_up, grad_qkv, grad_norms, natural, whole):
    width = v0.shape[1]
    few = natural.shape[1]
    per = width // LANES
    mine_wide = heads * HEAD_DIM
    shape = (WIDE, WIDE)
    source, out = lax.broadcasted_iota(jnp.int32, shape, 0), lane_index(shape)
    v = source & (LANES - 1)
    column = jnp.where(v < heads * HALF, (v // HALF) * HEAD_DIM + (source // LANES) * HALF + (v & (HALF - 1)), -1)
    back = jnp.where(out == column, 1.0, 0.0).astype(low)
    norm = jnp.zeros((1, mine_wide), full)
    for k, piece in enumerate((v0, v1, v2, v3)):
        spread_rows(grad_up, piece[0:few, :].astype(full), (sc[1] ^ k) * per, GROUP * per)
        for part in range(3):
            values = piece[few : 2 * few, part * WIDE : (part + 1) * WIDE]
            natural[sc[1] ^ k, :, part * WIDE : (part + 1) * WIDE] = values.astype(full) if part == 2 else mm(values, back)
        norm = norm + piece[2 * few : 2 * few + 1, :mine_wide].astype(full)
    grad_norms[...] = norm
    for part in range(3):
        for c in range(GROUP):
            to = (part * GROUP + c) * mine_wide
            whole[:, to : to + mine_wide] = natural[c, :, part * WIDE : part * WIDE + mine_wide]
    spread_rows(grad_qkv, whole[...], 0, whole.shape[1] // LANES)


class Late:
    def __init__(self, source, held, sem):
        self.copy, self.held, self.shape, self.here = pltpu.make_async_copy(source, held, sem), held, held.shape, False
        self.copy.start()

    def __getitem__(self, index):
        if not self.here:
            self.copy.wait()
            self.here = True
        return self.held[index]


def run(kernel, shapes, scratch, operands, spaces):
    place = {"s": pltpu.SMEM, "v": pltpu.VMEM, "a": pl.ANY, "h": pltpu.HBM}
    total = len(operands) + len(shapes) + len(scratch)
    late = [i for i, space in enumerate(spaces) if space == "h"]
    held = [pltpu.VMEM(operands[i].shape, operands[i].dtype) for i in late]

    def body(*refs):
        given = list(refs[:total])
        for n, i in enumerate(late):
            given[i] = Late(given[i], refs[total + n], refs[-1].at[n])
        kernel(*given)
        for i in late:
            given[i][...]

    return pl.pallas_call(
        body,
        out_shape=[jax.ShapeDtypeStruct(shape, kind) for shape, kind in shapes],
        in_specs=[pl.BlockSpec(memory_space=place[space]) for space in spaces],
        out_specs=[pl.BlockSpec(memory_space=pltpu.VMEM) for _ in shapes],
        scratch_shapes=[*scratch, *held, pltpu.SemaphoreType.DMA((len(held),))] if held else scratch,
        compiler_params=pltpu.CompilerParams(vmem_limit_bytes=52 * 2**20),
        cost_estimate=pl.CostEstimate(flops=1, bytes_accessed=1, transcendentals=0),
    )(*operands)


def exchange(value):
    values = value if isinstance(value, (list, tuple)) else [value] * GROUP
    return [values[0]] + [
        lax.ppermute(values[k], "ctx", [(i, i ^ k) for i in range(GROUP)]) for k in range(1, GROUP)
    ]


def towards(value, k):
    return lax.ppermute(value, "ctx", [(i, i ^ k) for i in range(GROUP)])


def along(value, k):
    count = lax.axis_size("dp")
    return lax.ppermute(value, "dp", [(i, i ^ k) for i in range(count)])


def swap(value):
    return lax.ppermute(value, "section", [(0, 1), (1, 0)])


def together(*values):
    return lax.optimization_barrier(values)


def on_device(tokens, cotangent, seq_bound, ln1_gain, ln1_shift, w_qkv, w_out, ln2_gain, ln2_shift, w_up, w_down):
    section = lax.axis_index("section")
    me = lax.axis_index("ctx")
    shards = lax.axis_size("dp")
    z = lax.axis_index("dp")
    rows, width = tokens.shape[1:]
    feed_width = w_up.shape[2]
    chunk = feed_width // GROUP
    heads = width // HEAD_DIM // GROUP
    mine_wide = heads * HEAD_DIM
    length = GROUP * rows
    few = width // (GROUP * shards)
    bound = lax.dynamic_index_in_dim(seq_bound[0], section, 0, keepdims=False)
    sc = jnp.stack([section, me, bound, z]).astype(jnp.int32)

    dma = pltpu.SemaphoreType.DMA
    vm = pltpu.VMEM
    piece = ((rows, width), low)
    wide_piece = ((rows, width), full)
    pair = ((2, width), full)

    x = lax.dynamic_index_in_dim(tokens, section, 0, keepdims=False)
    gathered = exchange(x)
    wq_own, wo_own, up_own, dn_own = w_qkv[0], w_out[0], w_up[0], w_down[0]
    wq_oth, wo_oth = swap(wq_own), swap(wo_own)
    norms_own = jnp.concatenate([ln1_gain, ln1_shift, ln2_gain, ln2_shift], axis=0)
    wo_oth, later = together(wo_oth, norms_own)
    norms_oth = swap(later)
    wq_oth, norms_oth, later = together(wq_oth, norms_oth, up_own)
    up_oth = swap(later)
    *gathered, later = together(*gathered, dn_own)
    dn_oth = swap(later)

    def attend(layer, gathered, *tables):
        table = ((length, LANES), full)
        given = len(tables)
        return run(
            functools.partial(attend_kernel, layer, heads),
            [table] * (2 - given) + [((length, width), low), ((length, 3 * WIDE), low), ((heads, length, length), low)] + [((rows, mine_wide), low)] * GROUP,
            [vm((3, width, WIDE), low), vm((width, 3 * WIDE), low), dma((3,))],
            (sc, *gathered, norms_own, norms_oth, *tables, wq_own, wq_oth),
            "svvvvvv" + "v" * given + "aa",
        )

    def attend_back(layer, grads, qkv, probs):
        return run(
            functools.partial(attend_back_kernel, layer, heads),
            [((length, 3 * WIDE), low)] + [piece] * GROUP,
            [
                vm((mine_wide, width), low), vm((3, width, WIDE), low), vm((width, 3 * WIDE), low), vm((length, WIDE), low),
                vm((heads * length, length), low), vm((heads * length, WIDE), low), vm((heads * length, WIDE), low), dma((4,)),
            ],
            (sc, *grads, qkv, probs, cos, sin, wo_own, wo_oth, wq_own, wq_oth),
            "svvvvvvvvaaaa",
        )

    half = width // 2

    def pair_grads(*products):
        out = ((width, half), low)
        operands = [piece for lefts, rights, _, _ in products for piece in (*lefts, *rights)]
        places = [(at_left, at_right) for _, _, at_left, at_right in products]
        return run(
            functools.partial(pair_grads_kernel, places),
            [out] * (2 * len(products)),
            [vm((len(products), length, width), low), vm((len(products), length, width), low), dma((2 * len(products), 2 * GROUP))],
            (sc, *operands), "s" + "a" * len(operands),
        )

    def attend_grads(n1, gmixed, fwd, ga, at_att):
        return run(
            functools.partial(attend_grads_kernel, at_att),
            [((width + mine_wide, half), low)] * 2,
            [vm((length, width), low), vm((length, 3 * WIDE), low), vm((length, WIDE), low), vm((length, width), low), dma((4, 2 * GROUP))],
            (sc, n1, gmixed, *fwd, *ga), "s" + "a" * (2 + 2 * GROUP),
        )

    square, attend_size = (width,), (width, mine_wide)

    def blocks_of(sizes, mine, theirs, *norms):
        total = sum(sum(size) for size in sizes) // shards + (16 if norms else 0)
        if small:
            (blocks,) = run(
                functools.partial(add_kernel, sizes), [((shards, total, half), low)], [], (*mine, *theirs, *norms),
                "v" * (2 * len(mine) + len(norms)),
            )
        else:
            parts = []
            for x, y, size in zip(mine, theirs, sizes):
                value = (x.astype(full) + y.astype(full)).astype(low)
                base = 0
                for part in size:
                    parts.append(value[base : base + part].reshape(shards, part // shards, half))
                    base += part
            blocks = jnp.concatenate(parts, axis=1)
        return blocks

    def over_dp(blocks):
        return lax.psum_scatter(blocks, "dp", scatter_dimension=0, tiled=False)

    def split(axis, sizes, mine, theirs):
        part = ((2, sum(sizes) // GROUP, half), low)
        return run(functools.partial(split_kernel, axis, sizes), [part, part], [], (sc, mine, theirs), "svv")

    def halve(axis, stay, got):
        part = stay.shape[1:]
        return run(functools.partial(halve_kernel, axis), [(part, full), (part, low)], [], (sc, stay, got), "svv")

    def level(token, *values):
        token, *values = together(token, *values)
        return together(swap(token), *values)[1:]

    feed_scratch = [vm((GROUP, width, chunk), low), vm((GROUP, chunk, width), low)]
    out_scratch = vm((GROUP, mine_wide, width), low)
    split_scratch = [vm((GROUP, rows, chunk), low), vm((GROUP, rows, WIDE), low)]
    small = shards == GROUP
    owner, other_way = (3, along) if small else (1, towards)

    cos, sin, n1_0, qkv_0, probs_0, *att = attend(0, gathered)
    att = exchange(att)
    weights = (wo_own, wo_oth, up_own, up_oth, dn_own, dn_oth)
    cot = lax.dynamic_index_in_dim(cotangent, section, 0, keepdims=False)
    *att, cot = together(*att, cot)
    y0, hidden_0, slope_0, *fwd_0 = run(
        functools.partial(feed_kernel, 0, shards),
        [piece, wide_piece, ((rows, feed_width), low)] + [((rows, 2 * width + WIDE), low)] * GROUP,
        [out_scratch, *feed_scratch, *split_scratch, dma((3 * GROUP,))],
        (sc, x, *att, norms_own, norms_oth, *weights),
        "svvvvvvvaaaaaa",
    )
    gathered_1 = exchange(y0)
    cots = [cot, other_way(cot, 1), None, other_way(cot, 3)]
    *gathered_1, fwd_0[1], fwd_0[2], cots[1], cots[3] = together(*gathered_1, fwd_0[1], fwd_0[2], cots[1], cots[3])
    fwd_0[1], fwd_0[2] = towards(fwd_0[1], 1), towards(fwd_0[2], 2)
    n1_1, qkv_1, probs_1, *att = attend(1, gathered_1, cos, sin)
    *att, fwd_0[1], fwd_0[2], fwd_0[3] = together(*att, *fwd_0[1:])
    att = exchange(att)
    fwd_0[3] = towards(fwd_0[3], 3)
    y1, gh_1, dn2_1, *rest = run(
        functools.partial(feed_turn_kernel, 1, shards, owner),
        [piece, wide_piece, pair] + [((rows, width + WIDE), low)] * GROUP + [((rows, 2 * width), low)] * GROUP + [piece] * GROUP,
        [
            out_scratch, *feed_scratch, *split_scratch, vm((rows, width), full), vm((rows, feed_width), low),
            vm((GROUP, rows, chunk), low), dma((3 * GROUP,)),
        ],
        (sc, y0, *att, norms_own, norms_oth, cot, *weights),
        "svvvvvvvvaaaaaa",
    )
    ga, up_1, down_1 = rest[:GROUP], rest[GROUP : 2 * GROUP], rest[2 * GROUP :]
    *ga, fwd_0[3] = together(*ga, fwd_0[3])
    ga_1 = exchange(ga)
    cots[2] = other_way(cot, 2)
    *ga_1, cots[2], down_1[1], down_1[3], up_1[1], up_1[2] = together(*ga_1, cots[2], down_1[1], down_1[3], up_1[1], up_1[2])
    up_1[1], up_1[2] = towards(up_1[1], 1), towards(up_1[2], 2)
    gmixed_1, *back = attend_back(1, ga_1, qkv_1, probs_1)
    *back, up_1[1], up_1[2], up_1[3], down_1[1], down_1[3] = together(*back, *up_1[1:], down_1[1], down_1[3])
    back = exchange(back)
    down_1[1], down_1[3] = other_way(down_1[1], 1), other_way(down_1[3], 3)
    att_1, att_1_go = attend_grads(n1_1, gmixed_1, ga_1, ga_1, width)
    *back, down_1[1], down_1[2], down_1[3], up_1[3], att_1, att_1_go = together(*back, *down_1[1:], up_1[3], att_1, att_1_go)
    up_1[3] = towards(up_1[3], 3)
    att_1_got = swap(att_1_go)
    gx_1, dn1_1, ga, gh_0, dn2_0, *bwd_0 = run(
        functools.partial(turn_kernel, 0),
        [wide_piece, pair, piece, wide_piece, pair] + [((rows, 2 * width), low)] * GROUP,
        [*feed_scratch, vm((GROUP, rows, chunk), low), dma((2 * GROUP,))],
        (sc, *back, gh_1, y0, hidden_0, slope_0, norms_own, norms_oth, up_own, up_oth, dn_own, dn_oth),
        "svvvvvvvvvvaaaa",
    )
    ga, att_1_got, up_1[3], down_1[2] = together(ga, att_1_got, up_1[3], down_1[2])
    ga_0 = exchange(ga)
    down_1[2] = other_way(down_1[2], 2)
    up_1_stay, up_1_go = pair_grads((up_1, up_1, 0, width))
    up_1_got = swap(up_1_go)
    grads_1 = blocks_of([attend_size, square], [att_1, up_1_stay], [att_1_got, up_1_got])
    *ga_0, grads_1, bwd_0[1], bwd_0[2], down_1[2] = together(*ga_0, grads_1, bwd_0[1], bwd_0[2], down_1[2])
    sum_1 = over_dp(grads_1)
    bwd_0[1], bwd_0[2] = towards(bwd_0[1], 1), towards(bwd_0[2], 2)
    gmixed_0, *back = attend_back(0, ga_0, qkv_0, probs_0)
    gmixed_0, *back, bwd_0[1], bwd_0[2], bwd_0[3] = together(gmixed_0, *back, *bwd_0[1:])
    bwd_0[3] = towards(bwd_0[3], 3)
    back = exchange(back)
    att_0, att_0_go = attend_grads(n1_0, gmixed_0, fwd_0, ga_0, 2 * width)
    *back, bwd_0[3], att_0, att_0_go = together(*back, bwd_0[3], att_0, att_0_go)
    att_0_got = swap(att_0_go)
    kept, sent, sums, sums_sent = run(
        last_kernel, [wide_piece, wide_piece, ((4, width), full), ((4, width), full)],
        [vm((rows, width), full), vm((2, width), full)],
        (sc, *back, gh_0, x, norms_own, norms_oth, gx_1, dn1_1, dn2_1, dn2_0), "svvvvvvvvvvvv",
    )
    sums, sums_sent, att_0_got, bwd_0[3], sum_1 = together(sums, sums_sent, att_0_got, bwd_0[3], sum_1)
    grads_0 = blocks_of([attend_size], [att_0], [att_0_got])
    grads_0, bwd_0[3] = together(grads_0, bwd_0[3])
    sum_0 = over_dp(grads_0)
    sums_got = swap(sums_sent)
    up_0, up_0_go, down_0, down_0_go = pair_grads((fwd_0, bwd_0, 0, 0), (fwd_0, bwd_0, width, width))
    up_0, up_0_go, down_0, down_0_go, sums_got = together(up_0, up_0_go, down_0, down_0_go, sums_got)
    up_0_got, down_0_got = swap(up_0_go), swap(down_0_go)
    sums = sums + sums_got
    down_1_stay, down_1_go = pair_grads((down_1, cots, 0, 0))
    up_0_got, down_0_got, down_1_stay, down_1_go = together(up_0_got, down_0_got, down_1_stay, down_1_go)
    down_1_got = swap(down_1_go)
    if small:
        sum_feed_0 = over_dp(blocks_of([square, square], [up_0, down_0], [up_0_got, down_0_got], sums))
        down_1_stay, down_1_go = split(1, square, down_1_stay, down_1_got)
        down_1_stay, down_1_go = halve(1, down_1_stay, towards(down_1_go, 1))
        tall = width // shards
        lanes = width // LANES
        everything = ((3 * tall + few, half), low)
        mine, other = run(
            pack_kernel, [everything, everything], [],
            (sc, sum_0, sum_feed_0, sum_1, down_1_stay, towards(down_1_go, 2)), "shhhvv",
        )
        grad_down, grad_out, *pieces = run(
            finish_kernel,
            [((tall * lanes, LANES), full), ((few * lanes, LANES), full)] + [((2 * few + 16, width), low)] * GROUP,
            [vm((3 * tall + few, width), full)],
            (sc, mine, swap(other), sum_feed_0), "svvv",
        )
        grad_up, grad_qkv, grad_norms = run(
            functools.partial(place_kernel, heads),
            [((few * GROUP * lanes, LANES), full), ((few * 3 * lanes, LANES), full), ((1, mine_wide), full)],
            [vm((GROUP, few, 3 * WIDE), full), vm((few, 3 * width), full)],
            (sc, *exchange(pieces)), "s" + "v" * GROUP,
        )
    else:
        sum_feed_0 = over_dp(blocks_of([square, square], [up_0, down_0], [up_0_got, down_0_got]))
        sum_down_1 = over_dp(blocks_of([square], [down_1_stay], [down_1_got]))
        grad_up, grad_down, grad_out, grad_qkv = many_shards(
            me, section, heads, few, jnp.concatenate([sum_0, sum_feed_0]), jnp.concatenate([sum_1, sum_down_1])
        )
        grad_norms = lax.psum_scatter(sums.reshape(shards * GROUP, -1), ("dp", "ctx"), scatter_dimension=0, tiled=True)

    def by_section(own, got):
        return jnp.where(section == 0, jnp.stack([own, got]), jnp.stack([got, own]))[None]

    y_own, y_sent = jnp.where(section == 0, y0, y1), jnp.where(section == 0, y1, y0)
    return (
        by_section(y_own, swap(y_sent)),
        by_section(kept, swap(sent)),
        grad_qkv.reshape(1, -1),
        grad_out.reshape(1, -1),
        grad_up.reshape(1, -1),
        grad_down.reshape(1, -1),
        grad_norms.reshape(1, -1),
    )


def many_shards(me, section, heads, few, first, second):
    own, other = jnp.where(section == 0, first, second), jnp.where(section == 0, second, first)
    got = swap(other)
    whole = jnp.where(section == 0, jnp.concatenate([own, got], axis=1), jnp.concatenate([got, own], axis=1))
    width = whole.shape[1]
    chunk, tall = width, GROUP * few
    t_qkv, t_out, t_up, t_down = whole[:tall], whole[tall : tall + few], whole[tall + few : 2 * tall + few], whole[2 * tall + few :]
    slim = jnp.concatenate([t_up, t_qkv], axis=1)
    slim = slim.reshape(GROUP, slim.shape[0] // GROUP, slim.shape[1])
    gets = jnp.stack(exchange([lax.dynamic_index_in_dim(slim, me ^ k, 0, keepdims=False) for k in range(GROUP)]))
    gets = jnp.stack([lax.dynamic_index_in_dim(gets, me ^ k, 0, keepdims=False) for k in range(GROUP)]).astype(full)
    few = gets.shape[1]
    grad_up = jnp.transpose(gets[:, :, :chunk], (1, 0, 2))
    cols = gets[:, :, chunk:].reshape(GROUP, few, 3, WIDE)
    turned = cols[:, :, :2].reshape(GROUP, few, 2, 2, LANES)[..., : heads * HALF]
    turned = turned.reshape(GROUP, few, 2, 2, heads, HALF).transpose(1, 2, 0, 4, 3, 5).reshape(few, 2 * width)
    plain = cols[:, :, 2, : heads * HEAD_DIM].transpose(1, 0, 2).reshape(few, width)
    return grad_up, t_down.astype(full), t_out.astype(full), jnp.concatenate([turned, plain], axis=1)


def solution(mesh):
    in_specs = (
        P(None, ("dp", "ctx"), None),
        P(None, ("dp", "ctx"), None),
        P("dp", None),
        P("section", None),
        P("section", None),
        P("section", None, None),
        P("section", None, None),
        P("section", None),
        P("section", None),
        P("section", None, None),
        P("section", None, None),
    )
    out_specs = (
        P("section", None, ("dp", "ctx"), None),
        P("section", None, ("dp", "ctx"), None),
        P("section", ("dp", "ctx")),
        P("section", ("dp", "ctx")),
        P("section", ("dp", "ctx")),
        P("section", ("dp", "ctx")),
        P("section", ("dp", "ctx")),
    )
    return jax.shard_map(
        on_device, mesh=mesh, in_specs=in_specs, out_specs=out_specs, check_vma=False
    )
```

```python
import functools
import math

import jax
import jax.numpy as jnp
from jax import lax
from jax.experimental import pallas as pl
from jax.experimental.pallas import tpu as pltpu
from jax.sharding import PartitionSpec as P

HEAD_DIM = 64
HALF = HEAD_DIM // 2
GROUP = 4
LANES = 128
WIDE = 2 * LANES

epsilon = 1e-05
rotary_base = 10000.0
masked_score = -1e30
low = jnp.bfloat16
full = jnp.float32

NT = (((1,), (1,)), ((), ()))
TN = (((0,), (0,)), ((), ()))


def mm(a, b):
    return jnp.dot(a, b, preferred_element_type=full)


def mm_nt(a, b):
    return lax.dot_general(a, b, NT, preferred_element_type=full)


def mm_tn(a, b):
    return lax.dot_general(a, b, TN, preferred_element_type=full)


def layer_norms(layer, sc, own, other):
    return jnp.where(sc[0] == layer, own[...], other[...])


def norm_stats(values):
    mean = jnp.mean(values, axis=-1, keepdims=True)
    centred = values - mean
    spread = jnp.mean(centred * centred, axis=-1, keepdims=True)
    scale = lax.rsqrt(spread + epsilon)
    return centred * scale, scale


def norm_backward(values, gain, grad):
    hat, scale = norm_stats(values)
    grad_gain = jnp.sum(grad * hat, axis=0, keepdims=True)
    grad_shift = jnp.sum(grad, axis=0, keepdims=True)
    inner = grad * gain
    first = jnp.mean(inner, axis=-1, keepdims=True)
    second = jnp.mean(inner * hat, axis=-1, keepdims=True)
    return scale * (inner - first - hat * second), grad_gain, grad_shift


def gelu_both(u):
    bell = jnp.exp(-0.5 * u * u)
    z = jnp.abs(u) * (0.5**0.5)
    t = 1.0 / (1.0 + 0.3275911 * z)
    poly = t * (
        0.254829592 + t * (-0.284496736 + t * (1.421413741 + t * (-1.453152027 + t * 1.061405429)))
    )
    tail = 0.5 * poly * bell
    cdf = jnp.where(u >= 0, 1.0 - tail, tail)
    return u * cdf, cdf + u * bell * (1.0 / math.sqrt(2.0 * math.pi))


class Fetch:
    def __init__(self, own, other, use_own, place, target, sem):
        self.parts = (own, other, use_own, place, target, sem)

    def start(self):
        own, other, use_own, place, target, sem = self.parts

        @pl.when(use_own)
        def _():
            pltpu.make_async_copy(own.at[place], target, sem).start()

        @pl.when(jnp.logical_not(use_own))
        def _():
            pltpu.make_async_copy(other.at[place], target, sem).start()

    def wait(self):
        own, other, use_own, place, target, sem = self.parts
        pltpu.make_async_copy(own.at[place], target, sem).wait()


def lane_index(shape):
    return lax.broadcasted_iota(jnp.int32, shape, 1)


def half_mask(head):
    return ((lane_index((1, WIDE)) & (LANES - 1)) // HALF) == head


def value_mask(head):
    return (lane_index((1, WIDE)) // HEAD_DIM) == head


def keep(values, mask):
    return jnp.where(mask, values, jnp.zeros_like(values))


class ProjectionWeights:
    def __init__(self, me, heads, mine, own, other, windows, target, sem):
        total = own.shape[0]
        at = me * (heads * HEAD_DIM)
        self.shift = lax.rem(at, LANES)
        start = at - self.shift
        self.windows, self.target, self.heads = windows, target, heads
        self.parts = []
        for part in range(3):
            span = pl.ds(pl.multiple_of(part * total + start, LANES), WIDE)
            self.parts.append(Fetch(own, other, mine, (slice(None), span), windows.at[part], sem.at[part]))

    def start(self):
        for part in self.parts:
            part.start()

    def wait(self):
        shape = (WIDE, WIDE)
        source, u = lax.broadcasted_iota(jnp.int32, shape, 0), lane_index(shape)
        v = u & (LANES - 1)
        turned = jnp.where(v < self.heads * HALF, (v // HALF) * HEAD_DIM + (u // LANES) * HALF + (v & (HALF - 1)) + self.shift, -1)
        plain = jnp.where(u < self.heads * HEAD_DIM, u + self.shift, -1)
        turned = jnp.where(source == turned, 1.0, 0.0).astype(low)
        plain = jnp.where(source == plain, 1.0, 0.0).astype(low)
        for part in range(3):
            self.parts[part].wait()
            chosen = mm(self.windows[part], plain if part == 2 else turned)
            self.target[:, part * WIDE : (part + 1) * WIDE] = chosen.astype(low)


def rotary_tables(me, bound, rows, cos, sin):
    for k in range(GROUP):
        here = slice(k * rows, (k + 1) * rows)
        spot = (me ^ k) * rows + lax.broadcasted_iota(jnp.int32, (rows, LANES), 0)
        relative = (spot - jnp.where(spot >= bound, bound, 0)).astype(full)
        steps = (lane_index((rows, LANES)) & (HALF - 1)).astype(full)
        angles = relative * jnp.exp(-math.log(rotary_base) * 2.0 * steps / HEAD_DIM)
        cos[here, :] = jnp.cos(angles)
        sin[here, :] = jnp.sin(angles)


def attend_kernel(layer, heads, sc, x0, x1, x2, x3, norms_own, norms_oth, *refs):
    if layer == 0:
        w_own, w_oth, cos, sin, n1, qkv, probs, a0, a1, a2, a3, win, w, mixed, scores, sem = refs
    else:
        cos, sin, w_own, w_oth, n1, qkv, probs, a0, a1, a2, a3, win, w, mixed, scores, sem = refs
    rows = x0.shape[0]
    weights = ProjectionWeights(sc[1], heads, sc[0] == layer, w_own, w_oth, win, w, sem)
    weights.start()
    if layer == 0:
        rotary_tables(sc[1], sc[2], rows, cos, sin)
    norms = layer_norms(layer, sc, norms_own, norms_oth)
    gain, shift = norms[0:1, :], norms[1:2, :]
    for k, x in enumerate((x0, x1, x2, x3)):
        hat, _ = norm_stats(x[...].astype(full))
        n1[k * rows : (k + 1) * rows, :] = (hat * gain + shift).astype(low)
    weights.wait()
    mixed[...] = mm(n1[...], w[...])
    for k in range(GROUP):
        here = slice(k * rows, (k + 1) * rows)
        c, s = cos[here, :], sin[here, :]
        for part in range(2):
            base = part * WIDE
            v1, v2 = mixed[here, base : base + LANES], mixed[here, base + LANES : base + WIDE]
            qkv[here, base : base + LANES] = (v1 * c - v2 * s).astype(low)
            qkv[here, base + LANES : base + WIDE] = (v2 * c + v1 * s).astype(low)
        qkv[here, 2 * WIDE :] = mixed[here, 2 * WIDE :].astype(low)
    me, bound = sc[1], sc[2]
    length = GROUP * rows
    spot = lax.broadcasted_iota(jnp.int32, (1, length), 1)
    place = jnp.zeros((1, length), jnp.int32)
    for k in range(GROUP):
        place = jnp.where(spot // rows == k, (me ^ k) * rows + spot - k * rows, place)
    seq_col = (place >= bound).astype(jnp.int32)
    for h in range(heads):
        scores[h] = mm_nt(keep(qkv[:, 0:WIDE], half_mask(h)), qkv[:, WIDE : 2 * WIDE])
    for h in range(heads):
        for k in range(GROUP):
            here = slice(k * rows, (k + 1) * rows)
            own = (me ^ k) * rows + lax.broadcasted_iota(jnp.int32, (rows, 1), 0)
            same = (own >= bound).astype(jnp.int32) == seq_col
            score = jnp.where(same, scores[h, here, :] * (HEAD_DIM**-0.5), masked_score)
            top = jnp.max(score, axis=-1, keepdims=True)
            expo = jnp.exp(score - top)
            probs[h, here, :] = (expo * (1.0 / jnp.sum(expo, axis=-1, keepdims=True))).astype(low)
    total = mm(probs[0], keep(qkv[:, 2 * WIDE :], value_mask(0)))
    for h in range(1, heads):
        total = total + mm(probs[h], keep(qkv[:, 2 * WIDE :], value_mask(h)))
    for k, out in enumerate((a0, a1, a2, a3)):
        out[...] = total[k * rows : (k + 1) * rows, : heads * HEAD_DIM].astype(low)


def attend_back_kernel(layer, heads, sc, g0, g1, g2, g3, qkv, probs, cos, sin, wo_own, wo_oth, w_own, w_oth, gmixed, p0, p1, p2, p3, wo, win, w, go, gs, qm, gom, ga, gp, sem):
    rows = g0.shape[0]
    width = heads * HEAD_DIM
    me = sc[1]
    mine = sc[0] == layer
    span = pl.ds(pl.multiple_of(me * width, HEAD_DIM), width)
    fetch_o = Fetch(wo_own, wo_oth, mine, (span, slice(None)), wo, sem.at[3])
    fetch_w = ProjectionWeights(me, heads, mine, w_own, w_oth, win, w, sem)
    fetch_o.start()
    fetch_w.start()
    length = GROUP * rows
    for k, g in enumerate((g0, g1, g2, g3)):
        ga[k * rows : (k + 1) * rows, :] = g[:, : wo.shape[1]]
    go[:, LANES:] = jnp.zeros((length, WIDE - LANES), low)
    fetch_o.wait()
    go[:, :width] = mm_nt(ga[...], wo[...]).astype(low)
    for h in range(heads):
        there = slice(h * length, (h + 1) * length)
        gom[there, :] = keep(go[...], value_mask(h))
        qm[there, :] = keep(qkv[:, 0:WIDE], half_mask(h))
        gp[h] = mm_nt(gom[there, :], qkv[:, 2 * WIDE :])
    for h in range(heads):
        for k in range(GROUP):
            here = slice(k * rows, (k + 1) * rows)
            p, g = probs[h, here, :].astype(full), gp[h, here, :]
            inner = jnp.sum(p * g, axis=-1, keepdims=True)
            gs[h * length + k * rows : h * length + (k + 1) * rows, :] = (p * (g - inner)).astype(low)
    gq = mm(gs[0:length, :], keep(qkv[:, WIDE : 2 * WIDE], half_mask(0)))
    gv = mm_tn(probs[0], gom[0:length, :])
    for h in range(1, heads):
        there = slice(h * length, (h + 1) * length)
        gq = gq + mm(gs[there, :], keep(qkv[:, WIDE : 2 * WIDE], half_mask(h)))
        gv = gv + mm_tn(probs[h], gom[there, :])
    gk = mm_tn(gs[...], qm[...])
    for base, value in ((0, gq), (WIDE, gk)):
        value = value * (HEAD_DIM**-0.5)
        v1, v2 = value[:, :LANES], value[:, LANES:]
        gmixed[:, base : base + LANES] = (v1 * cos[...] + v2 * sin[...]).astype(low)
        gmixed[:, base + LANES : base + WIDE] = (v2 * cos[...] - v1 * sin[...]).astype(low)
    gmixed[:, 2 * WIDE :] = gv.astype(low)
    fetch_w.wait()
    back = mm_nt(gmixed[...], w[...]).astype(low)
    for k, out in enumerate((p0, p1, p2, p3)):
        out[...] = back[k * rows : (k + 1) * rows, :]


class FeedWeights:
    def __init__(self, mine, up_own, up_oth, dn_own, dn_oth, wu, wd, sem, first):
        width = wu.shape[1]
        self.wu, self.wd = wu, wd
        self.up, self.down = [], []
        for j in range(GROUP):
            cut = slice(j * width, (j + 1) * width)
            self.up.append(Fetch(up_own, up_oth, mine, (slice(None), cut), wu.at[j], sem.at[first + j]))
            self.down.append(Fetch(dn_own, dn_oth, mine, (cut, slice(None)), wd.at[j], sem.at[first + GROUP + j]))


def feed_forward(sc, x, atts, norms, fetch_o, wo, feed, shards, y, hidden, slope, owner, parts, cols):
    rows, width = x.shape
    heads_wide = atts[0].shape[1]
    me = sc[1]
    for k in range(GROUP):
        fetch_o[k].wait()
    state = x[...].astype(full)
    for k in range(GROUP):
        state = state + mm(atts[k][...], wo[k])
        cols[me ^ k, :, :heads_wide] = atts[k][...]
    hidden[...] = state
    hat, _ = norm_stats(state)
    n2 = (hat * norms[2:3, :] + norms[3:4, :]).astype(low)
    step = width // (GROUP * shards)
    shares = []
    for target in range(GROUP):
        pieces = []
        for z in range(shards):
            at = (z * GROUP + target) * step
            pieces.append(cols[at // heads_wide, :, at % heads_wide : at % heads_wide + step])
        pieces.append(jnp.zeros((rows, WIDE - heads_wide), low))
        shares.append(jnp.concatenate(pieces, axis=1))
    for target in range(GROUP):
        cols[target] = shares[target]
    out = jnp.zeros((rows, width), full)
    chunk = feed.wu.shape[2]
    feed.up[0].wait()
    upward, act = mm(n2, feed.wu[0]), None
    for j in range(GROUP + 1):
        if j + 1 < GROUP:
            feed.up[j + 1].wait()
        if j < GROUP:
            feed.down[j].wait()
        before, now = act, upward
        if j + 1 < GROUP:
            upward = mm(n2, feed.wu[j + 1])
        if j < GROUP:
            act, grad = gelu_both(now)
            act = act.astype(low)
            slope[:, j * chunk : (j + 1) * chunk] = grad.astype(low)
            if owner == 3:
                parts[j] = act
            else:
                span = chunk // shards
                for b in range(chunk // span):
                    z, target = divmod(j * (chunk // span) + b, GROUP)
                    parts[target, :, z * span : (z + 1) * span] = act[:, b * span : (b + 1) * span]
        if before is not None:
            out = out + mm(before, feed.wd[j - 1])
    y[...] = (hidden[...] + out).astype(low)
    return n2


def feed_back(gf, grad_out, norms, feed, hidden, slope, gas, gh, dnorm, gu, waited):
    rows, width = gf.shape
    chunk = feed.wu.shape[2]
    grad = jnp.zeros((rows, width), full)
    if not waited:
        feed.down[0].wait()
    active, before = mm_nt(gf, feed.wd[0]), None
    for j in range(GROUP + 1):
        if not waited and j + 1 < GROUP:
            feed.down[j + 1].wait()
        if not waited and j < GROUP:
            feed.up[j].wait()
        last, now = before, active
        if j + 1 < GROUP:
            active = mm_nt(gf, feed.wd[j + 1])
        if j < GROUP:
            before = (now * slope[:, j * chunk : (j + 1) * chunk].astype(full)).astype(low)
            gu[j] = before
        if last is not None:
            grad = grad + mm_nt(last, feed.wu[j - 1])
    back, d_gain, d_shift = norm_backward(hidden[...], norms[2:3, :], grad)
    total = grad_out + back
    gh[...] = total
    for ga in gas:
        ga[:, 0:width] = total.astype(low)
    dnorm[0:1, :] = d_gain
    dnorm[1:2, :] = d_shift


def start_out(sc, mine, wo_own, wo_oth, wo, sem):
    width = wo.shape[1]
    out = []
    for k in range(GROUP):
        span = pl.ds(pl.multiple_of((sc[1] ^ k) * width, HEAD_DIM), width)
        out.append(Fetch(wo_own, wo_oth, mine, (span, slice(None)), wo.at[k], sem.at[k]))
    return out


def touch(x, spare, sem):
    copy = pltpu.make_async_copy(x.at[0 : spare.shape[0], :], spare, sem)
    copy.start()
    copy.wait()


def feed_kernel(layer, shards, sc, x, a0, a1, a2, a3, norms_own, norms_oth, wo_own, wo_oth, up_own, up_oth, dn_own, dn_oth, y, hidden, slope, m0, m1, m2, m3, wo, wu, wd, parts, cols, spare, spare_sem, sem):
    mine = sc[0] == layer
    norms = layer_norms(layer, sc, norms_own, norms_oth)
    fetch_o = start_out(sc, mine, wo_own, wo_oth, wo, sem)
    feed = FeedWeights(mine, up_own, up_oth, dn_own, dn_oth, wu, wd, sem, GROUP)
    for f in fetch_o + [f for pair in zip(feed.up, feed.down) for f in pair]:
        f.start()
    touch(x, spare, spare_sem)
    n2 = feed_forward(sc, x, (a0, a1, a2, a3), norms, fetch_o, wo, feed, shards, y, hidden, slope, 1, parts, cols)
    width = x.shape[1]
    for k, m in enumerate((m0, m1, m2, m3)):
        m[:, 0:width] = n2
        m[:, width : 2 * width] = parts[sc[1] ^ k]
        m[:, 2 * width :] = cols[sc[1] ^ k]


def feed_turn_kernel(layer, shards, owner, sc, x, a0, a1, a2, a3, norms_own, norms_oth, cot, wo_own, wo_oth, up_own, up_oth, dn_own, dn_oth, y, gh, dnorm, g0, g1, g2, g3, m0, m1, m2, m3, d0, d1, d2, d3, wo, wu, wd, parts, cols, hidden, slope, gu, sem):
    mine = sc[0] == layer
    norms = layer_norms(layer, sc, norms_own, norms_oth)
    fetch_o = start_out(sc, mine, wo_own, wo_oth, wo, sem)
    feed = FeedWeights(mine, up_own, up_oth, dn_own, dn_oth, wu, wd, sem, GROUP)
    for f in fetch_o + [f for pair in zip(feed.up, feed.down) for f in pair]:
        f.start()
    gas = (g0, g1, g2, g3)
    n2 = feed_forward(sc, x, (a0, a1, a2, a3), norms, fetch_o, wo, feed, shards, y, hidden, slope, owner, parts, cols)
    gf = cot[...]
    feed_back(gf, gf.astype(full), norms, feed, hidden, slope, gas, gh, dnorm, gu, True)
    width = x.shape[1]
    for k, (g, m, d) in enumerate(((g0, m0, d0), (g1, m1, d1), (g2, m2, d2), (g3, m3, d3))):
        g[:, width:] = cols[sc[1] ^ k]
        m[:, 0:width] = n2
        m[:, width:] = gu[sc[1] ^ k]
        d[...] = parts[sc[owner] ^ k]


def turn_kernel(layer, sc, r0, r1, r2, r3, gh_in, x_in, hidden, slope, norms_own, norms_oth, up_own, up_oth, dn_own, dn_oth, gx, dnorm_in, ga, gh, dnorm, m0, m1, m2, m3, wu, wd, gu, sem):
    mine = sc[0] == layer
    feed = FeedWeights(mine, up_own, up_oth, dn_own, dn_oth, wu, wd, sem, 0)
    for f in [f for pair in zip(feed.down, feed.up) for f in pair]:
        f.start()
    norms_in = layer_norms(layer + 1, sc, norms_own, norms_oth)
    norms = layer_norms(layer, sc, norms_own, norms_oth)
    top = first_norm_back(r0, r1, r2, r3, gh_in, x_in, norms_in, gx, dnorm_in)
    gf = top.astype(low)
    feed_back(gf, gf.astype(full), norms, feed, hidden, slope, (ga,), gh, dnorm, gu, False)
    width = gf.shape[1]
    for k, m in enumerate((m0, m1, m2, m3)):
        m[:, 0:width] = gu[sc[1] ^ k]
        m[:, width:] = gf


def first_norm_back(r0, r1, r2, r3, gh_in, x_in, norms_in, gx, dnorm):
    grad = r0[...].astype(full) + r1[...].astype(full) + r2[...].astype(full) + r3[...].astype(full)
    back, d_gain, d_shift = norm_backward(x_in[...].astype(full), norms_in[0:1, :], grad)
    dnorm[0:1, :] = d_gain
    dnorm[1:2, :] = d_shift
    total = gh_in[...] + back
    gx[...] = total
    return total


def last_kernel(sc, r0, r1, r2, r3, gh_in, x_in, norms_own, norms_oth, above, d1_1, d2_1, d2_0, kept, sent, sums, sums_sent, gx, dnorm):
    first_norm_back(r0, r1, r2, r3, gh_in, x_in, layer_norms(0, sc, norms_own, norms_oth), gx, dnorm)
    first = sc[0] == 0
    kept[...] = jnp.where(first, gx[...], above[...])
    sent[...] = jnp.where(first, above[...], gx[...])
    for at, zero, one in ((0, dnorm, d1_1), (2, d2_0, d2_1)):
        sums[at : at + 2, :] = jnp.where(first, zero[...], one[...])
        sums_sent[at : at + 2, :] = jnp.where(first, one[...], zero[...])


def gather_rows(pieces, at, target, half, section, sems):
    rows, width = pieces[0].shape[0], target.shape[1]
    copies = []
    for k, piece in enumerate(pieces):
        here = pl.ds(k * rows, rows)
        if half is None:
            copies.append(pltpu.make_async_copy(piece.at[:, pl.ds(at, width)], target.at[here, :], sems.at[k]))
            continue
        for i, part in enumerate((section, 1 - section)):
            source = pl.ds(pl.multiple_of(at + part * half, LANES), half)
            copies.append(pltpu.make_async_copy(piece.at[:, source], target.at[here, pl.ds(i * half, half)], sems.at[2 * k + i]))
    for copy in copies:
        copy.start()
    return copies


def tall_product(left, right, stay, go, base, step):
    half = stay.shape[1]
    for i in range(left.shape[1] // step):
        cut, put = slice(i * step, (i + 1) * step), slice(base + i * step, base + (i + 1) * step)
        product = mm_tn(left[:, cut], right[...]).astype(low)
        stay[put, :] = product[:, :half]
        go[put, :] = product[:, half:]


def pair_grads_kernel(places, sc, *refs):
    count = len(places)
    outs, (a, b, sem) = refs[2 * GROUP * count : -3], refs[-3:]
    half = outs[0].shape[1]
    copies = []
    for i, (at_left, at_right) in enumerate(places):
        lefts, rights = refs[2 * GROUP * i :][:GROUP], refs[2 * GROUP * i + GROUP :][:GROUP]
        copies.append(
            gather_rows(lefts, at_left, a.at[i], None, None, sem.at[2 * i]) + gather_rows(rights, at_right, b.at[i], half, sc[0], sem.at[2 * i + 1])
        )
    for i in range(count):
        for copy in copies[i]:
            copy.wait()
        tall_product(a.at[i], b.at[i], outs[2 * i], outs[2 * i + 1], 0, WIDE)


def padding_place(lane):
    part, u = lane // WIDE, lane & (WIDE - 1)
    v = u & (LANES - 1)
    used, half = 3 * HALF, WIDE - HEAD_DIM
    turned = jnp.where(v >= used, part * HEAD_DIM + (u // LANES) * HALF + v - used, -1)
    plain = jnp.where(u >= half, 2 * HEAD_DIM + u - half, -1)
    return jnp.where(part < 2, turned, plain)


def attend_grads_kernel(at_att, fold, sc, n1, gmixed, m0, m1, m2, m3, g0, g1, g2, g3, stay, go, left, right, a, b, sem):
    width, half = b.shape[1], stay.shape[1]
    first = gather_rows((n1,), 0, left, None, None, sem.at[0]) + gather_rows((gmixed,), 0, right, half, sc[0], sem.at[1])
    second = gather_rows((m0, m1, m2, m3), at_att, a, None, None, sem.at[2])
    second += gather_rows((g0, g1, g2, g3), 0, b, None if fold else half, sc[0], sem.at[3])
    for copy in first:
        copy.wait()
    tall_product(left, right, stay, go, 0, WIDE)
    for copy in second:
        copy.wait()
    if not fold:
        product = mm_tn(a[...], b[...])[: stay.shape[0] - width, :].astype(low)
        stay[width:, :] = product[:, :half]
        go[width:, :] = product[:, half:]
        return
    mine_wide = 3 * HEAD_DIM
    product = mm_tn(a[...], b[...])[:mine_wide, :].astype(low)
    shape = (mine_wide, 2 * half)
    lane = lane_index(shape)
    lane = jnp.where(lane < half, lane + sc[0] * half, lane - sc[0] * half)
    spread = jnp.where(lax.broadcasted_iota(jnp.int32, shape, 0) == padding_place(lane), 1.0, 0.0).astype(low)
    few = mine_wide // GROUP
    for q in range(GROUP):
        put = mm(product[:, q * mine_wide : (q + 1) * mine_wide], spread).astype(low)
        for z in range(GROUP):
            at = slice(z * mine_wide + q * few, z * mine_wide + (q + 1) * few)
            stay[at, :] = stay[at, :] + put[z * few : (z + 1) * few, :half]
            go[at, :] = go[at, :] + put[z * few : (z + 1) * few, half:]


def add_kernel(sizes, *refs):
    count = len(sizes)
    mine, theirs = refs[:count], refs[count : 2 * count]
    norms = refs[2 * count] if len(refs) > 2 * count + 1 else None
    out = refs[-1]
    blocks, total, half = out.shape
    for b in range(blocks):
        at = 0
        for x, y, size in zip(mine, theirs, sizes):
            base = 0
            for part in size:
                step = part // blocks
                span = slice(base + b * step, base + (b + 1) * step)
                out[b, at : at + step, :] = (x[span, :].astype(full) + y[span, :].astype(full)).astype(low)
                at += step
                base += part
        if norms is not None:
            row = lax.broadcasted_iota(jnp.int32, (total - at, half), 0)
            lower, upper = norms[b : b + 1, :half], norms[b : b + 1, half:]
            out[b, at:, :] = jnp.where(row == 0, lower, jnp.where(row == 1, upper, 0.0)).astype(low)


def split_kernel(axis, sizes, sc, mine, theirs, stay, go):
    for out, flip in ((stay, 0), (go, 1)):
        for j in range(2):
            block = 2 * j + ((sc[axis] & 1) ^ flip)
            at, base = 0, 0
            for size in sizes:
                step = size // GROUP
                span = pl.ds(pl.multiple_of(base + block * step, 16), step)
                out[j, at : at + step, :] = (mine[span, :].astype(full) + theirs[span, :].astype(full)).astype(low)
                at += step
                base += size


def halve_kernel(axis, sc, held, got, stay, go):
    high = sc[axis] >> 1
    stay[...] = held[high].astype(full) + got[high].astype(full)
    go[...] = (held[1 - high].astype(full) + got[1 - high].astype(full)).astype(low)


def pack_kernel(sc, att_0, grads_1, down_1, down_1_got, stay, go):
    step, split = down_1.shape[0], att_0.shape[0]
    first = sc[0] == 0
    att = (att_0[...], grads_1[0:split, :])
    stay[0:split, :] = jnp.where(first, att[0], att[1])
    go[0:split, :] = jnp.where(first, att[1], att[0])
    down = (down_1[...] + down_1_got[...].astype(full)).astype(low)
    for out in (stay, go):
        out[split : split + step, :] = grads_1[split:, :]
        out[split + step :, :] = down


def spread_rows(out, values, start, stride):
    for j in range(values.shape[1] // LANES):
        out[pl.ds(start + j, values.shape[0], stride=stride), :] = values[:, j * LANES : (j + 1) * LANES]


def finish_kernel(sc, mine, theirs, feed_0, feed_0_got, grad_down, grad_out, v0, v1, v2, v3, whole, out):
    half = mine.shape[1]
    width = 2 * half
    step = width // GROUP
    few = step // GROUP
    lanes = width // LANES
    whole[:, pl.ds(pl.multiple_of(sc[0] * half, LANES), half)] = mine[...].astype(full)
    whole[:, pl.ds(pl.multiple_of((1 - sc[0]) * half, LANES), half)] = theirs[...].astype(full)
    at_up = step

    @pl.when(sc[0] == 0)
    def _():
        whole[at_up:, 0:half] = feed_0[0 : 2 * step, :].astype(full)
        whole[at_up:, half:] = feed_0_got[0 : 2 * step, :].astype(full)

    shape = (width, step)
    gather = jnp.where(padding_place(lax.broadcasted_iota(jnp.int32, shape, 0)) == lane_index(shape), 1.0, 0.0).astype(low)
    for q in range(GROUP):
        out[:, q * step : (q + 1) * step] = mm(whole[q * few : (q + 1) * few, :].astype(low), gather)
    spread_rows(grad_out, out[...], 0, lanes)
    spread_rows(grad_down, whole[at_up + step :, :], 0, lanes)
    lower, upper = feed_0[2 * step : 2 * step + 1, :], feed_0[2 * step + 1 : 2 * step + 2, :]
    last = jnp.concatenate([lower, upper], axis=1)
    shares = [last[:, c * step : (c + 1) * step] for c in range(GROUP)]
    for k, v in enumerate((v0, v1, v2, v3)):
        at = (sc[1] ^ k) * few
        v[0:few, :] = whole[pl.ds(pl.multiple_of(at_up + at, few), few), :].astype(low)
        v[few : 2 * few, :] = whole[pl.ds(pl.multiple_of(at, few), few), :].astype(low)
        share = jnp.zeros_like(shares[0])
        for c in range(GROUP):
            share = jnp.where((sc[1] ^ k) == c, shares[c], share)
        v[2 * few :, :] = jnp.zeros((v.shape[0] - 2 * few, width), low)
        v[2 * few : 2 * few + 1, :step] = share


def place_kernel(heads, sc, v0, v1, v2, v3, grad_up, grad_qkv, grad_norms, natural, whole):
    width = v0.shape[1]
    few = natural.shape[1]
    per = width // LANES
    mine_wide = heads * HEAD_DIM
    shape = (WIDE, WIDE)
    source, out = lax.broadcasted_iota(jnp.int32, shape, 0), lane_index(shape)
    v = source & (LANES - 1)
    column = jnp.where(v < heads * HALF, (v // HALF) * HEAD_DIM + (source // LANES) * HALF + (v & (HALF - 1)), -1)
    back = jnp.where(out == column, 1.0, 0.0).astype(low)
    norm = jnp.zeros((1, mine_wide), full)
    for k, piece in enumerate((v0, v1, v2, v3)):
        spread_rows(grad_up, piece[0:few, :].astype(full), (sc[1] ^ k) * per, GROUP * per)
        for part in range(3):
            values = piece[few : 2 * few, part * WIDE : (part + 1) * WIDE]
            natural[sc[1] ^ k, :, part * WIDE : (part + 1) * WIDE] = values.astype(full) if part == 2 else mm(values, back)
        norm = norm + piece[2 * few : 2 * few + 1, :mine_wide].astype(full)
    grad_norms[...] = norm
    for part in range(3):
        for c in range(GROUP):
            to = (part * GROUP + c) * mine_wide
            whole[:, to : to + mine_wide] = natural[c, :, part * WIDE : part * WIDE + mine_wide]
    spread_rows(grad_qkv, whole[...], 0, whole.shape[1] // LANES)


class Late:
    def __init__(self, source, held, sem):
        self.copy, self.held, self.shape, self.here = pltpu.make_async_copy(source, held, sem), held, held.shape, False
        self.copy.start()

    def __getitem__(self, index):
        if not self.here:
            self.copy.wait()
            self.here = True
        return self.held[index]


def run(kernel, shapes, scratch, operands, spaces):
    place = {"s": pltpu.SMEM, "v": pltpu.VMEM, "a": pl.ANY, "h": pltpu.HBM}
    total = len(operands) + len(shapes) + len(scratch)
    late = [i for i, space in enumerate(spaces) if space == "h"]
    held = [pltpu.VMEM(operands[i].shape, operands[i].dtype) for i in late]

    def body(*refs):
        given = list(refs[:total])
        for n, i in enumerate(late):
            given[i] = Late(given[i], refs[total + n], refs[-1].at[n])
        kernel(*given)
        for i in late:
            given[i][...]

    return pl.pallas_call(
        body,
        out_shape=[jax.ShapeDtypeStruct(shape, kind) for shape, kind in shapes],
        in_specs=[pl.BlockSpec(memory_space=place[space]) for space in spaces],
        out_specs=[pl.BlockSpec(memory_space=pltpu.VMEM) for _ in shapes],
        scratch_shapes=[*scratch, *held, pltpu.SemaphoreType.DMA((len(held),))] if held else scratch,
        compiler_params=pltpu.CompilerParams(vmem_limit_bytes=52 * 2**20),
        cost_estimate=pl.CostEstimate(flops=1, bytes_accessed=1, transcendentals=0),
    )(*operands)


def exchange(value):
    values = value if isinstance(value, (list, tuple)) else [value] * GROUP
    return [values[0]] + [
        lax.ppermute(values[k], "ctx", [(i, i ^ k) for i in range(GROUP)]) for k in range(1, GROUP)
    ]


def towards(value, k):
    return lax.ppermute(value, "ctx", [(i, i ^ k) for i in range(GROUP)])


def along(value, k):
    count = lax.axis_size("dp")
    return lax.ppermute(value, "dp", [(i, i ^ k) for i in range(count)])


def swap(value):
    return lax.ppermute(value, "section", [(0, 1), (1, 0)])


def together(*values):
    return lax.optimization_barrier(values)


def on_device(tokens, cotangent, seq_bound, ln1_gain, ln1_shift, w_qkv, w_out, ln2_gain, ln2_shift, w_up, w_down):
    section = lax.axis_index("section")
    me = lax.axis_index("ctx")
    shards = lax.axis_size("dp")
    z = lax.axis_index("dp")
    rows, width = tokens.shape[1:]
    feed_width = w_up.shape[2]
    chunk = feed_width // GROUP
    heads = width // HEAD_DIM // GROUP
    mine_wide = heads * HEAD_DIM
    length = GROUP * rows
    few = width // (GROUP * shards)
    bound = lax.dynamic_index_in_dim(seq_bound[0], section, 0, keepdims=False)
    sc = jnp.stack([section, me, bound, z]).astype(jnp.int32)

    dma = pltpu.SemaphoreType.DMA
    vm = pltpu.VMEM
    piece = ((rows, width), low)
    wide_piece = ((rows, width), full)
    pair = ((2, width), full)

    x = lax.dynamic_index_in_dim(tokens, section, 0, keepdims=False)
    gathered = exchange(x)
    wq_own, wo_own, up_own, dn_own = w_qkv[0], w_out[0], w_up[0], w_down[0]
    wq_oth, wo_oth = swap(wq_own), swap(wo_own)
    norms_own = jnp.concatenate([ln1_gain, ln1_shift, ln2_gain, ln2_shift], axis=0)
    wo_oth, later = together(wo_oth, norms_own)
    norms_oth = swap(later)
    wq_oth, norms_oth, later = together(wq_oth, norms_oth, up_own)
    up_oth = swap(later)
    *gathered, later = together(*gathered, dn_own)
    dn_oth = swap(later)

    def attend(layer, gathered, *tables):
        table = ((length, LANES), full)
        given = len(tables)
        return run(
            functools.partial(attend_kernel, layer, heads),
            [table] * (2 - given) + [((length, width), low), ((length, 3 * WIDE), low), ((heads, length, length), low)] + [((rows, mine_wide), low)] * GROUP,
            [vm((3, width, WIDE), low), vm((width, 3 * WIDE), low), vm((length, 3 * WIDE), full), vm((heads, length, length), full), dma((3,))],
            (sc, *gathered, norms_own, norms_oth, *tables, wq_own, wq_oth),
            "svvvvvv" + "v" * given + "aa",
        )

    def attend_back(layer, grads, qkv, probs):
        return run(
            functools.partial(attend_back_kernel, layer, heads),
            [((length, 3 * WIDE), low)] + [piece] * GROUP,
            [
                vm((mine_wide, width), low), vm((3, width, WIDE), low), vm((width, 3 * WIDE), low), vm((length, WIDE), low),
                vm((heads * length, length), low), vm((heads * length, WIDE), low), vm((heads * length, WIDE), low),
                vm((length, width), low), vm((heads, length, length), full), dma((4,)),
            ],
            (sc, *grads, qkv, probs, cos, sin, wo_own, wo_oth, wq_own, wq_oth),
            "svvvvvvvvaaaa",
        )

    half = width // 2
    small = shards == GROUP
    square, attend_size = (width,), (width,) if small else (width, mine_wide)

    def pair_grads(*products):
        out = ((width, half), low)
        operands = [piece for lefts, rights, _, _ in products for piece in (*lefts, *rights)]
        places = [(at_left, at_right) for _, _, at_left, at_right in products]
        return run(
            functools.partial(pair_grads_kernel, places),
            [out] * (2 * len(products)),
            [vm((len(products), length, width), low), vm((len(products), length, width), low), dma((2 * len(products), 2 * GROUP))],
            (sc, *operands), "s" + "a" * len(operands),
        )

    def attend_grads(n1, gmixed, fwd, ga, at_att):
        return run(
            functools.partial(attend_grads_kernel, at_att, small),
            [((sum(attend_size), half), low)] * 2,
            [vm((length, width), low), vm((length, 3 * WIDE), low), vm((length, WIDE), low), vm((length, width), low), dma((4, 2 * GROUP))],
            (sc, n1, gmixed, *fwd, *ga), "s" + "a" * (2 + 2 * GROUP),
        )


    def blocks_of(sizes, mine, theirs, *norms):
        total = sum(sum(size) for size in sizes) // shards + (16 if norms else 0)
        if small:
            (blocks,) = run(
                functools.partial(add_kernel, sizes), [((shards, total, half), low)], [], (*mine, *theirs, *norms),
                "v" * (2 * len(mine) + len(norms)),
            )
        else:
            parts = []
            for x, y, size in zip(mine, theirs, sizes):
                value = (x.astype(full) + y.astype(full)).astype(low)
                base = 0
                for part in size:
                    parts.append(value[base : base + part].reshape(shards, part // shards, half))
                    base += part
            blocks = jnp.concatenate(parts, axis=1)
        return blocks

    def over_dp(blocks):
        return lax.psum_scatter(blocks, "dp", scatter_dimension=0, tiled=False)

    def split(axis, sizes, mine, theirs):
        part = ((2, sum(sizes) // GROUP, half), low)
        return run(functools.partial(split_kernel, axis, sizes), [part, part], [], (sc, mine, theirs), "svv")

    def halve(axis, stay, got):
        part = stay.shape[1:]
        return run(functools.partial(halve_kernel, axis), [(part, full), (part, low)], [], (sc, stay, got), "svv")

    def level(token, *values):
        token, *values = together(token, *values)
        return together(swap(token), *values)[1:]

    feed_scratch = [vm((GROUP, width, chunk), low), vm((GROUP, chunk, width), low)]
    out_scratch = vm((GROUP, mine_wide, width), low)
    split_scratch = [vm((GROUP, rows, chunk), low), vm((GROUP, rows, WIDE), low)]
    owner, other_way = (3, along) if small else (1, towards)

    cos, sin, n1_0, qkv_0, probs_0, *att = attend(0, gathered)
    att = exchange(att)
    weights = (wo_own, wo_oth, up_own, up_oth, dn_own, dn_oth)
    cot = lax.dynamic_index_in_dim(cotangent, section, 0, keepdims=False)
    *att, cot = together(*att, cot)
    y0, hidden_0, slope_0, *fwd_0 = run(
        functools.partial(feed_kernel, 0, shards),
        [piece, wide_piece, ((rows, feed_width), low)] + [((rows, 2 * width + WIDE), low)] * GROUP,
        [out_scratch, *feed_scratch, *split_scratch, vm((16, width), low), dma, dma((3 * GROUP,))],
        (sc, x, *att, norms_own, norms_oth, *weights),
        "svvvvvvvaaaaaa",
    )
    gathered_1 = exchange(y0)
    cots = [cot, other_way(cot, 1), None, other_way(cot, 3)]
    *gathered_1, fwd_0[1], fwd_0[2], cots[1], cots[3] = together(*gathered_1, fwd_0[1], fwd_0[2], cots[1], cots[3])
    fwd_0[1], fwd_0[2] = towards(fwd_0[1], 1), towards(fwd_0[2], 2)
    n1_1, qkv_1, probs_1, *att = attend(1, gathered_1, cos, sin)
    att = exchange(att)
    *att, fwd_0[1], fwd_0[2], fwd_0[3] = together(*att, *fwd_0[1:])
    fwd_0[3] = towards(fwd_0[3], 3)
    y1, gh_1, dn2_1, *rest = run(
        functools.partial(feed_turn_kernel, 1, shards, owner),
        [piece, wide_piece, pair] + [((rows, width + WIDE), low)] * GROUP + [((rows, 2 * width), low)] * GROUP + [piece] * GROUP,
        [
            out_scratch, *feed_scratch, *split_scratch, vm((rows, width), full), vm((rows, feed_width), low),
            vm((GROUP, rows, chunk), low), dma((3 * GROUP,)),
        ],
        (sc, y0, *att, norms_own, norms_oth, cot, *weights),
        "svvvvvvvvaaaaaa",
    )
    ga, up_1, down_1 = rest[:GROUP], rest[GROUP : 2 * GROUP], rest[2 * GROUP :]
    *ga, fwd_0[3] = together(*ga, fwd_0[3])
    ga_1 = exchange(ga)
    *ga_1, cots[2], down_1[1], down_1[3], up_1[1], up_1[2] = together(*ga_1, cot, down_1[1], down_1[3], up_1[1], up_1[2])
    cots[2] = other_way(cots[2], 2)
    up_1[1], up_1[2] = towards(up_1[1], 1), towards(up_1[2], 2)
    gmixed_1, *back = attend_back(1, ga_1, qkv_1, probs_1)
    *back, up_1[1], up_1[2], up_1[3], down_1[1], down_1[3], cots[2] = together(*back, *up_1[1:], down_1[1], down_1[3], cots[2])
    back = exchange(back)
    down_1[1], down_1[3] = other_way(down_1[1], 1), other_way(down_1[3], 3)
    att_1, att_1_go = attend_grads(n1_1, gmixed_1, ga_1, ga_1, width)
    *back, down_1[1], down_1[2], down_1[3], up_1[3], att_1, att_1_go = together(*back, *down_1[1:], up_1[3], att_1, att_1_go)
    up_1[3] = towards(up_1[3], 3)
    att_1_got = swap(att_1_go)
    gx_1, dn1_1, ga, gh_0, dn2_0, *bwd_0 = run(
        functools.partial(turn_kernel, 0),
        [wide_piece, pair, piece, wide_piece, pair] + [((rows, 2 * width), low)] * GROUP,
        [*feed_scratch, vm((GROUP, rows, chunk), low), dma((2 * GROUP,))],
        (sc, *back, gh_1, y0, hidden_0, slope_0, norms_own, norms_oth, up_own, up_oth, dn_own, dn_oth),
        "svvvvvvvvvvaaaa",
    )
    ga, att_1_got, up_1[3], down_1[2] = together(ga, att_1_got, up_1[3], down_1[2])
    ga_0 = exchange(ga)
    down_1[2] = other_way(down_1[2], 2)
    up_1_stay, up_1_go = pair_grads((up_1, up_1, 0, width))
    up_1_got = swap(up_1_go)
    grads_1 = blocks_of([attend_size, square], [att_1, up_1_stay], [att_1_got, up_1_got])
    *ga_0, grads_1, bwd_0[1], bwd_0[2], down_1[2] = together(*ga_0, grads_1, bwd_0[1], bwd_0[2], down_1[2])
    sum_1 = over_dp(grads_1)
    bwd_0[1], bwd_0[2] = towards(bwd_0[1], 1), towards(bwd_0[2], 2)
    gmixed_0, *back = attend_back(0, ga_0, qkv_0, probs_0)
    gmixed_0, *back, bwd_0[1], bwd_0[2], bwd_0[3] = together(gmixed_0, *back, *bwd_0[1:])
    bwd_0[3] = towards(bwd_0[3], 3)
    att_0, att_0_go = attend_grads(n1_0, gmixed_0, fwd_0, ga_0, 2 * width)
    att_0_got = swap(att_0_go)
    *back, att_0, att_0_got = together(*back, att_0, att_0_got)
    back = exchange(back)
    sum_0 = over_dp(blocks_of([attend_size], [att_0], [att_0_got]))
    up_0, up_0_go, down_0, down_0_go = pair_grads((fwd_0, bwd_0, 0, 0), (fwd_0, bwd_0, width, width))
    *back, up_0, up_0_go, down_0, down_0_go = together(*back, up_0, up_0_go, down_0, down_0_go)
    up_0_got, down_0_got = swap(up_0_go), swap(down_0_go)
    kept, sent, sums, sums_sent = run(
        last_kernel, [wide_piece, wide_piece, ((4, width), full), ((4, width), full)],
        [vm((rows, width), full), vm((2, width), full)],
        (sc, *back, gh_0, x, norms_own, norms_oth, gx_1, dn1_1, dn2_1, dn2_0), "svvvvvvvvvvvv",
    )
    sums, sums_sent, up_0_got, down_0_got, sum_1 = together(sums, sums_sent, up_0_got, down_0_got, sum_1)
    sums_got = swap(sums_sent)
    sums = sums + sums_got
    if small:
        grads_0 = blocks_of([square, square], [up_0, down_0], [up_0_got, down_0_got], sums)
        grads_0, down_1[0] = together(grads_0, down_1[0])
        sum_feed_0 = over_dp(grads_0)
    down_1_stay, down_1_go = pair_grads((down_1, cots, 0, 0))
    down_1_got = swap(down_1_go)
    if small:
        down_1_stay, down_1_go = split(1, square, down_1_stay, down_1_got)
        down_1_stay, down_1_go = halve(1, down_1_stay, towards(down_1_go, 1))
        tall = width // shards
        lanes = width // LANES
        everything = ((3 * tall, half), low)
        mine, other = run(
            pack_kernel, [everything, everything], [],
            (sc, sum_0, sum_1, down_1_stay, towards(down_1_go, 2)), "shhvv",
        )
        grad_down, grad_out, *pieces = run(
            finish_kernel,
            [((tall * lanes, LANES), full), ((few * lanes, LANES), full)] + [((2 * few + 16, width), low)] * GROUP,
            [vm((3 * tall, width), full), vm((few, width), full)],
            (sc, mine, swap(other), sum_feed_0, lax.ppermute(sum_feed_0, "section", [(1, 0)])), "svvvv",
        )
        grad_up, grad_qkv, grad_norms = run(
            functools.partial(place_kernel, heads),
            [((few * GROUP * lanes, LANES), full), ((few * 3 * lanes, LANES), full), ((1, mine_wide), full)],
            [vm((GROUP, few, 3 * WIDE), full), vm((few, 3 * width), full)],
            (sc, *exchange(pieces)), "s" + "v" * GROUP,
        )
    else:
        sum_feed_0 = over_dp(blocks_of([square, square], [up_0, down_0], [up_0_got, down_0_got]))
        sum_down_1 = over_dp(blocks_of([square], [down_1_stay], [down_1_got]))
        grad_up, grad_down, grad_out, grad_qkv = many_shards(
            me, section, heads, few, jnp.concatenate([sum_0, sum_feed_0]), jnp.concatenate([sum_1, sum_down_1])
        )
        grad_norms = lax.psum_scatter(sums.reshape(shards * GROUP, -1), ("dp", "ctx"), scatter_dimension=0, tiled=True)

    def by_section(own, got):
        return jnp.where(section == 0, jnp.stack([own, got]), jnp.stack([got, own]))[None]

    y_own, y_sent = jnp.where(section == 0, y0, y1), jnp.where(section == 0, y1, y0)
    return (
        by_section(y_own, swap(y_sent)),
        by_section(kept, swap(sent)),
        grad_qkv.reshape(1, -1),
        grad_out.reshape(1, -1),
        grad_up.reshape(1, -1),
        grad_down.reshape(1, -1),
        grad_norms.reshape(1, -1),
    )


def many_shards(me, section, heads, few, first, second):
    own, other = jnp.where(section == 0, first, second), jnp.where(section == 0, second, first)
    got = swap(other)
    whole = jnp.where(section == 0, jnp.concatenate([own, got], axis=1), jnp.concatenate([got, own], axis=1))
    width = whole.shape[1]
    chunk, tall = width, GROUP * few
    t_qkv, t_out, t_up, t_down = whole[:tall], whole[tall : tall + few], whole[tall + few : 2 * tall + few], whole[2 * tall + few :]
    slim = jnp.concatenate([t_up, t_qkv], axis=1)
    slim = slim.reshape(GROUP, slim.shape[0] // GROUP, slim.shape[1])
    gets = jnp.stack(exchange([lax.dynamic_index_in_dim(slim, me ^ k, 0, keepdims=False) for k in range(GROUP)]))
    gets = jnp.stack([lax.dynamic_index_in_dim(gets, me ^ k, 0, keepdims=False) for k in range(GROUP)]).astype(full)
    few = gets.shape[1]
    grad_up = jnp.transpose(gets[:, :, :chunk], (1, 0, 2))
    cols = gets[:, :, chunk:].reshape(GROUP, few, 3, WIDE)
    turned = cols[:, :, :2].reshape(GROUP, few, 2, 2, LANES)[..., : heads * HALF]
    turned = turned.reshape(GROUP, few, 2, 2, heads, HALF).transpose(1, 2, 0, 4, 3, 5).reshape(few, 2 * width)
    plain = cols[:, :, 2, : heads * HEAD_DIM].transpose(1, 0, 2).reshape(few, width)
    return grad_up, t_down.astype(full), t_out.astype(full), jnp.concatenate([turned, plain], axis=1)


def solution(mesh):
    in_specs = (
        P(None, ("dp", "ctx"), None),
        P(None, ("dp", "ctx"), None),
        P("dp", None),
        P("section", None),
        P("section", None),
        P("section", None, None),
        P("section", None, None),
        P("section", None),
        P("section", None),
        P("section", None, None),
        P("section", None, None),
    )
    out_specs = (
        P("section", None, ("dp", "ctx"), None),
        P("section", None, ("dp", "ctx"), None),
        P("section", ("dp", "ctx")),
        P("section", ("dp", "ctx")),
        P("section", ("dp", "ctx")),
        P("section", ("dp", "ctx")),
        P("section", ("dp", "ctx")),
    )
    return jax.shard_map(
        on_device, mesh=mesh, in_specs=in_specs, out_specs=out_specs, check_vma=False
    )
```

```python
import functools
import math

import jax
import jax.numpy as jnp
from jax import lax
from jax.experimental import pallas as pl
from jax.experimental.pallas import tpu as pltpu
from jax.sharding import PartitionSpec as P

HEAD_DIM = 64
HALF = HEAD_DIM // 2
GROUP = 4
LANES = 128
WIDE = 2 * LANES

epsilon = 1e-05
rotary_base = 10000.0
masked_score = -1e30
low = jnp.bfloat16
full = jnp.float32

NT = (((1,), (1,)), ((), ()))
TN = (((0,), (0,)), ((), ()))


def mm(a, b):
    return jnp.dot(a, b, preferred_element_type=full)


def mm_nt(a, b):
    return lax.dot_general(a, b, NT, preferred_element_type=full)


def mm_tn(a, b):
    return lax.dot_general(a, b, TN, preferred_element_type=full)


def layer_norms(layer, sc, own, other):
    return jnp.where(sc[0] == layer, own[...], other[...])


def norm_stats(values):
    mean = jnp.mean(values, axis=-1, keepdims=True)
    centred = values - mean
    spread = jnp.mean(centred * centred, axis=-1, keepdims=True)
    scale = lax.rsqrt(spread + epsilon)
    return centred * scale, scale


def norm_backward(values, gain, grad):
    hat, scale = norm_stats(values)
    grad_gain = jnp.sum(grad * hat, axis=0, keepdims=True)
    grad_shift = jnp.sum(grad, axis=0, keepdims=True)
    inner = grad * gain
    first = jnp.mean(inner, axis=-1, keepdims=True)
    second = jnp.mean(inner * hat, axis=-1, keepdims=True)
    return scale * (inner - first - hat * second), grad_gain, grad_shift


def gelu_both(u):
    bell = jnp.exp(-0.5 * u * u)
    z = jnp.abs(u) * (0.5**0.5)
    t = 1.0 / (1.0 + 0.3275911 * z)
    poly = t * (
        0.254829592 + t * (-0.284496736 + t * (1.421413741 + t * (-1.453152027 + t * 1.061405429)))
    )
    tail = 0.5 * poly * bell
    cdf = jnp.where(u >= 0, 1.0 - tail, tail)
    return u * cdf, cdf + u * bell * (1.0 / math.sqrt(2.0 * math.pi))


class Fetch:
    def __init__(self, own, other, use_own, place, target, sem):
        self.parts = (own, other, use_own, place, target, sem)

    def start(self):
        own, other, use_own, place, target, sem = self.parts

        @pl.when(use_own)
        def _():
            pltpu.make_async_copy(own.at[place], target, sem).start()

        @pl.when(jnp.logical_not(use_own))
        def _():
            pltpu.make_async_copy(other.at[place], target, sem).start()

    def wait(self):
        own, other, use_own, place, target, sem = self.parts
        pltpu.make_async_copy(own.at[place], target, sem).wait()


def lane_index(shape):
    return lax.broadcasted_iota(jnp.int32, shape, 1)


def half_mask(head):
    return ((lane_index((1, WIDE)) & (LANES - 1)) // HALF) == head


def value_mask(head):
    return (lane_index((1, WIDE)) // HEAD_DIM) == head


def keep(values, mask):
    return jnp.where(mask, values, jnp.zeros_like(values))


class ProjectionWeights:
    def __init__(self, me, heads, mine, own, other, windows, target, sem):
        total = own.shape[0]
        at = me * (heads * HEAD_DIM)
        self.shift = lax.rem(at, LANES)
        start = at - self.shift
        self.windows, self.target, self.heads = windows, target, heads
        self.parts = []
        for part in range(3):
            span = pl.ds(pl.multiple_of(part * total + start, LANES), WIDE)
            self.parts.append(Fetch(own, other, mine, (slice(None), span), windows.at[part], sem.at[part]))

    def start(self):
        for part in self.parts:
            part.start()

    def wait(self):
        shape = (WIDE, WIDE)
        source, u = lax.broadcasted_iota(jnp.int32, shape, 0), lane_index(shape)
        v = u & (LANES - 1)
        turned = jnp.where(v < self.heads * HALF, (v // HALF) * HEAD_DIM + (u // LANES) * HALF + (v & (HALF - 1)) + self.shift, -1)
        plain = jnp.where(u < self.heads * HEAD_DIM, u + self.shift, -1)
        turned = jnp.where(source == turned, 1.0, 0.0).astype(low)
        plain = jnp.where(source == plain, 1.0, 0.0).astype(low)
        for part in range(3):
            self.parts[part].wait()
            chosen = mm(self.windows[part], plain if part == 2 else turned)
            self.target[:, part * WIDE : (part + 1) * WIDE] = chosen.astype(low)


def rotary_tables(me, bound, rows, cos, sin):
    for k in range(GROUP):
        here = slice(k * rows, (k + 1) * rows)
        spot = (me ^ k) * rows + lax.broadcasted_iota(jnp.int32, (rows, LANES), 0)
        relative = (spot - jnp.where(spot >= bound, bound, 0)).astype(full)
        steps = (lane_index((rows, LANES)) & (HALF - 1)).astype(full)
        angles = relative * jnp.exp(-math.log(rotary_base) * 2.0 * steps / HEAD_DIM)
        cos[here, :] = jnp.cos(angles)
        sin[here, :] = jnp.sin(angles)


def attend_kernel(layer, heads, sc, bounds, x0, x1, x2, x3, norms_own, norms_oth, *refs):
    bound = jnp.where(sc[0] == 0, bounds[0, 0], bounds[0, 1])
    if layer == 0:
        w_own, w_oth, cos, sin, n1, qkv, probs, a0, a1, a2, a3, win, w, mixed, scores, sem = refs
    else:
        cos, sin, w_own, w_oth, n1, qkv, probs, a0, a1, a2, a3, win, w, mixed, scores, sem = refs
    rows = x0.shape[0]
    weights = ProjectionWeights(sc[1], heads, sc[0] == layer, w_own, w_oth, win, w, sem)
    weights.start()
    if layer == 0:
        rotary_tables(sc[1], bound, rows, cos, sin)
    norms = layer_norms(layer, sc, norms_own, norms_oth)
    gain, shift = norms[0:1, :], norms[1:2, :]
    for k, x in enumerate((x0, x1, x2, x3)):
        hat, _ = norm_stats(x[...].astype(full))
        n1[k * rows : (k + 1) * rows, :] = (hat * gain + shift).astype(low)
    weights.wait()
    mixed[...] = mm(n1[...], w[...])
    for k in range(GROUP):
        here = slice(k * rows, (k + 1) * rows)
        c, s = cos[here, :], sin[here, :]
        for part in range(2):
            base = part * WIDE
            v1, v2 = mixed[here, base : base + LANES], mixed[here, base + LANES : base + WIDE]
            qkv[here, base : base + LANES] = (v1 * c - v2 * s).astype(low)
            qkv[here, base + LANES : base + WIDE] = (v2 * c + v1 * s).astype(low)
        qkv[here, 2 * WIDE :] = mixed[here, 2 * WIDE :].astype(low)
    me = sc[1]
    length = GROUP * rows
    spot = lax.broadcasted_iota(jnp.int32, (1, length), 1)
    place = jnp.zeros((1, length), jnp.int32)
    for k in range(GROUP):
        place = jnp.where(spot // rows == k, (me ^ k) * rows + spot - k * rows, place)
    seq_col = (place >= bound).astype(jnp.int32)
    for h in range(heads):
        scores[h] = mm_nt(keep(qkv[:, 0:WIDE], half_mask(h)), qkv[:, WIDE : 2 * WIDE])
    for h in range(heads):
        for k in range(GROUP):
            here = slice(k * rows, (k + 1) * rows)
            own = (me ^ k) * rows + lax.broadcasted_iota(jnp.int32, (rows, 1), 0)
            same = (own >= bound).astype(jnp.int32) == seq_col
            score = jnp.where(same, scores[h, here, :] * (HEAD_DIM**-0.5), masked_score)
            top = jnp.max(score, axis=-1, keepdims=True)
            expo = jnp.exp(score - top)
            probs[h, here, :] = (expo * (1.0 / jnp.sum(expo, axis=-1, keepdims=True))).astype(low)
    total = mm(probs[0], keep(qkv[:, 2 * WIDE :], value_mask(0)))
    for h in range(1, heads):
        total = total + mm(probs[h], keep(qkv[:, 2 * WIDE :], value_mask(h)))
    for k, out in enumerate((a0, a1, a2, a3)):
        out[...] = total[k * rows : (k + 1) * rows, : heads * HEAD_DIM].astype(low)


def attend_back_kernel(layer, heads, sc, g0, g1, g2, g3, qkv, probs, cos, sin, wo_own, wo_oth, w_own, w_oth, gmixed, p0, p1, p2, p3, wo, win, w, go, gs, qm, gom, ga, gp, sem):
    rows = g0.shape[0]
    width = heads * HEAD_DIM
    me = sc[1]
    mine = sc[0] == layer
    span = pl.ds(pl.multiple_of(me * width, HEAD_DIM), width)
    fetch_o = Fetch(wo_own, wo_oth, mine, (span, slice(None)), wo, sem.at[3])
    fetch_w = ProjectionWeights(me, heads, mine, w_own, w_oth, win, w, sem)
    fetch_o.start()
    fetch_w.start()
    length = GROUP * rows
    for k, g in enumerate((g0, g1, g2, g3)):
        ga[k * rows : (k + 1) * rows, :] = g[:, : wo.shape[1]]
    go[:, LANES:] = jnp.zeros((length, WIDE - LANES), low)
    fetch_o.wait()
    go[:, :width] = mm_nt(ga[...], wo[...]).astype(low)
    for h in range(heads):
        there = slice(h * length, (h + 1) * length)
        gom[there, :] = keep(go[...], value_mask(h))
        qm[there, :] = keep(qkv[:, 0:WIDE], half_mask(h))
        gp[h] = mm_nt(gom[there, :], qkv[:, 2 * WIDE :])
    for h in range(heads):
        for k in range(GROUP):
            here = slice(k * rows, (k + 1) * rows)
            p, g = probs[h, here, :].astype(full), gp[h, here, :]
            inner = jnp.sum(p * g, axis=-1, keepdims=True)
            gs[h * length + k * rows : h * length + (k + 1) * rows, :] = (p * (g - inner)).astype(low)
    gq = mm(gs[0:length, :], keep(qkv[:, WIDE : 2 * WIDE], half_mask(0)))
    gv = mm_tn(probs[0], gom[0:length, :])
    for h in range(1, heads):
        there = slice(h * length, (h + 1) * length)
        gq = gq + mm(gs[there, :], keep(qkv[:, WIDE : 2 * WIDE], half_mask(h)))
        gv = gv + mm_tn(probs[h], gom[there, :])
    gk = mm_tn(gs[...], qm[...])
    for base, value in ((0, gq), (WIDE, gk)):
        value = value * (HEAD_DIM**-0.5)
        v1, v2 = value[:, :LANES], value[:, LANES:]
        gmixed[:, base : base + LANES] = (v1 * cos[...] + v2 * sin[...]).astype(low)
        gmixed[:, base + LANES : base + WIDE] = (v2 * cos[...] - v1 * sin[...]).astype(low)
    gmixed[:, 2 * WIDE :] = gv.astype(low)
    fetch_w.wait()
    back = mm_nt(gmixed[...], w[...]).astype(low)
    for k, out in enumerate((p0, p1, p2, p3)):
        out[...] = back[k * rows : (k + 1) * rows, :]


class FeedWeights:
    def __init__(self, mine, up_own, up_oth, dn_own, dn_oth, wu, wd, sem, first):
        width = wu.shape[1]
        self.wu, self.wd = wu, wd
        self.up, self.down = [], []
        for j in range(GROUP):
            cut = slice(j * width, (j + 1) * width)
            self.up.append(Fetch(up_own, up_oth, mine, (slice(None), cut), wu.at[j], sem.at[first + j]))
            self.down.append(Fetch(dn_own, dn_oth, mine, (cut, slice(None)), wd.at[j], sem.at[first + GROUP + j]))


def feed_forward(sc, x, atts, norms, fetch_o, wo, feed, shards, y, hidden, slope, owner, parts, cols):
    rows, width = x.shape
    heads_wide = atts[0].shape[1]
    me = sc[1]
    for k in range(GROUP):
        fetch_o[k].wait()
    state = x[...].astype(full)
    for k in range(GROUP):
        state = state + mm(atts[k][...], wo[k])
        cols[me ^ k, :, :heads_wide] = atts[k][...]
    hidden[...] = state
    hat, _ = norm_stats(state)
    n2 = (hat * norms[2:3, :] + norms[3:4, :]).astype(low)
    step = width // (GROUP * shards)
    shares = []
    for target in range(GROUP):
        pieces = []
        for z in range(shards):
            at = (z * GROUP + target) * step
            pieces.append(cols[at // heads_wide, :, at % heads_wide : at % heads_wide + step])
        pieces.append(jnp.zeros((rows, WIDE - heads_wide), low))
        shares.append(jnp.concatenate(pieces, axis=1))
    for target in range(GROUP):
        cols[target] = shares[target]
    out = jnp.zeros((rows, width), full)
    chunk = feed.wu.shape[2]
    for j in range(GROUP):
        feed.up[j].wait()
        act, grad = gelu_both(mm(n2, feed.wu[j]))
        act = act.astype(low)
        slope[:, j * chunk : (j + 1) * chunk] = grad.astype(low)
        feed.down[j].wait()
        out = out + mm(act, feed.wd[j])
        if owner == 3:
            parts[j] = act
            continue
        span = chunk // shards
        for b in range(chunk // span):
            z, target = divmod(j * (chunk // span) + b, GROUP)
            parts[target, :, z * span : (z + 1) * span] = act[:, b * span : (b + 1) * span]
    y[...] = (hidden[...] + out).astype(low)
    return n2


def feed_back(gf, grad_out, norms, feed, hidden, slope, gas, gh, dnorm, gu, waited):
    rows, width = gf.shape
    chunk = feed.wu.shape[2]
    grad = jnp.zeros((rows, width), full)
    for j in range(GROUP):
        if not waited:
            feed.down[j].wait()
        got = mm_nt(gf, feed.wd[j]) * slope[:, j * chunk : (j + 1) * chunk].astype(full)
        got = got.astype(low)
        gu[j] = got
        if not waited:
            feed.up[j].wait()
        grad = grad + mm_nt(got, feed.wu[j])
    back, d_gain, d_shift = norm_backward(hidden[...], norms[2:3, :], grad)
    total = grad_out + back
    gh[...] = total
    for ga in gas:
        ga[:, 0:width] = total.astype(low)
    dnorm[0:1, :] = d_gain
    dnorm[1:2, :] = d_shift


def start_out(sc, mine, wo_own, wo_oth, wo, sem):
    width = wo.shape[1]
    out = []
    for k in range(GROUP):
        span = pl.ds(pl.multiple_of((sc[1] ^ k) * width, HEAD_DIM), width)
        out.append(Fetch(wo_own, wo_oth, mine, (span, slice(None)), wo.at[k], sem.at[k]))
    return out


def touch(x, spare, sem):
    copy = pltpu.make_async_copy(x.at[0 : spare.shape[0], :], spare, sem)
    copy.start()
    copy.wait()


def feed_kernel(layer, shards, sc, x, a0, a1, a2, a3, norms_own, norms_oth, wo_own, wo_oth, up_own, up_oth, dn_own, dn_oth, y, hidden, slope, m0, m1, m2, m3, wo, wu, wd, parts, cols, spare, spare_sem, sem):
    mine = sc[0] == layer
    norms = layer_norms(layer, sc, norms_own, norms_oth)
    fetch_o = start_out(sc, mine, wo_own, wo_oth, wo, sem)
    feed = FeedWeights(mine, up_own, up_oth, dn_own, dn_oth, wu, wd, sem, GROUP)
    for f in fetch_o + [f for pair in zip(feed.up, feed.down) for f in pair]:
        f.start()
    touch(x, spare, spare_sem)
    n2 = feed_forward(sc, x, (a0, a1, a2, a3), norms, fetch_o, wo, feed, shards, y, hidden, slope, 1, parts, cols)
    width = x.shape[1]
    for k, m in enumerate((m0, m1, m2, m3)):
        m[:, 0:width] = n2
        m[:, width : 2 * width] = parts[sc[1] ^ k]
        m[:, 2 * width :] = cols[sc[1] ^ k]


def feed_turn_kernel(layer, shards, owner, sc, x, a0, a1, a2, a3, norms_own, norms_oth, cot, wo_own, wo_oth, up_own, up_oth, dn_own, dn_oth, y, gh, dnorm, g0, g1, g2, g3, m0, m1, m2, m3, d0, d1, d2, d3, wo, wu, wd, parts, cols, hidden, slope, gu, sem):
    mine = sc[0] == layer
    norms = layer_norms(layer, sc, norms_own, norms_oth)
    fetch_o = start_out(sc, mine, wo_own, wo_oth, wo, sem)
    feed = FeedWeights(mine, up_own, up_oth, dn_own, dn_oth, wu, wd, sem, GROUP)
    for f in fetch_o + [f for pair in zip(feed.up, feed.down) for f in pair]:
        f.start()
    gas = (g0, g1, g2, g3)
    n2 = feed_forward(sc, x, (a0, a1, a2, a3), norms, fetch_o, wo, feed, shards, y, hidden, slope, owner, parts, cols)
    gf = cot[...]
    feed_back(gf, gf.astype(full), norms, feed, hidden, slope, gas, gh, dnorm, gu, True)
    width = x.shape[1]
    for k, (g, m, d) in enumerate(((g0, m0, d0), (g1, m1, d1), (g2, m2, d2), (g3, m3, d3))):
        g[:, width:] = cols[sc[1] ^ k]
        m[:, 0:width] = n2
        m[:, width:] = gu[sc[1] ^ k]
        d[...] = parts[sc[owner] ^ k]


def turn_kernel(layer, sc, r0, r1, r2, r3, gh_in, x_in, hidden, slope, norms_own, norms_oth, up_own, up_oth, dn_own, dn_oth, gx, dnorm_in, ga, gh, dnorm, m0, m1, m2, m3, wu, wd, gu, sem):
    mine = sc[0] == layer
    feed = FeedWeights(mine, up_own, up_oth, dn_own, dn_oth, wu, wd, sem, 0)
    for f in [f for pair in zip(feed.down, feed.up) for f in pair]:
        f.start()
    norms_in = layer_norms(layer + 1, sc, norms_own, norms_oth)
    norms = layer_norms(layer, sc, norms_own, norms_oth)
    top = first_norm_back(r0, r1, r2, r3, gh_in, x_in, norms_in, gx, dnorm_in)
    gf = top.astype(low)
    feed_back(gf, gf.astype(full), norms, feed, hidden, slope, (ga,), gh, dnorm, gu, False)
    width = gf.shape[1]
    for k, m in enumerate((m0, m1, m2, m3)):
        m[:, 0:width] = gu[sc[1] ^ k]
        m[:, width:] = gf


def first_norm_back(r0, r1, r2, r3, gh_in, x_in, norms_in, gx, dnorm):
    grad = r0[...].astype(full) + r1[...].astype(full) + r2[...].astype(full) + r3[...].astype(full)
    back, d_gain, d_shift = norm_backward(x_in[...].astype(full), norms_in[0:1, :], grad)
    dnorm[0:1, :] = d_gain
    dnorm[1:2, :] = d_shift
    total = gh_in[...] + back
    gx[...] = total
    return total


def last_kernel(sc, r0, r1, r2, r3, gh_in, x_in, norms_own, norms_oth, above, d1_1, d2_1, d2_0, kept, sent, sums, sums_sent, gx, dnorm):
    first_norm_back(r0, r1, r2, r3, gh_in, x_in, layer_norms(0, sc, norms_own, norms_oth), gx, dnorm)
    first = sc[0] == 0
    kept[...] = jnp.where(first, gx[...], above[...])
    sent[...] = jnp.where(first, above[...], gx[...])
    for at, zero, one in ((0, dnorm, d1_1), (2, d2_0, d2_1)):
        sums[at : at + 2, :] = jnp.where(first, zero[...], one[...])
        sums_sent[at : at + 2, :] = jnp.where(first, one[...], zero[...])


def gather_rows(pieces, at, target, half, section, sems):
    rows, width = pieces[0].shape[0], target.shape[1]
    copies = []
    for k, piece in enumerate(pieces):
        here = pl.ds(k * rows, rows)
        if half is None:
            copies.append(pltpu.make_async_copy(piece.at[:, pl.ds(at, width)], target.at[here, :], sems.at[k]))
            continue
        for i, part in enumerate((section, 1 - section)):
            source = pl.ds(pl.multiple_of(at + part * half, LANES), half)
            copies.append(pltpu.make_async_copy(piece.at[:, source], target.at[here, pl.ds(i * half, half)], sems.at[2 * k + i]))
    for copy in copies:
        copy.start()
    return copies


def tall_product(left, right, stay, go, base, step):
    half = stay.shape[1]
    for i in range(left.shape[1] // step):
        cut, put = slice(i * step, (i + 1) * step), slice(base + i * step, base + (i + 1) * step)
        product = mm_tn(left[:, cut], right[...]).astype(low)
        stay[put, :] = product[:, :half]
        go[put, :] = product[:, half:]


def pair_grads_kernel(places, sc, *refs):
    count = len(places)
    outs, (a, b, sem) = refs[2 * GROUP * count : -3], refs[-3:]
    half = outs[0].shape[1]
    copies = []
    for i, (at_left, at_right) in enumerate(places):
        lefts, rights = refs[2 * GROUP * i :][:GROUP], refs[2 * GROUP * i + GROUP :][:GROUP]
        copies.append(
            gather_rows(lefts, at_left, a.at[i], None, None, sem.at[2 * i]) + gather_rows(rights, at_right, b.at[i], half, sc[0], sem.at[2 * i + 1])
        )
    for i in range(count):
        for copy in copies[i]:
            copy.wait()
        tall_product(a.at[i], b.at[i], outs[2 * i], outs[2 * i + 1], 0, WIDE)


def padding_place(lane):
    part, u = lane // WIDE, lane & (WIDE - 1)
    v = u & (LANES - 1)
    used, half = 3 * HALF, WIDE - HEAD_DIM
    turned = jnp.where(v >= used, part * HEAD_DIM + (u // LANES) * HALF + v - used, -1)
    plain = jnp.where(u >= half, 2 * HEAD_DIM + u - half, -1)
    return jnp.where(part < 2, turned, plain)


def attend_grads_kernel(at_att, fold, sc, n1, gmixed, m0, m1, m2, m3, g0, g1, g2, g3, stay, go, left, right, a, b, sem):
    width, half = b.shape[1], stay.shape[1]
    first = gather_rows((n1,), 0, left, None, None, sem.at[0]) + gather_rows((gmixed,), 0, right, half, sc[0], sem.at[1])
    second = gather_rows((m0, m1, m2, m3), at_att, a, None, None, sem.at[2])
    second += gather_rows((g0, g1, g2, g3), 0, b, None if fold else half, sc[0], sem.at[3])
    for copy in first:
        copy.wait()
    tall_product(left, right, stay, go, 0, WIDE)
    for copy in second:
        copy.wait()
    if not fold:
        product = mm_tn(a[...], b[...])[: stay.shape[0] - width, :].astype(low)
        stay[width:, :] = product[:, :half]
        go[width:, :] = product[:, half:]
        return
    mine_wide = 3 * HEAD_DIM
    product = mm_tn(a[...], b[...])[:mine_wide, :].astype(low)
    shape = (mine_wide, 2 * half)
    lane = lane_index(shape)
    lane = jnp.where(lane < half, lane + sc[0] * half, lane - sc[0] * half)
    spread = jnp.where(lax.broadcasted_iota(jnp.int32, shape, 0) == padding_place(lane), 1.0, 0.0).astype(low)
    few = mine_wide // GROUP
    for q in range(GROUP):
        put = mm(product[:, q * mine_wide : (q + 1) * mine_wide], spread).astype(low)
        for z in range(GROUP):
            at = slice(z * mine_wide + q * few, z * mine_wide + (q + 1) * few)
            stay[at, :] = stay[at, :] + put[z * few : (z + 1) * few, :half]
            go[at, :] = go[at, :] + put[z * few : (z + 1) * few, half:]


def add_kernel(sizes, *refs):
    count = len(sizes)
    mine, theirs = refs[:count], refs[count : 2 * count]
    norms = refs[2 * count] if len(refs) > 2 * count + 1 else None
    out = refs[-1]
    blocks, total, half = out.shape
    for b in range(blocks):
        at = 0
        for x, y, size in zip(mine, theirs, sizes):
            base = 0
            for part in size:
                step = part // blocks
                span = slice(base + b * step, base + (b + 1) * step)
                out[b, at : at + step, :] = (x[span, :].astype(full) + y[span, :].astype(full)).astype(low)
                at += step
                base += part
        if norms is not None:
            row = lax.broadcasted_iota(jnp.int32, (total - at, half), 0)
            lower, upper = norms[b : b + 1, :half], norms[b : b + 1, half:]
            out[b, at:, :] = jnp.where(row == 0, lower, jnp.where(row == 1, upper, 0.0)).astype(low)


def split_kernel(axis, sizes, sc, mine, theirs, stay, go):
    for out, flip in ((stay, 0), (go, 1)):
        for j in range(2):
            block = 2 * j + ((sc[axis] & 1) ^ flip)
            at, base = 0, 0
            for size in sizes:
                step = size // GROUP
                span = pl.ds(pl.multiple_of(base + block * step, 16), step)
                out[j, at : at + step, :] = (mine[span, :].astype(full) + theirs[span, :].astype(full)).astype(low)
                at += step
                base += size


def halve_kernel(axis, sc, held, got, stay, go):
    high = sc[axis] >> 1
    stay[...] = held[high].astype(full) + got[high].astype(full)
    go[...] = (held[1 - high].astype(full) + got[1 - high].astype(full)).astype(low)


def attend_pack_kernel(sc, att_0, grads_1, stay, go):
    first = sc[0] == 0
    zero, one = att_0[...], grads_1[0 : att_0.shape[0], :]
    stay[...] = jnp.where(first, zero, one)
    go[...] = jnp.where(first, one, zero)


def feed_pack_kernel(grads_1, down_1, down_1_got, out):
    split = down_1.shape[0]
    out[0:split, :] = grads_1[split:, :]
    out[split:, :] = (down_1[...] + down_1_got[...].astype(full)).astype(low)


def spread_rows(out, values, start, stride):
    for j in range(values.shape[1] // LANES):
        out[pl.ds(start + j, values.shape[0], stride=stride), :] = values[:, j * LANES : (j + 1) * LANES]


def join_halves(sc, whole, mine, theirs):
    half = mine.shape[1]
    whole[:, pl.ds(pl.multiple_of(sc[0] * half, LANES), half)] = mine[...].astype(full)
    whole[:, pl.ds(pl.multiple_of((1 - sc[0]) * half, LANES), half)] = theirs[...].astype(full)


def attend_finish_kernel(sc, mine, theirs, grad_out, v0, v1, v2, v3, whole, out):
    join_halves(sc, whole, mine, theirs)
    width = whole.shape[1]
    step = width // GROUP
    few = step // GROUP
    shape = (width, step)
    gather = jnp.where(padding_place(lax.broadcasted_iota(jnp.int32, shape, 0)) == lane_index(shape), 1.0, 0.0).astype(low)
    for q in range(GROUP):
        out[:, q * step : (q + 1) * step] = mm(whole[q * few : (q + 1) * few, :].astype(low), gather)
    spread_rows(grad_out, out[...], 0, width // LANES)
    for k, v in enumerate((v0, v1, v2, v3)):
        v[...] = whole[pl.ds(pl.multiple_of((sc[1] ^ k) * few, few), few), :].astype(low)


def qkv_place_kernel(heads, sc, v0, v1, v2, v3, grad_qkv, natural, whole):
    mine_wide = heads * HEAD_DIM
    shape = (WIDE, WIDE)
    source, out = lax.broadcasted_iota(jnp.int32, shape, 0), lane_index(shape)
    v = source & (LANES - 1)
    column = jnp.where(v < heads * HALF, (v // HALF) * HEAD_DIM + (source // LANES) * HALF + (v & (HALF - 1)), -1)
    back = jnp.where(out == column, 1.0, 0.0).astype(low)
    for k, piece in enumerate((v0, v1, v2, v3)):
        for part in range(3):
            values = piece[:, part * WIDE : (part + 1) * WIDE]
            natural[sc[1] ^ k, :, part * WIDE : (part + 1) * WIDE] = values.astype(full) if part == 2 else mm(values, back)
    for part in range(3):
        for c in range(GROUP):
            to = (part * GROUP + c) * mine_wide
            whole[:, to : to + mine_wide] = natural[c, :, part * WIDE : part * WIDE + mine_wide]
    spread_rows(grad_qkv, whole[...], 0, whole.shape[1] // LANES)


def feed_finish_kernel(sc, mine, theirs, feed_0, feed_0_got, grad_down, u0, u1, u2, u3, whole):
    join_halves(sc, whole, mine, theirs)
    half = mine.shape[1]
    width = 2 * half
    step = width // GROUP
    few = step // GROUP

    @pl.when(sc[0] == 0)
    def _():
        whole[:, 0:half] = feed_0[0 : 2 * step, :].astype(full)
        whole[:, half:] = feed_0_got[0 : 2 * step, :].astype(full)

    last = jnp.concatenate([feed_0[2 * step : 2 * step + 1, :], feed_0[2 * step + 1 : 2 * step + 2, :]], axis=1)
    shares = [last[:, c * step : (c + 1) * step] for c in range(GROUP)]
    for k, u in enumerate((u0, u1, u2, u3)):
        u[0:few, :] = whole[pl.ds(pl.multiple_of((sc[1] ^ k) * few, few), few), :].astype(low)
        share = jnp.zeros_like(shares[0])
        for c in range(GROUP):
            share = jnp.where((sc[1] ^ k) == c, shares[c], share)
        u[few:, :] = jnp.zeros((u.shape[0] - few, width), low)
        u[few : few + 1, :step] = share
    spread_rows(grad_down, whole[step:, :], 0, width // LANES)


def up_place_kernel(sc, u0, u1, u2, u3, grad_up, grad_norms):
    step = grad_norms.shape[1]
    few = step // GROUP
    per = u0.shape[1] // LANES
    norm = jnp.zeros((1, step), full)
    for k, u in enumerate((u0, u1, u2, u3)):
        spread_rows(grad_up, u[0:few, :].astype(full), (sc[1] ^ k) * per, GROUP * per)
        norm = norm + u[few : few + 1, :step].astype(full)
    grad_norms[...] = norm


class Late:
    def __init__(self, source, held, sem):
        self.copy, self.held, self.shape, self.here = pltpu.make_async_copy(source, held, sem), held, held.shape, False
        self.copy.start()

    def __getitem__(self, index):
        if not self.here:
            self.copy.wait()
            self.here = True
        return self.held[index]


def run(kernel, shapes, scratch, operands, spaces):
    place = {"s": pltpu.SMEM, "v": pltpu.VMEM, "a": pl.ANY, "h": pltpu.HBM}
    total = len(operands) + len(shapes) + len(scratch)
    late = [i for i, space in enumerate(spaces) if space == "h"]
    held = [pltpu.VMEM(operands[i].shape, operands[i].dtype) for i in late]

    def body(*refs):
        given = list(refs[:total])
        for n, i in enumerate(late):
            given[i] = Late(given[i], refs[total + n], refs[-1].at[n])
        kernel(*given)
        for i in late:
            given[i][...]

    return pl.pallas_call(
        body,
        out_shape=[jax.ShapeDtypeStruct(shape, kind) for shape, kind in shapes],
        in_specs=[pl.BlockSpec(memory_space=place[space]) for space in spaces],
        out_specs=[pl.BlockSpec(memory_space=pltpu.VMEM) for _ in shapes],
        scratch_shapes=[*scratch, *held, pltpu.SemaphoreType.DMA((len(held),))] if held else scratch,
        compiler_params=pltpu.CompilerParams(vmem_limit_bytes=52 * 2**20),
        cost_estimate=pl.CostEstimate(flops=1, bytes_accessed=1, transcendentals=0),
    )(*operands)


def exchange(value):
    values = value if isinstance(value, (list, tuple)) else [value] * GROUP
    return [values[0]] + [
        lax.ppermute(values[k], "ctx", [(i, i ^ k) for i in range(GROUP)]) for k in range(1, GROUP)
    ]


def towards(value, k):
    return lax.ppermute(value, "ctx", [(i, i ^ k) for i in range(GROUP)])


def along(value, k):
    count = lax.axis_size("dp")
    return lax.ppermute(value, "dp", [(i, i ^ k) for i in range(count)])


def swap(value):
    return lax.ppermute(value, "section", [(0, 1), (1, 0)])


def together(*values):
    return lax.optimization_barrier(values)


def on_device(tokens, cotangent, seq_bound, ln1_gain, ln1_shift, w_qkv, w_out, ln2_gain, ln2_shift, w_up, w_down):
    section = lax.axis_index("section")
    me = lax.axis_index("ctx")
    shards = lax.axis_size("dp")
    z = lax.axis_index("dp")
    rows, width = tokens.shape[1:]
    feed_width = w_up.shape[2]
    chunk = feed_width // GROUP
    heads = width // HEAD_DIM // GROUP
    mine_wide = heads * HEAD_DIM
    length = GROUP * rows
    few = width // (GROUP * shards)
    sc = jnp.stack([section, me, section, z]).astype(jnp.int32)

    dma = pltpu.SemaphoreType.DMA
    vm = pltpu.VMEM
    piece = ((rows, width), low)
    wide_piece = ((rows, width), full)
    pair = ((2, width), full)

    x = lax.dynamic_index_in_dim(tokens, section, 0, keepdims=False)
    gathered = exchange(x)
    wq_own, wo_own, up_own, dn_own = w_qkv[0], w_out[0], w_up[0], w_down[0]
    wq_oth, wo_oth = swap(wq_own), swap(wo_own)
    norms_own = jnp.concatenate([ln1_gain, ln1_shift, ln2_gain, ln2_shift], axis=0)
    wo_oth, later = together(wo_oth, norms_own)
    norms_oth = swap(later)
    wq_oth, norms_oth, later = together(wq_oth, norms_oth, up_own)
    up_oth = swap(later)
    *gathered, later = together(*gathered, dn_own)
    dn_oth = swap(later)

    def attend(layer, gathered, *tables):
        table = ((length, LANES), full)
        given = len(tables)
        return run(
            functools.partial(attend_kernel, layer, heads),
            [table] * (2 - given) + [((length, width), low), ((length, 3 * WIDE), low), ((heads, length, length), low)] + [((rows, mine_wide), low)] * GROUP,
            [vm((3, width, WIDE), low), vm((width, 3 * WIDE), low), vm((length, 3 * WIDE), full), vm((heads, length, length), full), dma((3,))],
            (sc, seq_bound, *gathered, norms_own, norms_oth, *tables, wq_own, wq_oth),
            "ssvvvvvv" + "v" * given + "aa",
        )

    def attend_back(layer, grads, qkv, probs):
        return run(
            functools.partial(attend_back_kernel, layer, heads),
            [((length, 3 * WIDE), low)] + [piece] * GROUP,
            [
                vm((mine_wide, width), low), vm((3, width, WIDE), low), vm((width, 3 * WIDE), low), vm((length, WIDE), low),
                vm((heads * length, length), low), vm((heads * length, WIDE), low), vm((heads * length, WIDE), low),
                vm((length, width), low), vm((heads, length, length), full), dma((4,)),
            ],
            (sc, *grads, qkv, probs, cos, sin, wo_own, wo_oth, wq_own, wq_oth),
            "svvvvvvvvaaaa",
        )

    half = width // 2
    small = shards == GROUP
    square, attend_size = (width,), (width,) if small else (width, mine_wide)

    def pair_grads(*products):
        out = ((width, half), low)
        operands = [piece for lefts, rights, _, _ in products for piece in (*lefts, *rights)]
        places = [(at_left, at_right) for _, _, at_left, at_right in products]
        return run(
            functools.partial(pair_grads_kernel, places),
            [out] * (2 * len(products)),
            [vm((len(products), length, width), low), vm((len(products), length, width), low), dma((2 * len(products), 2 * GROUP))],
            (sc, *operands), "s" + "a" * len(operands),
        )

    def attend_grads(n1, gmixed, fwd, ga, at_att):
        return run(
            functools.partial(attend_grads_kernel, at_att, small),
            [((sum(attend_size), half), low)] * 2,
            [vm((length, width), low), vm((length, 3 * WIDE), low), vm((length, WIDE), low), vm((length, width), low), dma((4, 2 * GROUP))],
            (sc, n1, gmixed, *fwd, *ga), "s" + "a" * (2 + 2 * GROUP),
        )


    def blocks_of(sizes, mine, theirs, *norms):
        total = sum(sum(size) for size in sizes) // shards + (16 if norms else 0)
        if small:
            (blocks,) = run(
                functools.partial(add_kernel, sizes), [((shards, total, half), low)], [], (*mine, *theirs, *norms),
                "v" * (2 * len(mine) + len(norms)),
            )
        else:
            parts = []
            for x, y, size in zip(mine, theirs, sizes):
                value = (x.astype(full) + y.astype(full)).astype(low)
                base = 0
                for part in size:
                    parts.append(value[base : base + part].reshape(shards, part // shards, half))
                    base += part
            blocks = jnp.concatenate(parts, axis=1)
        return blocks

    def over_dp(blocks):
        return lax.psum_scatter(blocks, "dp", scatter_dimension=0, tiled=False)

    def split(axis, sizes, mine, theirs):
        part = ((2, sum(sizes) // GROUP, half), low)
        return run(functools.partial(split_kernel, axis, sizes), [part, part], [], (sc, mine, theirs), "svv")

    def halve(axis, stay, got):
        part = stay.shape[1:]
        return run(functools.partial(halve_kernel, axis), [(part, full), (part, low)], [], (sc, stay, got), "svv")

    def level(token, *values):
        token, *values = together(token, *values)
        return together(swap(token), *values)[1:]

    feed_scratch = [vm((GROUP, width, chunk), low), vm((GROUP, chunk, width), low)]
    out_scratch = vm((GROUP, mine_wide, width), low)
    split_scratch = [vm((GROUP, rows, chunk), low), vm((GROUP, rows, WIDE), low)]
    owner, other_way = (3, along) if small else (1, towards)

    cos, sin, n1_0, qkv_0, probs_0, *att = attend(0, gathered)
    att = exchange(att)
    weights = (wo_own, wo_oth, up_own, up_oth, dn_own, dn_oth)
    cot = lax.dynamic_index_in_dim(cotangent, section, 0, keepdims=False)
    *att, cot = together(*att, cot)
    y0, hidden_0, slope_0, *fwd_0 = run(
        functools.partial(feed_kernel, 0, shards),
        [piece, wide_piece, ((rows, feed_width), low)] + [((rows, 2 * width + WIDE), low)] * GROUP,
        [out_scratch, *feed_scratch, *split_scratch, vm((16, width), low), dma, dma((3 * GROUP,))],
        (sc, x, *att, norms_own, norms_oth, *weights),
        "svvvvvvvaaaaaa",
    )
    gathered_1 = exchange(y0)
    cots = [cot, other_way(cot, 1), None, other_way(cot, 3)]
    *gathered_1, fwd_0[1], fwd_0[2], cots[1], cots[3] = together(*gathered_1, fwd_0[1], fwd_0[2], cots[1], cots[3])
    fwd_0[1], fwd_0[2] = towards(fwd_0[1], 1), towards(fwd_0[2], 2)
    n1_1, qkv_1, probs_1, *att = attend(1, gathered_1, cos, sin)
    att = exchange(att)
    *att, fwd_0[1], fwd_0[2], fwd_0[3] = together(*att, *fwd_0[1:])
    fwd_0[3] = towards(fwd_0[3], 3)
    y1, gh_1, dn2_1, *rest = run(
        functools.partial(feed_turn_kernel, 1, shards, owner),
        [piece, wide_piece, pair] + [((rows, width + WIDE), low)] * GROUP + [((rows, 2 * width), low)] * GROUP + [piece] * GROUP,
        [
            out_scratch, *feed_scratch, *split_scratch, vm((rows, width), full), vm((rows, feed_width), low),
            vm((GROUP, rows, chunk), low), dma((3 * GROUP,)),
        ],
        (sc, y0, *att, norms_own, norms_oth, cot, *weights),
        "svvvvvvvvaaaaaa",
    )
    ga, up_1, down_1 = rest[:GROUP], rest[GROUP : 2 * GROUP], rest[2 * GROUP :]
    *ga, fwd_0[3] = together(*ga, fwd_0[3])
    ga_1 = exchange(ga)
    *ga_1, cots[2], down_1[1], down_1[3], up_1[1], up_1[2] = together(*ga_1, cot, down_1[1], down_1[3], up_1[1], up_1[2])
    cots[2] = other_way(cots[2], 2)
    up_1[1], up_1[2] = towards(up_1[1], 1), towards(up_1[2], 2)
    gmixed_1, *back = attend_back(1, ga_1, qkv_1, probs_1)
    *back, up_1[1], up_1[2], up_1[3], down_1[1], down_1[3], cots[2] = together(*back, *up_1[1:], down_1[1], down_1[3], cots[2])
    back = exchange(back)
    down_1[1], down_1[3] = other_way(down_1[1], 1), other_way(down_1[3], 3)
    att_1, att_1_go = attend_grads(n1_1, gmixed_1, ga_1, ga_1, width)
    *back, down_1[1], down_1[2], down_1[3], up_1[3], att_1, att_1_go = together(*back, *down_1[1:], up_1[3], att_1, att_1_go)
    up_1[3] = towards(up_1[3], 3)
    att_1_got = swap(att_1_go)
    gx_1, dn1_1, ga, gh_0, dn2_0, *bwd_0 = run(
        functools.partial(turn_kernel, 0),
        [wide_piece, pair, piece, wide_piece, pair] + [((rows, 2 * width), low)] * GROUP,
        [*feed_scratch, vm((GROUP, rows, chunk), low), dma((2 * GROUP,))],
        (sc, *back, gh_1, y0, hidden_0, slope_0, norms_own, norms_oth, up_own, up_oth, dn_own, dn_oth),
        "svvvvvvvvvvaaaa",
    )
    ga, att_1_got, up_1[3], down_1[2] = together(ga, att_1_got, up_1[3], down_1[2])
    ga_0 = exchange(ga)
    down_1[2] = other_way(down_1[2], 2)
    up_1_stay, up_1_go = pair_grads((up_1, up_1, 0, width))
    up_1_got = swap(up_1_go)
    grads_1 = blocks_of([attend_size, square], [att_1, up_1_stay], [att_1_got, up_1_got])
    *ga_0, grads_1, bwd_0[1], bwd_0[2], down_1[2] = together(*ga_0, grads_1, bwd_0[1], bwd_0[2], down_1[2])
    sum_1 = over_dp(grads_1)
    bwd_0[1], bwd_0[2] = towards(bwd_0[1], 1), towards(bwd_0[2], 2)
    gmixed_0, *back = attend_back(0, ga_0, qkv_0, probs_0)
    gmixed_0, *back, bwd_0[1], bwd_0[2], bwd_0[3] = together(gmixed_0, *back, *bwd_0[1:])
    bwd_0[3] = towards(bwd_0[3], 3)
    att_0, att_0_go = attend_grads(n1_0, gmixed_0, fwd_0, ga_0, 2 * width)
    att_0_got = swap(att_0_go)
    *back, att_0, att_0_got = together(*back, att_0, att_0_got)
    back = exchange(back)
    sum_0 = over_dp(blocks_of([attend_size], [att_0], [att_0_got]))
    down_1_stay, down_1_go = pair_grads((down_1, cots, 0, 0))
    bwd_0[3], down_1_stay, down_1_go = together(bwd_0[3], down_1_stay, down_1_go)
    up_0, up_0_go, down_0, down_0_go = pair_grads((fwd_0, bwd_0, 0, 0), (fwd_0, bwd_0, width, width))
    *back, up_0, up_0_go, down_0, down_0_go = together(*back, up_0, up_0_go, down_0, down_0_go)
    up_0_got, down_0_got, down_1_got = swap(up_0_go), swap(down_0_go), swap(down_1_go)
    kept, sent, sums, sums_sent = run(
        last_kernel, [wide_piece, wide_piece, ((4, width), full), ((4, width), full)],
        [vm((rows, width), full), vm((2, width), full)],
        (sc, *back, gh_0, x, norms_own, norms_oth, gx_1, dn1_1, dn2_1, dn2_0), "svvvvvvvvvvvv",
    )
    y_own, y_got = jnp.where(section == 0, y0, y1), swap(jnp.where(section == 0, y1, y0))
    sums, sums_sent, up_0_got, down_0_got, down_1_got, sum_1, y_got = together(sums, sums_sent, up_0_got, down_0_got, down_1_got, sum_1, y_got)
    sums_got = swap(sums_sent)
    sums = sums + sums_got
    if small:
        grads_0 = blocks_of([square, square], [up_0, down_0], [up_0_got, down_0_got], sums)
        sum_feed_0 = over_dp(grads_0)
    if small:
        tall = width // shards
        lanes = width // LANES
        one, two = ((tall, half), low), ((2 * tall, half), low)
        down_1_stay, down_1_go = split(1, square, down_1_stay, down_1_got)
        down_1_got = towards(down_1_go, 1)
        att, att_go = run(attend_pack_kernel, [one, one], [], (sc, sum_0, sum_1), "shh")
        grad_out, *pieces = run(
            attend_finish_kernel, [((few * lanes, LANES), full)] + [((few, width), low)] * GROUP,
            [vm((tall, width), full), vm((few, width), full)], (sc, att, swap(att_go)), "svv",
        )
        down_1_got, grad_out, *pieces = together(down_1_got, grad_out, *pieces)
        down_1_stay, down_1_go = halve(1, down_1_stay, down_1_got)
        down_1_got = towards(down_1_go, 2)
        pieces = exchange(pieces)
        down_1_got, *pieces = together(down_1_got, *pieces)
        (feed,) = run(feed_pack_kernel, [two], [], (sum_1, down_1_stay, down_1_got), "hvv")
        feed_got = lax.ppermute(feed, "section", [(0, 1)])
        (grad_qkv,) = run(
            functools.partial(qkv_place_kernel, heads), [((few * 3 * lanes, LANES), full)],
            [vm((GROUP, few, 3 * WIDE), full), vm((few, 3 * width), full)], (sc, *pieces), "s" + "v" * GROUP,
        )
        sum_feed_0, grad_out, grad_qkv, feed_got = together(sum_feed_0, grad_out, grad_qkv, feed_got)
        grad_down, *pieces = run(
            feed_finish_kernel, [((tall * lanes, LANES), full)] + [((few + 16, width), low)] * GROUP, [vm((2 * tall, width), full)],
            (sc, feed, feed_got, sum_feed_0, lax.ppermute(sum_feed_0, "section", [(1, 0)])), "svvvv",
        )
        grad_up, grad_norms = run(
            up_place_kernel, [((few * GROUP * lanes, LANES), full), ((1, mine_wide), full)], [], (sc, *exchange(pieces)), "s" + "v" * GROUP,
        )
    else:
        sum_feed_0 = over_dp(blocks_of([square, square], [up_0, down_0], [up_0_got, down_0_got]))
        sum_down_1 = over_dp(blocks_of([square], [down_1_stay], [down_1_got]))
        grad_up, grad_down, grad_out, grad_qkv = many_shards(
            me, section, heads, few, jnp.concatenate([sum_0, sum_feed_0]), jnp.concatenate([sum_1, sum_down_1])
        )
        grad_norms = lax.psum_scatter(sums.reshape(shards * GROUP, -1), ("dp", "ctx"), scatter_dimension=0, tiled=True)

    def by_section(own, got):
        return jnp.where(section == 0, jnp.stack([own, got]), jnp.stack([got, own]))[None]

    return (
        by_section(y_own, y_got),
        by_section(kept, swap(sent)),
        grad_qkv.reshape(1, -1),
        grad_out.reshape(1, -1),
        grad_up.reshape(1, -1),
        grad_down.reshape(1, -1),
        grad_norms.reshape(1, -1),
    )


def many_shards(me, section, heads, few, first, second):
    own, other = jnp.where(section == 0, first, second), jnp.where(section == 0, second, first)
    got = swap(other)
    whole = jnp.where(section == 0, jnp.concatenate([own, got], axis=1), jnp.concatenate([got, own], axis=1))
    width = whole.shape[1]
    chunk, tall = width, GROUP * few
    t_qkv, t_out, t_up, t_down = whole[:tall], whole[tall : tall + few], whole[tall + few : 2 * tall + few], whole[2 * tall + few :]
    slim = jnp.concatenate([t_up, t_qkv], axis=1)
    slim = slim.reshape(GROUP, slim.shape[0] // GROUP, slim.shape[1])
    gets = jnp.stack(exchange([lax.dynamic_index_in_dim(slim, me ^ k, 0, keepdims=False) for k in range(GROUP)]))
    gets = jnp.stack([lax.dynamic_index_in_dim(gets, me ^ k, 0, keepdims=False) for k in range(GROUP)]).astype(full)
    few = gets.shape[1]
    grad_up = jnp.transpose(gets[:, :, :chunk], (1, 0, 2))
    cols = gets[:, :, chunk:].reshape(GROUP, few, 3, WIDE)
    turned = cols[:, :, :2].reshape(GROUP, few, 2, 2, LANES)[..., : heads * HALF]
    turned = turned.reshape(GROUP, few, 2, 2, heads, HALF).transpose(1, 2, 0, 4, 3, 5).reshape(few, 2 * width)
    plain = cols[:, :, 2, : heads * HEAD_DIM].transpose(1, 0, 2).reshape(few, width)
    return grad_up, t_down.astype(full), t_out.astype(full), jnp.concatenate([turned, plain], axis=1)


def solution(mesh):
    in_specs = (
        P(None, ("dp", "ctx"), None),
        P(None, ("dp", "ctx"), None),
        P("dp", None),
        P("section", None),
        P("section", None),
        P("section", None, None),
        P("section", None, None),
        P("section", None),
        P("section", None),
        P("section", None, None),
        P("section", None, None),
    )
    out_specs = (
        P("section", None, ("dp", "ctx"), None),
        P("section", None, ("dp", "ctx"), None),
        P("section", ("dp", "ctx")),
        P("section", ("dp", "ctx")),
        P("section", ("dp", "ctx")),
        P("section", ("dp", "ctx")),
        P("section", ("dp", "ctx")),
    )
    return jax.shard_map(
        on_device, mesh=mesh, in_specs=in_specs, out_specs=out_specs, check_vma=False
    )
```

```python
import functools
import math

import jax
import jax.numpy as jnp
from jax import lax
from jax.experimental import pallas as pl
from jax.experimental.pallas import tpu as pltpu
from jax.sharding import PartitionSpec as P

HEAD_DIM = 64
HALF = HEAD_DIM // 2
GROUP = 4
LANES = 128
WIDE = 2 * LANES

epsilon = 1e-05
rotary_base = 10000.0
masked_score = -1e30
low = jnp.bfloat16
full = jnp.float32

NT = (((1,), (1,)), ((), ()))
TN = (((0,), (0,)), ((), ()))


def mm(a, b):
    return jnp.dot(a, b, preferred_element_type=full)


def mm_nt(a, b):
    return lax.dot_general(a, b, NT, preferred_element_type=full)


def mm_tn(a, b):
    return lax.dot_general(a, b, TN, preferred_element_type=full)


def layer_norms(layer, sc, own, other):
    return jnp.where(sc[0] == layer, own[...], other[...])


def norm_stats(values):
    mean = jnp.mean(values, axis=-1, keepdims=True)
    centred = values - mean
    spread = jnp.mean(centred * centred, axis=-1, keepdims=True)
    scale = lax.rsqrt(spread + epsilon)
    return centred * scale, scale


def norm_backward(values, gain, grad):
    hat, scale = norm_stats(values)
    grad_gain = jnp.sum(grad * hat, axis=0, keepdims=True)
    grad_shift = jnp.sum(grad, axis=0, keepdims=True)
    inner = grad * gain
    first = jnp.mean(inner, axis=-1, keepdims=True)
    second = jnp.mean(inner * hat, axis=-1, keepdims=True)
    return scale * (inner - first - hat * second), grad_gain, grad_shift


def gelu_both(u):
    bell = jnp.exp(-0.5 * u * u)
    z = jnp.abs(u) * (0.5**0.5)
    t = 1.0 / (1.0 + 0.3275911 * z)
    poly = t * (
        0.254829592 + t * (-0.284496736 + t * (1.421413741 + t * (-1.453152027 + t * 1.061405429)))
    )
    tail = 0.5 * poly * bell
    cdf = jnp.where(u >= 0, 1.0 - tail, tail)
    return u * cdf, cdf + u * bell * (1.0 / math.sqrt(2.0 * math.pi))


class Fetch:
    def __init__(self, own, other, use_own, place, target, sem):
        self.parts = (own, other, use_own, place, target, sem)

    def start(self):
        own, other, use_own, place, target, sem = self.parts

        @pl.when(use_own)
        def _():
            pltpu.make_async_copy(own.at[place], target, sem).start()

        @pl.when(jnp.logical_not(use_own))
        def _():
            pltpu.make_async_copy(other.at[place], target, sem).start()

    def wait(self):
        own, other, use_own, place, target, sem = self.parts
        pltpu.make_async_copy(own.at[place], target, sem).wait()


def lane_index(shape):
    return lax.broadcasted_iota(jnp.int32, shape, 1)


def half_mask(head):
    return ((lane_index((1, WIDE)) & (LANES - 1)) // HALF) == head


def value_mask(head):
    return (lane_index((1, WIDE)) // HEAD_DIM) == head


def keep(values, mask):
    return jnp.where(mask, values, jnp.zeros_like(values))


class ProjectionWeights:
    def __init__(self, me, heads, mine, own, other, windows, target, sem):
        total = own.shape[0]
        at = me * (heads * HEAD_DIM)
        self.shift = lax.rem(at, LANES)
        start = at - self.shift
        self.windows, self.target, self.heads = windows, target, heads
        self.parts = []
        for part in range(3):
            span = pl.ds(pl.multiple_of(part * total + start, LANES), WIDE)
            self.parts.append(Fetch(own, other, mine, (slice(None), span), windows.at[part], sem.at[part]))

    def start(self):
        for part in self.parts:
            part.start()

    def wait(self):
        shape = (WIDE, WIDE)
        source, u = lax.broadcasted_iota(jnp.int32, shape, 0), lane_index(shape)
        v = u & (LANES - 1)
        turned = jnp.where(v < self.heads * HALF, (v // HALF) * HEAD_DIM + (u // LANES) * HALF + (v & (HALF - 1)) + self.shift, -1)
        plain = jnp.where(u < self.heads * HEAD_DIM, u + self.shift, -1)
        turned = jnp.where(source == turned, 1.0, 0.0).astype(low)
        plain = jnp.where(source == plain, 1.0, 0.0).astype(low)
        for part in range(3):
            self.parts[part].wait()
            chosen = mm(self.windows[part], plain if part == 2 else turned)
            self.target[:, part * WIDE : (part + 1) * WIDE] = chosen.astype(low)


def rotary_tables(me, bound, rows, cos, sin):
    for k in range(GROUP):
        here = slice(k * rows, (k + 1) * rows)
        spot = (me ^ k) * rows + lax.broadcasted_iota(jnp.int32, (rows, LANES), 0)
        relative = (spot - jnp.where(spot >= bound, bound, 0)).astype(full)
        steps = (lane_index((rows, LANES)) & (HALF - 1)).astype(full)
        angles = relative * jnp.exp(-math.log(rotary_base) * 2.0 * steps / HEAD_DIM)
        cos[here, :] = jnp.cos(angles)
        sin[here, :] = jnp.sin(angles)


def attend_kernel(layer, heads, sc, bounds, x0, x1, x2, x3, norms_own, norms_oth, *refs):
    bound = jnp.where(sc[0] == 0, bounds[0, 0], bounds[0, 1])
    if layer == 0:
        w_own, w_oth, cos, sin, n1, qkv, probs, a0, a1, a2, a3, win, w, mixed, scores, sem = refs
    else:
        cos, sin, w_own, w_oth, n1, qkv, probs, a0, a1, a2, a3, win, w, mixed, scores, sem = refs
    rows = x0.shape[0]
    weights = ProjectionWeights(sc[1], heads, sc[0] == layer, w_own, w_oth, win, w, sem)
    weights.start()
    if layer == 0:
        rotary_tables(sc[1], bound, rows, cos, sin)
    norms = layer_norms(layer, sc, norms_own, norms_oth)
    gain, shift = norms[0:1, :], norms[1:2, :]
    for k, x in enumerate((x0, x1, x2, x3)):
        hat, _ = norm_stats(x[...].astype(full))
        n1[k * rows : (k + 1) * rows, :] = (hat * gain + shift).astype(low)
    weights.wait()
    mixed[...] = mm(n1[...], w[...])
    for k in range(GROUP):
        here = slice(k * rows, (k + 1) * rows)
        c, s = cos[here, :], sin[here, :]
        for part in range(2):
            base = part * WIDE
            v1, v2 = mixed[here, base : base + LANES], mixed[here, base + LANES : base + WIDE]
            qkv[here, base : base + LANES] = (v1 * c - v2 * s).astype(low)
            qkv[here, base + LANES : base + WIDE] = (v2 * c + v1 * s).astype(low)
        qkv[here, 2 * WIDE :] = mixed[here, 2 * WIDE :].astype(low)
    me = sc[1]
    length = GROUP * rows
    spot = lax.broadcasted_iota(jnp.int32, (1, length), 1)
    place = jnp.zeros((1, length), jnp.int32)
    for k in range(GROUP):
        place = jnp.where(spot // rows == k, (me ^ k) * rows + spot - k * rows, place)
    seq_col = (place >= bound).astype(jnp.int32)
    for h in range(heads):
        scores[h] = mm_nt(keep(qkv[:, 0:WIDE], half_mask(h)), qkv[:, WIDE : 2 * WIDE])
    for h in range(heads):
        for k in range(GROUP):
            here = slice(k * rows, (k + 1) * rows)
            own = (me ^ k) * rows + lax.broadcasted_iota(jnp.int32, (rows, 1), 0)
            same = (own >= bound).astype(jnp.int32) == seq_col
            score = jnp.where(same, scores[h, here, :] * (HEAD_DIM**-0.5), masked_score)
            top = jnp.max(score, axis=-1, keepdims=True)
            expo = jnp.exp(score - top)
            probs[h, here, :] = (expo * (1.0 / jnp.sum(expo, axis=-1, keepdims=True))).astype(low)
    total = mm(probs[0], keep(qkv[:, 2 * WIDE :], value_mask(0)))
    for h in range(1, heads):
        total = total + mm(probs[h], keep(qkv[:, 2 * WIDE :], value_mask(h)))
    for k, out in enumerate((a0, a1, a2, a3)):
        out[...] = total[k * rows : (k + 1) * rows, : heads * HEAD_DIM].astype(low)


def attend_back_kernel(layer, heads, sc, g0, g1, g2, g3, qkv, probs, cos, sin, wo_own, wo_oth, w_own, w_oth, gmixed, p0, p1, p2, p3, wo, win, w, go, gs, qm, gom, ga, gp, sem):
    rows = g0.shape[0]
    width = heads * HEAD_DIM
    me = sc[1]
    mine = sc[0] == layer
    span = pl.ds(pl.multiple_of(me * width, HEAD_DIM), width)
    fetch_o = Fetch(wo_own, wo_oth, mine, (span, slice(None)), wo, sem.at[3])
    fetch_w = ProjectionWeights(me, heads, mine, w_own, w_oth, win, w, sem)
    fetch_o.start()
    fetch_w.start()
    length = GROUP * rows
    for k, g in enumerate((g0, g1, g2, g3)):
        ga[k * rows : (k + 1) * rows, :] = g[:, : wo.shape[1]]
    go[:, LANES:] = jnp.zeros((length, WIDE - LANES), low)
    fetch_o.wait()
    go[:, :width] = mm_nt(ga[...], wo[...]).astype(low)
    for h in range(heads):
        there = slice(h * length, (h + 1) * length)
        gom[there, :] = keep(go[...], value_mask(h))
        qm[there, :] = keep(qkv[:, 0:WIDE], half_mask(h))
        gp[h] = mm_nt(gom[there, :], qkv[:, 2 * WIDE :])
    for h in range(heads):
        for k in range(GROUP):
            here = slice(k * rows, (k + 1) * rows)
            p, g = probs[h, here, :].astype(full), gp[h, here, :]
            inner = jnp.sum(p * g, axis=-1, keepdims=True)
            gs[h * length + k * rows : h * length + (k + 1) * rows, :] = (p * (g - inner)).astype(low)
    gq = mm(gs[0:length, :], keep(qkv[:, WIDE : 2 * WIDE], half_mask(0)))
    gv = mm_tn(probs[0], gom[0:length, :])
    for h in range(1, heads):
        there = slice(h * length, (h + 1) * length)
        gq = gq + mm(gs[there, :], keep(qkv[:, WIDE : 2 * WIDE], half_mask(h)))
        gv = gv + mm_tn(probs[h], gom[there, :])
    gk = mm_tn(gs[...], qm[...])
    for base, value in ((0, gq), (WIDE, gk)):
        value = value * (HEAD_DIM**-0.5)
        v1, v2 = value[:, :LANES], value[:, LANES:]
        gmixed[:, base : base + LANES] = (v1 * cos[...] + v2 * sin[...]).astype(low)
        gmixed[:, base + LANES : base + WIDE] = (v2 * cos[...] - v1 * sin[...]).astype(low)
    gmixed[:, 2 * WIDE :] = gv.astype(low)
    fetch_w.wait()
    back = mm_nt(gmixed[...], w[...]).astype(low)
    for k, out in enumerate((p0, p1, p2, p3)):
        out[...] = back[k * rows : (k + 1) * rows, :]


class FeedWeights:
    def __init__(self, mine, up_own, up_oth, dn_own, dn_oth, wu, wd, sem, first):
        width = wu.shape[1]
        self.wu, self.wd = wu, wd
        self.up, self.down = [], []
        for j in range(GROUP):
            cut = slice(j * width, (j + 1) * width)
            self.up.append(Fetch(up_own, up_oth, mine, (slice(None), cut), wu.at[j], sem.at[first + j]))
            self.down.append(Fetch(dn_own, dn_oth, mine, (cut, slice(None)), wd.at[j], sem.at[first + GROUP + j]))


def feed_forward(sc, x, atts, norms, fetch_o, wo, feed, shards, y, hidden, slope, owner, parts, cols):
    rows, width = x.shape
    heads_wide = atts[0].shape[1]
    me = sc[1]
    for k in range(GROUP):
        fetch_o[k].wait()
    state = x[...].astype(full)
    for k in range(GROUP):
        state = state + mm(atts[k][...], wo[k])
        cols[me ^ k, :, :heads_wide] = atts[k][...]
    hidden[...] = state
    hat, _ = norm_stats(state)
    n2 = (hat * norms[2:3, :] + norms[3:4, :]).astype(low)
    step = width // (GROUP * shards)
    shares = []
    for target in range(GROUP):
        pieces = []
        for z in range(shards):
            at = (z * GROUP + target) * step
            pieces.append(cols[at // heads_wide, :, at % heads_wide : at % heads_wide + step])
        pieces.append(jnp.zeros((rows, WIDE - heads_wide), low))
        shares.append(jnp.concatenate(pieces, axis=1))
    for target in range(GROUP):
        cols[target] = shares[target]
    out = jnp.zeros((rows, width), full)
    chunk = feed.wu.shape[2]
    for j in range(GROUP):
        feed.up[j].wait()
        act, grad = gelu_both(mm(n2, feed.wu[j]))
        act = act.astype(low)
        slope[:, j * chunk : (j + 1) * chunk] = grad.astype(low)
        feed.down[j].wait()
        out = out + mm(act, feed.wd[j])
        if owner == 3:
            parts[j] = act
            continue
        span = chunk // shards
        for b in range(chunk // span):
            z, target = divmod(j * (chunk // span) + b, GROUP)
            parts[target, :, z * span : (z + 1) * span] = act[:, b * span : (b + 1) * span]
    y[...] = (hidden[...] + out).astype(low)
    return n2


def feed_back(gf, grad_out, norms, feed, hidden, slope, gas, gh, dnorm, gu, waited):
    rows, width = gf.shape
    chunk = feed.wu.shape[2]
    grad = jnp.zeros((rows, width), full)
    for j in range(GROUP):
        if not waited:
            feed.down[j].wait()
        got = mm_nt(gf, feed.wd[j]) * slope[:, j * chunk : (j + 1) * chunk].astype(full)
        got = got.astype(low)
        gu[j] = got
        if not waited:
            feed.up[j].wait()
        grad = grad + mm_nt(got, feed.wu[j])
    back, d_gain, d_shift = norm_backward(hidden[...], norms[2:3, :], grad)
    total = grad_out + back
    gh[...] = total
    for ga in gas:
        ga[:, 0:width] = total.astype(low)
    dnorm[0:1, :] = d_gain
    dnorm[1:2, :] = d_shift


def start_out(sc, mine, wo_own, wo_oth, wo, sem):
    width = wo.shape[1]
    out = []
    for k in range(GROUP):
        span = pl.ds(pl.multiple_of((sc[1] ^ k) * width, HEAD_DIM), width)
        out.append(Fetch(wo_own, wo_oth, mine, (span, slice(None)), wo.at[k], sem.at[k]))
    return out


def touch(x, spare, sem):
    copy = pltpu.make_async_copy(x.at[0 : spare.shape[0], :], spare, sem)
    copy.start()
    copy.wait()


def feed_kernel(layer, shards, sc, x, a0, a1, a2, a3, norms_own, norms_oth, wo_own, wo_oth, up_own, up_oth, dn_own, dn_oth, y, hidden, slope, m0, m1, m2, m3, wo, wu, wd, parts, cols, spare, spare_sem, sem):
    mine = sc[0] == layer
    norms = layer_norms(layer, sc, norms_own, norms_oth)
    fetch_o = start_out(sc, mine, wo_own, wo_oth, wo, sem)
    feed = FeedWeights(mine, up_own, up_oth, dn_own, dn_oth, wu, wd, sem, GROUP)
    for f in fetch_o + [f for pair in zip(feed.up, feed.down) for f in pair]:
        f.start()
    touch(x, spare, spare_sem)
    n2 = feed_forward(sc, x, (a0, a1, a2, a3), norms, fetch_o, wo, feed, shards, y, hidden, slope, 1, parts, cols)
    width = x.shape[1]
    for k, m in enumerate((m0, m1, m2, m3)):
        m[:, 0:width] = n2
        m[:, width : 2 * width] = parts[sc[1] ^ k]
        m[:, 2 * width :] = cols[sc[1] ^ k]


def feed_turn_kernel(layer, shards, owner, sc, x, a0, a1, a2, a3, norms_own, norms_oth, cot, wo_own, wo_oth, up_own, up_oth, dn_own, dn_oth, y, gh, dnorm, g0, g1, g2, g3, m0, m1, m2, m3, d0, d1, d2, d3, wo, wu, wd, parts, cols, hidden, slope, gu, sem):
    mine = sc[0] == layer
    norms = layer_norms(layer, sc, norms_own, norms_oth)
    fetch_o = start_out(sc, mine, wo_own, wo_oth, wo, sem)
    feed = FeedWeights(mine, up_own, up_oth, dn_own, dn_oth, wu, wd, sem, GROUP)
    for f in fetch_o + [f for pair in zip(feed.up, feed.down) for f in pair]:
        f.start()
    gas = (g0, g1, g2, g3)
    n2 = feed_forward(sc, x, (a0, a1, a2, a3), norms, fetch_o, wo, feed, shards, y, hidden, slope, owner, parts, cols)
    gf = cot[...]
    feed_back(gf, gf.astype(full), norms, feed, hidden, slope, gas, gh, dnorm, gu, True)
    width = x.shape[1]
    for k, (g, m, d) in enumerate(((g0, m0, d0), (g1, m1, d1), (g2, m2, d2), (g3, m3, d3))):
        g[:, width:] = cols[sc[1] ^ k]
        m[:, 0:width] = n2
        m[:, width:] = gu[sc[1] ^ k]
        d[...] = parts[sc[owner] ^ k]


def turn_kernel(layer, sc, r0, r1, r2, r3, gh_in, x_in, hidden, slope, norms_own, norms_oth, up_own, up_oth, dn_own, dn_oth, gx, dnorm_in, ga, gh, dnorm, m0, m1, m2, m3, wu, wd, gu, sem):
    mine = sc[0] == layer
    feed = FeedWeights(mine, up_own, up_oth, dn_own, dn_oth, wu, wd, sem, 0)
    for f in [f for pair in zip(feed.down, feed.up) for f in pair]:
        f.start()
    norms_in = layer_norms(layer + 1, sc, norms_own, norms_oth)
    norms = layer_norms(layer, sc, norms_own, norms_oth)
    top = first_norm_back(r0, r1, r2, r3, gh_in, x_in, norms_in, gx, dnorm_in)
    gf = top.astype(low)
    feed_back(gf, gf.astype(full), norms, feed, hidden, slope, (ga,), gh, dnorm, gu, False)
    width = gf.shape[1]
    for k, m in enumerate((m0, m1, m2, m3)):
        m[:, 0:width] = gu[sc[1] ^ k]
        m[:, width:] = gf


def first_norm_back(r0, r1, r2, r3, gh_in, x_in, norms_in, gx, dnorm):
    grad = r0[...].astype(full) + r1[...].astype(full) + r2[...].astype(full) + r3[...].astype(full)
    back, d_gain, d_shift = norm_backward(x_in[...].astype(full), norms_in[0:1, :], grad)
    dnorm[0:1, :] = d_gain
    dnorm[1:2, :] = d_shift
    total = gh_in[...] + back
    gx[...] = total
    return total


def last_kernel(sc, r0, r1, r2, r3, gh_in, x_in, norms_own, norms_oth, above, d1_1, d2_1, d2_0, kept, sent, sums, sums_sent, gx, dnorm):
    first_norm_back(r0, r1, r2, r3, gh_in, x_in, layer_norms(0, sc, norms_own, norms_oth), gx, dnorm)
    first = sc[0] == 0
    kept[...] = jnp.where(first, gx[...], above[...])
    sent[...] = jnp.where(first, above[...], gx[...])
    for at, zero, one in ((0, dnorm, d1_1), (2, d2_0, d2_1)):
        sums[at : at + 2, :] = jnp.where(first, zero[...], one[...])
        sums_sent[at : at + 2, :] = jnp.where(first, one[...], zero[...])


def gather_rows(pieces, at, target, half, section, sems):
    rows, width = pieces[0].shape[0], target.shape[1]
    copies = []
    for k, piece in enumerate(pieces):
        here = pl.ds(k * rows, rows)
        if half is None:
            copies.append(pltpu.make_async_copy(piece.at[:, pl.ds(at, width)], target.at[here, :], sems.at[k]))
            continue
        for i, part in enumerate((section, 1 - section)):
            source = pl.ds(pl.multiple_of(at + part * half, LANES), half)
            copies.append(pltpu.make_async_copy(piece.at[:, source], target.at[here, pl.ds(i * half, half)], sems.at[2 * k + i]))
    for copy in copies:
        copy.start()
    return copies


def tall_product(left, right, stay, go, base, step):
    half = stay.shape[1]
    for i in range(left.shape[1] // step):
        cut, put = slice(i * step, (i + 1) * step), slice(base + i * step, base + (i + 1) * step)
        product = mm_tn(left[:, cut], right[...]).astype(low)
        stay[put, :] = product[:, :half]
        go[put, :] = product[:, half:]


def pair_grads_kernel(places, sc, *refs):
    count = len(places)
    outs, (a, b, sem) = refs[2 * GROUP * count : -3], refs[-3:]
    half = outs[0].shape[1]
    copies = []
    for i, (at_left, at_right) in enumerate(places):
        lefts, rights = refs[2 * GROUP * i :][:GROUP], refs[2 * GROUP * i + GROUP :][:GROUP]
        copies.append(
            gather_rows(lefts, at_left, a.at[i], None, None, sem.at[2 * i]) + gather_rows(rights, at_right, b.at[i], half, sc[0], sem.at[2 * i + 1])
        )
    for i in range(count):
        for copy in copies[i]:
            copy.wait()
        tall_product(a.at[i], b.at[i], outs[2 * i], outs[2 * i + 1], 0, WIDE)


def padding_place(lane):
    part, u = lane // WIDE, lane & (WIDE - 1)
    v = u & (LANES - 1)
    used, half = 3 * HALF, WIDE - HEAD_DIM
    turned = jnp.where(v >= used, part * HEAD_DIM + (u // LANES) * HALF + v - used, -1)
    plain = jnp.where(u >= half, 2 * HEAD_DIM + u - half, -1)
    return jnp.where(part < 2, turned, plain)


def attend_grads_kernel(at_att, fold, sc, n1, gmixed, m0, m1, m2, m3, g0, g1, g2, g3, stay, go, left, right, a, b, sem):
    width, half = b.shape[1], stay.shape[1]
    first = gather_rows((n1,), 0, left, None, None, sem.at[0]) + gather_rows((gmixed,), 0, right, half, sc[0], sem.at[1])
    second = gather_rows((m0, m1, m2, m3), at_att, a, None, None, sem.at[2])
    second += gather_rows((g0, g1, g2, g3), 0, b, None if fold else half, sc[0], sem.at[3])
    for copy in first:
        copy.wait()
    tall_product(left, right, stay, go, 0, WIDE)
    for copy in second:
        copy.wait()
    if not fold:
        product = mm_tn(a[...], b[...])[: stay.shape[0] - width, :].astype(low)
        stay[width:, :] = product[:, :half]
        go[width:, :] = product[:, half:]
        return
    mine_wide = 3 * HEAD_DIM
    product = mm_tn(a[...], b[...])[:mine_wide, :].astype(low)
    shape = (mine_wide, 2 * half)
    lane = lane_index(shape)
    lane = jnp.where(lane < half, lane + sc[0] * half, lane - sc[0] * half)
    spread = jnp.where(lax.broadcasted_iota(jnp.int32, shape, 0) == padding_place(lane), 1.0, 0.0).astype(low)
    few = mine_wide // GROUP
    for q in range(GROUP):
        put = mm(product[:, q * mine_wide : (q + 1) * mine_wide], spread).astype(low)
        for z in range(GROUP):
            at = slice(z * mine_wide + q * few, z * mine_wide + (q + 1) * few)
            stay[at, :] = stay[at, :] + put[z * few : (z + 1) * few, :half]
            go[at, :] = go[at, :] + put[z * few : (z + 1) * few, half:]


def add_kernel(sizes, *refs):
    count = len(sizes)
    mine, theirs = refs[:count], refs[count : 2 * count]
    norms = refs[2 * count] if len(refs) > 2 * count + 1 else None
    out = refs[-1]
    blocks, total, half = out.shape
    for b in range(blocks):
        at = 0
        for x, y, size in zip(mine, theirs, sizes):
            base = 0
            for part in size:
                step = part // blocks
                span = slice(base + b * step, base + (b + 1) * step)
                out[b, at : at + step, :] = (x[span, :].astype(full) + y[span, :].astype(full)).astype(low)
                at += step
                base += part
        if norms is not None:
            row = lax.broadcasted_iota(jnp.int32, (total - at, half), 0)
            lower, upper = norms[b : b + 1, :half], norms[b : b + 1, half:]
            out[b, at:, :] = jnp.where(row == 0, lower, jnp.where(row == 1, upper, 0.0)).astype(low)


def split_kernel(axis, sizes, sc, mine, theirs, stay, go):
    for out, flip in ((stay, 0), (go, 1)):
        for j in range(2):
            block = 2 * j + ((sc[axis] & 1) ^ flip)
            at, base = 0, 0
            for size in sizes:
                step = size // GROUP
                span = pl.ds(pl.multiple_of(base + block * step, 16), step)
                out[j, at : at + step, :] = (mine[span, :].astype(full) + theirs[span, :].astype(full)).astype(low)
                at += step
                base += size


def halve_kernel(axis, sc, held, got, stay, go):
    high = sc[axis] >> 1
    stay[...] = held[high].astype(full) + got[high].astype(full)
    go[...] = (held[1 - high].astype(full) + got[1 - high].astype(full)).astype(low)


def attend_pack_kernel(sc, att_0, grads_1, stay, go):
    first = sc[0] == 0
    zero, one = att_0[...], grads_1[0 : att_0.shape[0], :]
    stay[...] = jnp.where(first, zero, one)
    go[...] = jnp.where(first, one, zero)


def feed_pack_kernel(grads_1, down_1, down_1_got, out):
    split = down_1.shape[0]
    out[0:split, :] = grads_1[split:, :]
    out[split:, :] = (down_1[...] + down_1_got[...].astype(full)).astype(low)


def spread_rows(out, values, start, stride):
    for j in range(values.shape[1] // LANES):
        out[pl.ds(start + j, values.shape[0], stride=stride), :] = values[:, j * LANES : (j + 1) * LANES]


def join_halves(sc, whole, mine, theirs):
    half = mine.shape[1]
    whole[:, pl.ds(pl.multiple_of(sc[0] * half, LANES), half)] = mine[...].astype(full)
    whole[:, pl.ds(pl.multiple_of((1 - sc[0]) * half, LANES), half)] = theirs[...].astype(full)


def attend_finish_kernel(sc, mine, theirs, grad_out, v0, v1, v2, v3, whole, out):
    join_halves(sc, whole, mine, theirs)
    width = whole.shape[1]
    step = width // GROUP
    few = step // GROUP
    shape = (width, step)
    gather = jnp.where(padding_place(lax.broadcasted_iota(jnp.int32, shape, 0)) == lane_index(shape), 1.0, 0.0).astype(low)
    for q in range(GROUP):
        out[:, q * step : (q + 1) * step] = mm(whole[q * few : (q + 1) * few, :].astype(low), gather)
    spread_rows(grad_out, out[...], 0, width // LANES)
    for k, v in enumerate((v0, v1, v2, v3)):
        v[...] = whole[pl.ds(pl.multiple_of((sc[1] ^ k) * few, few), few), :].astype(low)


def qkv_place_kernel(heads, sc, v0, v1, v2, v3, grad_qkv, natural, whole):
    mine_wide = heads * HEAD_DIM
    shape = (WIDE, WIDE)
    source, out = lax.broadcasted_iota(jnp.int32, shape, 0), lane_index(shape)
    v = source & (LANES - 1)
    column = jnp.where(v < heads * HALF, (v // HALF) * HEAD_DIM + (source // LANES) * HALF + (v & (HALF - 1)), -1)
    back = jnp.where(out == column, 1.0, 0.0).astype(low)
    for k, piece in enumerate((v0, v1, v2, v3)):
        for part in range(3):
            values = piece[:, part * WIDE : (part + 1) * WIDE]
            natural[sc[1] ^ k, :, part * WIDE : (part + 1) * WIDE] = values.astype(full) if part == 2 else mm(values, back)
    for part in range(3):
        for c in range(GROUP):
            to = (part * GROUP + c) * mine_wide
            whole[:, to : to + mine_wide] = natural[c, :, part * WIDE : part * WIDE + mine_wide]
    spread_rows(grad_qkv, whole[...], 0, whole.shape[1] // LANES)


def feed_finish_kernel(sc, mine, theirs, feed_0, feed_0_got, grad_down, u0, u1, u2, u3, whole):
    join_halves(sc, whole, mine, theirs)
    half = mine.shape[1]
    width = 2 * half
    step = width // GROUP
    few = step // GROUP

    @pl.when(sc[0] == 0)
    def _():
        whole[:, 0:half] = feed_0[0 : 2 * step, :].astype(full)
        whole[:, half:] = feed_0_got[0 : 2 * step, :].astype(full)

    last = jnp.concatenate([feed_0[2 * step : 2 * step + 1, :], feed_0[2 * step + 1 : 2 * step + 2, :]], axis=1)
    shares = [last[:, c * step : (c + 1) * step] for c in range(GROUP)]
    for k, u in enumerate((u0, u1, u2, u3)):
        u[0:few, :] = whole[pl.ds(pl.multiple_of((sc[1] ^ k) * few, few), few), :].astype(low)
        share = jnp.zeros_like(shares[0])
        for c in range(GROUP):
            share = jnp.where((sc[1] ^ k) == c, shares[c], share)
        u[few:, :] = jnp.zeros((u.shape[0] - few, width), low)
        u[few : few + 1, :step] = share
    spread_rows(grad_down, whole[step:, :], 0, width // LANES)


def up_place_kernel(sc, u0, u1, u2, u3, grad_up, grad_norms):
    step = grad_norms.shape[1]
    few = step // GROUP
    per = u0.shape[1] // LANES
    norm = jnp.zeros((1, step), full)
    for k, u in enumerate((u0, u1, u2, u3)):
        spread_rows(grad_up, u[0:few, :].astype(full), (sc[1] ^ k) * per, GROUP * per)
        norm = norm + u[few : few + 1, :step].astype(full)
    grad_norms[...] = norm


class Late:
    def __init__(self, source, held, sem):
        self.copy, self.held, self.shape, self.here = pltpu.make_async_copy(source, held, sem), held, held.shape, False
        self.copy.start()

    def __getitem__(self, index):
        if not self.here:
            self.copy.wait()
            self.here = True
        return self.held[index]


def run(kernel, shapes, scratch, operands, spaces):
    place = {"s": pltpu.SMEM, "v": pltpu.VMEM, "a": pl.ANY, "h": pltpu.HBM}
    total = len(operands) + len(shapes) + len(scratch)
    late = [i for i, space in enumerate(spaces) if space == "h"]
    held = [pltpu.VMEM(operands[i].shape, operands[i].dtype) for i in late]

    def body(*refs):
        given = list(refs[:total])
        for n, i in enumerate(late):
            given[i] = Late(given[i], refs[total + n], refs[-1].at[n])
        kernel(*given)
        for i in late:
            given[i][...]

    return pl.pallas_call(
        body,
        out_shape=[jax.ShapeDtypeStruct(shape, kind) for shape, kind in shapes],
        in_specs=[pl.BlockSpec(memory_space=place[space]) for space in spaces],
        out_specs=[pl.BlockSpec(memory_space=pltpu.VMEM) for _ in shapes],
        scratch_shapes=[*scratch, *held, pltpu.SemaphoreType.DMA((len(held),))] if held else scratch,
        compiler_params=pltpu.CompilerParams(vmem_limit_bytes=52 * 2**20),
        cost_estimate=pl.CostEstimate(flops=1, bytes_accessed=1, transcendentals=0),
    )(*operands)


def exchange(value):
    values = value if isinstance(value, (list, tuple)) else [value] * GROUP
    return [values[0]] + [
        lax.ppermute(values[k], "ctx", [(i, i ^ k) for i in range(GROUP)]) for k in range(1, GROUP)
    ]


def towards(value, k):
    return lax.ppermute(value, "ctx", [(i, i ^ k) for i in range(GROUP)])


def along(value, k):
    count = lax.axis_size("dp")
    return lax.ppermute(value, "dp", [(i, i ^ k) for i in range(count)])


def swap(value):
    return lax.ppermute(value, "section", [(0, 1), (1, 0)])


def together(*values):
    return lax.optimization_barrier(values)


def on_device(tokens, cotangent, seq_bound, ln1_gain, ln1_shift, w_qkv, w_out, ln2_gain, ln2_shift, w_up, w_down):
    section = lax.axis_index("section")
    me = lax.axis_index("ctx")
    shards = lax.axis_size("dp")
    z = lax.axis_index("dp")
    rows, width = tokens.shape[1:]
    feed_width = w_up.shape[2]
    chunk = feed_width // GROUP
    heads = width // HEAD_DIM // GROUP
    mine_wide = heads * HEAD_DIM
    length = GROUP * rows
    few = width // (GROUP * shards)
    sc = jnp.stack([section, me, section, z]).astype(jnp.int32)

    dma = pltpu.SemaphoreType.DMA
    vm = pltpu.VMEM
    piece = ((rows, width), low)
    wide_piece = ((rows, width), full)
    pair = ((2, width), full)

    x = lax.dynamic_index_in_dim(tokens, section, 0, keepdims=False)
    gathered = exchange(x)
    wq_own, wo_own, up_own, dn_own = w_qkv[0], w_out[0], w_up[0], w_down[0]
    wq_oth, wo_oth = swap(wq_own), swap(wo_own)
    norms_own = jnp.concatenate([ln1_gain, ln1_shift, ln2_gain, ln2_shift], axis=0)
    wo_oth, later = together(wo_oth, norms_own)
    norms_oth = swap(later)
    wq_oth, norms_oth, later = together(wq_oth, norms_oth, up_own)
    up_oth = swap(later)
    *gathered, later = together(*gathered, dn_own)
    dn_oth = swap(later)

    def attend(layer, gathered, *tables):
        table = ((length, LANES), full)
        given = len(tables)
        return run(
            functools.partial(attend_kernel, layer, heads),
            [table] * (2 - given) + [((length, width), low), ((length, 3 * WIDE), low), ((heads, length, length), low)] + [((rows, mine_wide), low)] * GROUP,
            [vm((3, width, WIDE), low), vm((width, 3 * WIDE), low), vm((length, 3 * WIDE), full), vm((heads, length, length), full), dma((3,))],
            (sc, seq_bound, *gathered, norms_own, norms_oth, *tables, wq_own, wq_oth),
            "ssvvvvvv" + "v" * given + "aa",
        )

    def attend_back(layer, grads, qkv, probs):
        return run(
            functools.partial(attend_back_kernel, layer, heads),
            [((length, 3 * WIDE), low)] + [piece] * GROUP,
            [
                vm((mine_wide, width), low), vm((3, width, WIDE), low), vm((width, 3 * WIDE), low), vm((length, WIDE), low),
                vm((heads * length, length), low), vm((heads * length, WIDE), low), vm((heads * length, WIDE), low),
                vm((length, width), low), vm((heads, length, length), full), dma((4,)),
            ],
            (sc, *grads, qkv, probs, cos, sin, wo_own, wo_oth, wq_own, wq_oth),
            "svvvvvvvvaaaa",
        )

    half = width // 2
    small = shards == GROUP
    square, attend_size = (width,), (width,) if small else (width, mine_wide)

    def pair_grads(*products):
        out = ((width, half), low)
        operands = [piece for lefts, rights, _, _ in products for piece in (*lefts, *rights)]
        places = [(at_left, at_right) for _, _, at_left, at_right in products]
        return run(
            functools.partial(pair_grads_kernel, places),
            [out] * (2 * len(products)),
            [vm((len(products), length, width), low), vm((len(products), length, width), low), dma((2 * len(products), 2 * GROUP))],
            (sc, *operands), "s" + "a" * len(operands),
        )

    def attend_grads(n1, gmixed, fwd, ga, at_att):
        return run(
            functools.partial(attend_grads_kernel, at_att, small),
            [((sum(attend_size), half), low)] * 2,
            [vm((length, width), low), vm((length, 3 * WIDE), low), vm((length, WIDE), low), vm((length, width), low), dma((4, 2 * GROUP))],
            (sc, n1, gmixed, *fwd, *ga), "s" + "a" * (2 + 2 * GROUP),
        )


    def blocks_of(sizes, mine, theirs, *norms):
        total = sum(sum(size) for size in sizes) // shards + (16 if norms else 0)
        if small:
            (blocks,) = run(
                functools.partial(add_kernel, sizes), [((shards, total, half), low)], [], (*mine, *theirs, *norms),
                "v" * (2 * len(mine) + len(norms)),
            )
        else:
            parts = []
            for x, y, size in zip(mine, theirs, sizes):
                value = (x.astype(full) + y.astype(full)).astype(low)
                base = 0
                for part in size:
                    parts.append(value[base : base + part].reshape(shards, part // shards, half))
                    base += part
            blocks = jnp.concatenate(parts, axis=1)
        return blocks

    def over_dp(blocks):
        return lax.psum_scatter(blocks, "dp", scatter_dimension=0, tiled=False)

    def split(axis, sizes, mine, theirs):
        part = ((2, sum(sizes) // GROUP, half), low)
        return run(functools.partial(split_kernel, axis, sizes), [part, part], [], (sc, mine, theirs), "svv")

    def halve(axis, stay, got):
        part = stay.shape[1:]
        return run(functools.partial(halve_kernel, axis), [(part, full), (part, low)], [], (sc, stay, got), "svv")

    def level(token, *values):
        token, *values = together(token, *values)
        return together(swap(token), *values)[1:]

    feed_scratch = [vm((GROUP, width, chunk), low), vm((GROUP, chunk, width), low)]
    out_scratch = vm((GROUP, mine_wide, width), low)
    split_scratch = [vm((GROUP, rows, chunk), low), vm((GROUP, rows, WIDE), low)]
    owner, other_way = (3, along) if small else (1, towards)

    cos, sin, n1_0, qkv_0, probs_0, *att = attend(0, gathered)
    att = exchange(att)
    weights = (wo_own, wo_oth, up_own, up_oth, dn_own, dn_oth)
    cot = lax.dynamic_index_in_dim(cotangent, section, 0, keepdims=False)
    *att, cot = together(*att, cot)
    y0, hidden_0, slope_0, *fwd_0 = run(
        functools.partial(feed_kernel, 0, shards),
        [piece, wide_piece, ((rows, feed_width), low)] + [((rows, 2 * width + WIDE), low)] * GROUP,
        [out_scratch, *feed_scratch, *split_scratch, vm((16, width), low), dma, dma((3 * GROUP,))],
        (sc, x, *att, norms_own, norms_oth, *weights),
        "svvvvvvvaaaaaa",
    )
    gathered_1 = exchange(y0)
    cots = [cot, other_way(cot, 1), None, other_way(cot, 3)]
    *gathered_1, fwd_0[1], fwd_0[2], cots[1], cots[3] = together(*gathered_1, fwd_0[1], fwd_0[2], cots[1], cots[3])
    fwd_0[1], fwd_0[2] = towards(fwd_0[1], 1), towards(fwd_0[2], 2)
    n1_1, qkv_1, probs_1, *att = attend(1, gathered_1, cos, sin)
    att = exchange(att)
    *att, fwd_0[1], fwd_0[2], fwd_0[3] = together(*att, *fwd_0[1:])
    fwd_0[3] = towards(fwd_0[3], 3)
    y1, gh_1, dn2_1, *rest = run(
        functools.partial(feed_turn_kernel, 1, shards, owner),
        [piece, wide_piece, pair] + [((rows, width + WIDE), low)] * GROUP + [((rows, 2 * width), low)] * GROUP + [piece] * GROUP,
        [
            out_scratch, *feed_scratch, *split_scratch, vm((rows, width), full), vm((rows, feed_width), low),
            vm((GROUP, rows, chunk), low), dma((3 * GROUP,)),
        ],
        (sc, y0, *att, norms_own, norms_oth, cot, *weights),
        "svvvvvvvvaaaaaa",
    )
    ga, up_1, down_1 = rest[:GROUP], rest[GROUP : 2 * GROUP], rest[2 * GROUP :]
    *ga, fwd_0[3] = together(*ga, fwd_0[3])
    ga_1 = exchange(ga)
    *ga_1, cots[2], down_1[1], down_1[3], up_1[1], up_1[2] = together(*ga_1, cot, down_1[1], down_1[3], up_1[1], up_1[2])
    cots[2] = other_way(cots[2], 2)
    up_1[1], up_1[2] = towards(up_1[1], 1), towards(up_1[2], 2)
    gmixed_1, *back = attend_back(1, ga_1, qkv_1, probs_1)
    *back, up_1[1], up_1[2], up_1[3], down_1[1], down_1[3], cots[2] = together(*back, *up_1[1:], down_1[1], down_1[3], cots[2])
    back = exchange(back)
    down_1[1], down_1[3] = other_way(down_1[1], 1), other_way(down_1[3], 3)
    att_1, att_1_go = attend_grads(n1_1, gmixed_1, ga_1, ga_1, width)
    *back, down_1[1], down_1[2], down_1[3], up_1[3], att_1, att_1_go = together(*back, *down_1[1:], up_1[3], att_1, att_1_go)
    down_1[2] = other_way(down_1[2], 2)
    up_1[3] = towards(up_1[3], 3)
    att_1_got = swap(att_1_go)
    gx_1, dn1_1, ga, gh_0, dn2_0, *bwd_0 = run(
        functools.partial(turn_kernel, 0),
        [wide_piece, pair, piece, wide_piece, pair] + [((rows, 2 * width), low)] * GROUP,
        [*feed_scratch, vm((GROUP, rows, chunk), low), dma((2 * GROUP,))],
        (sc, *back, gh_1, y0, hidden_0, slope_0, norms_own, norms_oth, up_own, up_oth, dn_own, dn_oth),
        "svvvvvvvvvvaaaa",
    )
    ga, att_1_got, up_1[3], down_1[2] = together(ga, att_1_got, up_1[3], down_1[2])
    ga_0 = exchange(ga)
    up_1_stay, up_1_go = pair_grads((up_1, up_1, 0, width))
    up_1_got = swap(up_1_go)
    grads_1 = blocks_of([attend_size, square], [att_1, up_1_stay], [att_1_got, up_1_got])
    *ga_0, grads_1, bwd_0[1], bwd_0[2] = together(*ga_0, grads_1, bwd_0[1], bwd_0[2])
    sum_1 = over_dp(grads_1)
    bwd_0[1], bwd_0[2] = towards(bwd_0[1], 1), towards(bwd_0[2], 2)
    gmixed_0, *back = attend_back(0, ga_0, qkv_0, probs_0)
    gmixed_0, *back, bwd_0[1], bwd_0[2], bwd_0[3] = together(gmixed_0, *back, *bwd_0[1:])
    bwd_0[3] = towards(bwd_0[3], 3)
    att_0, att_0_go = attend_grads(n1_0, gmixed_0, fwd_0, ga_0, 2 * width)
    att_0_got = swap(att_0_go)
    *back, att_0, att_0_got = together(*back, att_0, att_0_got)
    back = exchange(back)
    sum_0 = over_dp(blocks_of([attend_size], [att_0], [att_0_got]))
    down_1_stay, down_1_go = pair_grads((down_1, cots, 0, 0))
    bwd_0[3], down_1_stay, down_1_go = together(bwd_0[3], down_1_stay, down_1_go)
    up_0, up_0_go, down_0, down_0_go = pair_grads((fwd_0, bwd_0, 0, 0), (fwd_0, bwd_0, width, width))
    *back, up_0, up_0_go, down_0, down_0_go = together(*back, up_0, up_0_go, down_0, down_0_go)
    up_0_got, down_0_got, down_1_got = swap(up_0_go), swap(down_0_go), swap(down_1_go)
    kept, sent, sums, sums_sent = run(
        last_kernel, [wide_piece, wide_piece, ((4, width), full), ((4, width), full)],
        [vm((rows, width), full), vm((2, width), full)],
        (sc, *back, gh_0, x, norms_own, norms_oth, gx_1, dn1_1, dn2_1, dn2_0), "svvvvvvvvvvvv",
    )
    y_own, y_got = jnp.where(section == 0, y0, y1), swap(jnp.where(section == 0, y1, y0))
    sums, sums_sent, up_0_got, down_0_got, down_1_got, sum_1, y_got = together(sums, sums_sent, up_0_got, down_0_got, down_1_got, sum_1, y_got)
    sums_got = swap(sums_sent)
    sums = sums + sums_got
    if small:
        grads_0 = blocks_of([square, square], [up_0, down_0], [up_0_got, down_0_got], sums)
        sum_feed_0 = over_dp(grads_0)
    if small:
        tall = width // shards
        lanes = width // LANES
        one, two = ((tall, half), low), ((2 * tall, half), low)
        down_1_stay, down_1_go = split(1, square, down_1_stay, down_1_got)
        down_1_got = towards(down_1_go, 1)
        att, att_go = run(attend_pack_kernel, [one, one], [], (sc, sum_0, sum_1), "shh")
        grad_out, *pieces = run(
            attend_finish_kernel, [((few * lanes, LANES), full)] + [((few, width), low)] * GROUP,
            [vm((tall, width), full), vm((few, width), full)], (sc, att, swap(att_go)), "svv",
        )
        down_1_got, grad_out, *pieces = together(down_1_got, grad_out, *pieces)
        down_1_stay, down_1_go = halve(1, down_1_stay, down_1_got)
        down_1_got = towards(down_1_go, 2)
        pieces = exchange(pieces)
        down_1_got, *pieces = together(down_1_got, *pieces)
        (feed,) = run(feed_pack_kernel, [two], [], (sum_1, down_1_stay, down_1_got), "hvv")
        feed_got = lax.ppermute(feed, "section", [(0, 1)])
        (grad_qkv,) = run(
            functools.partial(qkv_place_kernel, heads), [((few * 3 * lanes, LANES), full)],
            [vm((GROUP, few, 3 * WIDE), full), vm((few, 3 * width), full)], (sc, *pieces), "s" + "v" * GROUP,
        )
        sum_feed_0, grad_out, grad_qkv, feed_got = together(sum_feed_0, grad_out, grad_qkv, feed_got)
        grad_down, *pieces = run(
            feed_finish_kernel, [((tall * lanes, LANES), full)] + [((few + 16, width), low)] * GROUP, [vm((2 * tall, width), full)],
            (sc, feed, feed_got, sum_feed_0, lax.ppermute(sum_feed_0, "section", [(1, 0)])), "svvvv",
        )
        grad_up, grad_norms = run(
            up_place_kernel, [((few * GROUP * lanes, LANES), full), ((1, mine_wide), full)], [], (sc, *exchange(pieces)), "s" + "v" * GROUP,
        )
    else:
        sum_feed_0 = over_dp(blocks_of([square, square], [up_0, down_0], [up_0_got, down_0_got]))
        sum_down_1 = over_dp(blocks_of([square], [down_1_stay], [down_1_got]))
        grad_up, grad_down, grad_out, grad_qkv = many_shards(
            me, section, heads, few, jnp.concatenate([sum_0, sum_feed_0]), jnp.concatenate([sum_1, sum_down_1])
        )
        grad_norms = lax.psum_scatter(sums.reshape(shards * GROUP, -1), ("dp", "ctx"), scatter_dimension=0, tiled=True)

    def by_section(own, got):
        return jnp.where(section == 0, jnp.stack([own, got]), jnp.stack([got, own]))[None]

    return (
        by_section(y_own, y_got),
        by_section(kept, swap(sent)),
        grad_qkv.reshape(1, -1),
        grad_out.reshape(1, -1),
        grad_up.reshape(1, -1),
        grad_down.reshape(1, -1),
        grad_norms.reshape(1, -1),
    )


def many_shards(me, section, heads, few, first, second):
    own, other = jnp.where(section == 0, first, second), jnp.where(section == 0, second, first)
    got = swap(other)
    whole = jnp.where(section == 0, jnp.concatenate([own, got], axis=1), jnp.concatenate([got, own], axis=1))
    width = whole.shape[1]
    chunk, tall = width, GROUP * few
    t_qkv, t_out, t_up, t_down = whole[:tall], whole[tall : tall + few], whole[tall + few : 2 * tall + few], whole[2 * tall + few :]
    slim = jnp.concatenate([t_up, t_qkv], axis=1)
    slim = slim.reshape(GROUP, slim.shape[0] // GROUP, slim.shape[1])
    gets = jnp.stack(exchange([lax.dynamic_index_in_dim(slim, me ^ k, 0, keepdims=False) for k in range(GROUP)]))
    gets = jnp.stack([lax.dynamic_index_in_dim(gets, me ^ k, 0, keepdims=False) for k in range(GROUP)]).astype(full)
    few = gets.shape[1]
    grad_up = jnp.transpose(gets[:, :, :chunk], (1, 0, 2))
    cols = gets[:, :, chunk:].reshape(GROUP, few, 3, WIDE)
    turned = cols[:, :, :2].reshape(GROUP, few, 2, 2, LANES)[..., : heads * HALF]
    turned = turned.reshape(GROUP, few, 2, 2, heads, HALF).transpose(1, 2, 0, 4, 3, 5).reshape(few, 2 * width)
    plain = cols[:, :, 2, : heads * HEAD_DIM].transpose(1, 0, 2).reshape(few, width)
    return grad_up, t_down.astype(full), t_out.astype(full), jnp.concatenate([turned, plain], axis=1)


def solution(mesh):
    in_specs = (
        P(None, ("dp", "ctx"), None),
        P(None, ("dp", "ctx"), None),
        P("dp", None),
        P("section", None),
        P("section", None),
        P("section", None, None),
        P("section", None, None),
        P("section", None),
        P("section", None),
        P("section", None, None),
        P("section", None, None),
    )
    out_specs = (
        P("section", None, ("dp", "ctx"), None),
        P("section", None, ("dp", "ctx"), None),
        P("section", ("dp", "ctx")),
        P("section", ("dp", "ctx")),
        P("section", ("dp", "ctx")),
        P("section", ("dp", "ctx")),
        P("section", ("dp", "ctx")),
    )
    return jax.shard_map(
        on_device, mesh=mesh, in_specs=in_specs, out_specs=out_specs, check_vma=False
    )
```

```python
import functools
import math

import jax
import jax.numpy as jnp
from jax import lax
from jax.experimental import pallas as pl
from jax.experimental.pallas import tpu as pltpu
from jax.sharding import PartitionSpec as P

HEAD_DIM = 64
HALF = HEAD_DIM // 2
GROUP = 4
LANES = 128
WIDE = 2 * LANES

epsilon = 1e-05
rotary_base = 10000.0
masked_score = -1e30
low = jnp.bfloat16
full = jnp.float32

NT = (((1,), (1,)), ((), ()))
TN = (((0,), (0,)), ((), ()))


def mm(a, b):
    return jnp.dot(a, b, preferred_element_type=full)


def mm_nt(a, b):
    return lax.dot_general(a, b, NT, preferred_element_type=full)


def mm_tn(a, b):
    return lax.dot_general(a, b, TN, preferred_element_type=full)


def layer_norms(layer, sc, own, other):
    return jnp.where(sc[0] == layer, own[...], other[...])


def norm_stats(values):
    mean = jnp.mean(values, axis=-1, keepdims=True)
    centred = values - mean
    spread = jnp.mean(centred * centred, axis=-1, keepdims=True)
    scale = lax.rsqrt(spread + epsilon)
    return centred * scale, scale


def norm_backward(values, gain, grad):
    hat, scale = norm_stats(values)
    grad_gain = jnp.sum(grad * hat, axis=0, keepdims=True)
    grad_shift = jnp.sum(grad, axis=0, keepdims=True)
    inner = grad * gain
    first = jnp.mean(inner, axis=-1, keepdims=True)
    second = jnp.mean(inner * hat, axis=-1, keepdims=True)
    return scale * (inner - first - hat * second), grad_gain, grad_shift


def gelu_both(u):
    bell = jnp.exp(-0.5 * u * u)
    z = jnp.abs(u) * (0.5**0.5)
    t = 1.0 / (1.0 + 0.3275911 * z)
    poly = t * (
        0.254829592 + t * (-0.284496736 + t * (1.421413741 + t * (-1.453152027 + t * 1.061405429)))
    )
    tail = 0.5 * poly * bell
    cdf = jnp.where(u >= 0, 1.0 - tail, tail)
    return u * cdf, cdf + u * bell * (1.0 / math.sqrt(2.0 * math.pi))


class Fetch:
    def __init__(self, own, other, use_own, place, target, sem):
        self.parts = (own, other, use_own, place, target, sem)

    def start(self):
        own, other, use_own, place, target, sem = self.parts

        @pl.when(use_own)
        def _():
            pltpu.make_async_copy(own.at[place], target, sem).start()

        @pl.when(jnp.logical_not(use_own))
        def _():
            pltpu.make_async_copy(other.at[place], target, sem).start()

    def wait(self):
        own, other, use_own, place, target, sem = self.parts
        pltpu.make_async_copy(own.at[place], target, sem).wait()


def lane_index(shape):
    return lax.broadcasted_iota(jnp.int32, shape, 1)


def half_mask(head):
    return ((lane_index((1, WIDE)) & (LANES - 1)) // HALF) == head


def value_mask(head):
    return (lane_index((1, WIDE)) // HEAD_DIM) == head


def keep(values, mask):
    return jnp.where(mask, values, jnp.zeros_like(values))


class ProjectionWeights:
    def __init__(self, me, heads, mine, own, other, windows, target, sem):
        total = own.shape[0]
        at = me * (heads * HEAD_DIM)
        self.shift = lax.rem(at, LANES)
        start = at - self.shift
        self.windows, self.target, self.heads = windows, target, heads
        self.parts = []
        for part in range(3):
            span = pl.ds(pl.multiple_of(part * total + start, LANES), WIDE)
            self.parts.append(Fetch(own, other, mine, (slice(None), span), windows.at[part], sem.at[part]))

    def start(self):
        for part in self.parts:
            part.start()

    def wait(self):
        shape = (WIDE, WIDE)
        source, u = lax.broadcasted_iota(jnp.int32, shape, 0), lane_index(shape)
        v = u & (LANES - 1)
        turned = jnp.where(v < self.heads * HALF, (v // HALF) * HEAD_DIM + (u // LANES) * HALF + (v & (HALF - 1)) + self.shift, -1)
        plain = jnp.where(u < self.heads * HEAD_DIM, u + self.shift, -1)
        turned = jnp.where(source == turned, 1.0, 0.0).astype(low)
        plain = jnp.where(source == plain, 1.0, 0.0).astype(low)
        for part in range(3):
            self.parts[part].wait()
            chosen = mm(self.windows[part], plain if part == 2 else turned)
            self.target[:, part * WIDE : (part + 1) * WIDE] = chosen.astype(low)


def rotary_tables(me, bound, rows, cos, sin):
    for k in range(GROUP):
        here = slice(k * rows, (k + 1) * rows)
        spot = (me ^ k) * rows + lax.broadcasted_iota(jnp.int32, (rows, LANES), 0)
        relative = (spot - jnp.where(spot >= bound, bound, 0)).astype(full)
        steps = (lane_index((rows, LANES)) & (HALF - 1)).astype(full)
        angles = relative * jnp.exp(-math.log(rotary_base) * 2.0 * steps / HEAD_DIM)
        cos[here, :] = jnp.cos(angles)
        sin[here, :] = jnp.sin(angles)


def attend_kernel(layer, heads, sc, bounds, x0, x1, x2, x3, norms_own, norms_oth, *refs):
    bound = jnp.where(sc[0] == 0, bounds[0, 0], bounds[0, 1])
    if layer == 0:
        w_own, w_oth, cos, sin, n1, qkv, probs, a0, a1, a2, a3, win, w, mixed, scores, sem = refs
    else:
        cos, sin, w_own, w_oth, n1, qkv, probs, a0, a1, a2, a3, win, w, mixed, scores, sem = refs
    rows = x0.shape[0]
    weights = ProjectionWeights(sc[1], heads, sc[0] == layer, w_own, w_oth, win, w, sem)
    weights.start()
    if layer == 0:
        rotary_tables(sc[1], bound, rows, cos, sin)
    norms = layer_norms(layer, sc, norms_own, norms_oth)
    gain, shift = norms[0:1, :], norms[1:2, :]
    for k, x in enumerate((x0, x1, x2, x3)):
        hat, _ = norm_stats(x[...].astype(full))
        n1[k * rows : (k + 1) * rows, :] = (hat * gain + shift).astype(low)
    weights.wait()
    mixed[...] = mm(n1[...], w[...])
    for k in range(GROUP):
        here = slice(k * rows, (k + 1) * rows)
        c, s = cos[here, :], sin[here, :]
        for part in range(2):
            base = part * WIDE
            v1, v2 = mixed[here, base : base + LANES], mixed[here, base + LANES : base + WIDE]
            qkv[here, base : base + LANES] = (v1 * c - v2 * s).astype(low)
            qkv[here, base + LANES : base + WIDE] = (v2 * c + v1 * s).astype(low)
        qkv[here, 2 * WIDE :] = mixed[here, 2 * WIDE :].astype(low)
    me = sc[1]
    length = GROUP * rows
    spot = lax.broadcasted_iota(jnp.int32, (1, length), 1)
    place = jnp.zeros((1, length), jnp.int32)
    for k in range(GROUP):
        place = jnp.where(spot // rows == k, (me ^ k) * rows + spot - k * rows, place)
    seq_col = (place >= bound).astype(jnp.int32)
    for h in range(heads):
        scores[h] = mm_nt(keep(qkv[:, 0:WIDE], half_mask(h)), qkv[:, WIDE : 2 * WIDE])
    for h in range(heads):
        for k in range(GROUP):
            here = slice(k * rows, (k + 1) * rows)
            own = (me ^ k) * rows + lax.broadcasted_iota(jnp.int32, (rows, 1), 0)
            same = (own >= bound).astype(jnp.int32) == seq_col
            score = jnp.where(same, scores[h, here, :] * (HEAD_DIM**-0.5), masked_score)
            top = jnp.max(score, axis=-1, keepdims=True)
            expo = jnp.exp(score - top)
            probs[h, here, :] = (expo * (1.0 / jnp.sum(expo, axis=-1, keepdims=True))).astype(low)
    total = mm(probs[0], keep(qkv[:, 2 * WIDE :], value_mask(0)))
    for h in range(1, heads):
        total = total + mm(probs[h], keep(qkv[:, 2 * WIDE :], value_mask(h)))
    for k, out in enumerate((a0, a1, a2, a3)):
        out[...] = total[k * rows : (k + 1) * rows, : heads * HEAD_DIM].astype(low)


def attend_back_kernel(layer, heads, sc, g0, g1, g2, g3, qkv, probs, cos, sin, wo_own, wo_oth, w_own, w_oth, gmixed, p0, p1, p2, p3, wo, win, w, go, gs, qm, gom, ga, gp, sem):
    rows = g0.shape[0]
    width = heads * HEAD_DIM
    me = sc[1]
    mine = sc[0] == layer
    span = pl.ds(pl.multiple_of(me * width, HEAD_DIM), width)
    fetch_o = Fetch(wo_own, wo_oth, mine, (span, slice(None)), wo, sem.at[3])
    fetch_w = ProjectionWeights(me, heads, mine, w_own, w_oth, win, w, sem)
    fetch_o.start()
    fetch_w.start()
    length = GROUP * rows
    for k, g in enumerate((g0, g1, g2, g3)):
        ga[k * rows : (k + 1) * rows, :] = g[:, : wo.shape[1]]
    go[:, LANES:] = jnp.zeros((length, WIDE - LANES), low)
    fetch_o.wait()
    go[:, :width] = mm_nt(ga[...], wo[...]).astype(low)
    for h in range(heads):
        there = slice(h * length, (h + 1) * length)
        gom[there, :] = keep(go[...], value_mask(h))
        qm[there, :] = keep(qkv[:, 0:WIDE], half_mask(h))
        gp[h] = mm_nt(gom[there, :], qkv[:, 2 * WIDE :])
    for h in range(heads):
        for k in range(GROUP):
            here = slice(k * rows, (k + 1) * rows)
            p, g = probs[h, here, :].astype(full), gp[h, here, :]
            inner = jnp.sum(p * g, axis=-1, keepdims=True)
            gs[h * length + k * rows : h * length + (k + 1) * rows, :] = (p * (g - inner)).astype(low)
    gq = mm(gs[0:length, :], keep(qkv[:, WIDE : 2 * WIDE], half_mask(0)))
    gv = mm_tn(probs[0], gom[0:length, :])
    for h in range(1, heads):
        there = slice(h * length, (h + 1) * length)
        gq = gq + mm(gs[there, :], keep(qkv[:, WIDE : 2 * WIDE], half_mask(h)))
        gv = gv + mm_tn(probs[h], gom[there, :])
    gk = mm_tn(gs[...], qm[...])
    for base, value in ((0, gq), (WIDE, gk)):
        value = value * (HEAD_DIM**-0.5)
        v1, v2 = value[:, :LANES], value[:, LANES:]
        gmixed[:, base : base + LANES] = (v1 * cos[...] + v2 * sin[...]).astype(low)
        gmixed[:, base + LANES : base + WIDE] = (v2 * cos[...] - v1 * sin[...]).astype(low)
    gmixed[:, 2 * WIDE :] = gv.astype(low)
    fetch_w.wait()
    back = mm_nt(gmixed[...], w[...]).astype(low)
    for k, out in enumerate((p0, p1, p2, p3)):
        out[...] = back[k * rows : (k + 1) * rows, :]


class FeedWeights:
    def __init__(self, mine, up_own, up_oth, dn_own, dn_oth, wu, wd, sem, first):
        width = wu.shape[1]
        self.wu, self.wd = wu, wd
        self.up, self.down = [], []
        for j in range(GROUP):
            cut = slice(j * width, (j + 1) * width)
            self.up.append(Fetch(up_own, up_oth, mine, (slice(None), cut), wu.at[j], sem.at[first + j]))
            self.down.append(Fetch(dn_own, dn_oth, mine, (cut, slice(None)), wd.at[j], sem.at[first + GROUP + j]))


def feed_forward(sc, x, atts, norms, fetch_o, wo, feed, shards, y, hidden, slope, owner, parts, cols):
    rows, width = x.shape
    heads_wide = atts[0].shape[1]
    me = sc[1]
    for k in range(GROUP):
        fetch_o[k].wait()
    state = x[...].astype(full)
    for k in range(GROUP):
        state = state + mm(atts[k][...], wo[k])
        cols[me ^ k, :, :heads_wide] = atts[k][...]
    hidden[...] = state
    hat, _ = norm_stats(state)
    n2 = (hat * norms[2:3, :] + norms[3:4, :]).astype(low)
    step = width // (GROUP * shards)
    shares = []
    for target in range(GROUP):
        pieces = []
        for z in range(shards):
            at = (z * GROUP + target) * step
            pieces.append(cols[at // heads_wide, :, at % heads_wide : at % heads_wide + step])
        pieces.append(jnp.zeros((rows, WIDE - heads_wide), low))
        shares.append(jnp.concatenate(pieces, axis=1))
    for target in range(GROUP):
        cols[target] = shares[target]
    out = jnp.zeros((rows, width), full)
    chunk = feed.wu.shape[2]
    for j in range(GROUP):
        feed.up[j].wait()
        act, grad = gelu_both(mm(n2, feed.wu[j]))
        act = act.astype(low)
        slope[:, j * chunk : (j + 1) * chunk] = grad.astype(low)
        feed.down[j].wait()
        out = out + mm(act, feed.wd[j])
        if owner == 3:
            parts[j] = act
            continue
        span = chunk // shards
        for b in range(chunk // span):
            z, target = divmod(j * (chunk // span) + b, GROUP)
            parts[target, :, z * span : (z + 1) * span] = act[:, b * span : (b + 1) * span]
    y[...] = (hidden[...] + out).astype(low)
    return n2


def feed_back(gf, grad_out, norms, feed, hidden, slope, gas, gh, dnorm, gu, waited):
    rows, width = gf.shape
    chunk = feed.wu.shape[2]
    grad = jnp.zeros((rows, width), full)
    for j in range(GROUP):
        if not waited:
            feed.down[j].wait()
        got = mm_nt(gf, feed.wd[j]) * slope[:, j * chunk : (j + 1) * chunk].astype(full)
        got = got.astype(low)
        gu[j] = got
        if not waited:
            feed.up[j].wait()
        grad = grad + mm_nt(got, feed.wu[j])
    back, d_gain, d_shift = norm_backward(hidden[...], norms[2:3, :], grad)
    total = grad_out + back
    gh[...] = total
    for ga in gas:
        ga[:, 0:width] = total.astype(low)
    dnorm[0:1, :] = d_gain
    dnorm[1:2, :] = d_shift


def start_out(sc, mine, wo_own, wo_oth, wo, sem):
    width = wo.shape[1]
    out = []
    for k in range(GROUP):
        span = pl.ds(pl.multiple_of((sc[1] ^ k) * width, HEAD_DIM), width)
        out.append(Fetch(wo_own, wo_oth, mine, (span, slice(None)), wo.at[k], sem.at[k]))
    return out


def touch(x, spare, sem):
    copy = pltpu.make_async_copy(x.at[0 : spare.shape[0], :], spare, sem)
    copy.start()
    copy.wait()


def feed_kernel(layer, shards, sc, x, a0, a1, a2, a3, norms_own, norms_oth, wo_own, wo_oth, up_own, up_oth, dn_own, dn_oth, y, hidden, slope, m0, m1, m2, m3, wo, wu, wd, parts, cols, spare, spare_sem, sem):
    mine = sc[0] == layer
    norms = layer_norms(layer, sc, norms_own, norms_oth)
    fetch_o = start_out(sc, mine, wo_own, wo_oth, wo, sem)
    feed = FeedWeights(mine, up_own, up_oth, dn_own, dn_oth, wu, wd, sem, GROUP)
    for f in fetch_o + [f for pair in zip(feed.up, feed.down) for f in pair]:
        f.start()
    touch(x, spare, spare_sem)
    n2 = feed_forward(sc, x, (a0, a1, a2, a3), norms, fetch_o, wo, feed, shards, y, hidden, slope, 1, parts, cols)
    width = x.shape[1]
    for k, m in enumerate((m0, m1, m2, m3)):
        m[:, 0:width] = n2
        m[:, width : 2 * width] = parts[sc[1] ^ k]
        m[:, 2 * width :] = cols[sc[1] ^ k]


def feed_turn_kernel(layer, shards, owner, sc, x, a0, a1, a2, a3, norms_own, norms_oth, cot, wo_own, wo_oth, up_own, up_oth, dn_own, dn_oth, y, gh, dnorm, g0, g1, g2, g3, m0, m1, m2, m3, d0, d1, d2, d3, wo, wu, wd, parts, cols, hidden, slope, gu, sem):
    mine = sc[0] == layer
    norms = layer_norms(layer, sc, norms_own, norms_oth)
    fetch_o = start_out(sc, mine, wo_own, wo_oth, wo, sem)
    feed = FeedWeights(mine, up_own, up_oth, dn_own, dn_oth, wu, wd, sem, GROUP)
    for f in fetch_o + [f for pair in zip(feed.up, feed.down) for f in pair]:
        f.start()
    gas = (g0, g1, g2, g3)
    n2 = feed_forward(sc, x, (a0, a1, a2, a3), norms, fetch_o, wo, feed, shards, y, hidden, slope, owner, parts, cols)
    gf = cot[...]
    feed_back(gf, gf.astype(full), norms, feed, hidden, slope, gas, gh, dnorm, gu, True)
    width = x.shape[1]
    for k, (g, m, d) in enumerate(((g0, m0, d0), (g1, m1, d1), (g2, m2, d2), (g3, m3, d3))):
        g[:, width:] = cols[sc[1] ^ k]
        m[:, 0:width] = n2
        m[:, width:] = gu[sc[1] ^ k]
        d[...] = parts[sc[owner] ^ k]


def turn_kernel(layer, sc, r0, r1, r2, r3, gh_in, x_in, hidden, slope, norms_own, norms_oth, up_own, up_oth, dn_own, dn_oth, gx, dnorm_in, ga, gh, dnorm, m0, m1, m2, m3, wu, wd, gu, sem):
    mine = sc[0] == layer
    feed = FeedWeights(mine, up_own, up_oth, dn_own, dn_oth, wu, wd, sem, 0)
    for f in [f for pair in zip(feed.down, feed.up) for f in pair]:
        f.start()
    norms_in = layer_norms(layer + 1, sc, norms_own, norms_oth)
    norms = layer_norms(layer, sc, norms_own, norms_oth)
    top = first_norm_back(r0, r1, r2, r3, gh_in, x_in, norms_in, gx, dnorm_in)
    gf = top.astype(low)
    feed_back(gf, gf.astype(full), norms, feed, hidden, slope, (ga,), gh, dnorm, gu, False)
    width = gf.shape[1]
    for k, m in enumerate((m0, m1, m2, m3)):
        m[:, 0:width] = gu[sc[1] ^ k]
        m[:, width:] = gf


def first_norm_back(r0, r1, r2, r3, gh_in, x_in, norms_in, gx, dnorm):
    grad = r0[...].astype(full) + r1[...].astype(full) + r2[...].astype(full) + r3[...].astype(full)
    back, d_gain, d_shift = norm_backward(x_in[...].astype(full), norms_in[0:1, :], grad)
    dnorm[0:1, :] = d_gain
    dnorm[1:2, :] = d_shift
    total = gh_in[...] + back
    gx[...] = total
    return total


def last_kernel(sc, r0, r1, r2, r3, gh_in, x_in, norms_own, norms_oth, above, d1_1, d2_1, d2_0, kept, sent, sums, sums_sent, gx, dnorm):
    first_norm_back(r0, r1, r2, r3, gh_in, x_in, layer_norms(0, sc, norms_own, norms_oth), gx, dnorm)
    first = sc[0] == 0
    kept[...] = jnp.where(first, gx[...], above[...])
    sent[...] = jnp.where(first, above[...], gx[...])
    for at, zero, one in ((0, dnorm, d1_1), (2, d2_0, d2_1)):
        sums[at : at + 2, :] = jnp.where(first, zero[...], one[...])
        sums_sent[at : at + 2, :] = jnp.where(first, one[...], zero[...])


def gather_rows(pieces, at, target, half, section, sems):
    rows, width = pieces[0].shape[0], target.shape[1]
    copies = []
    for k, piece in enumerate(pieces):
        here = pl.ds(k * rows, rows)
        if half is None:
            copies.append(pltpu.make_async_copy(piece.at[:, pl.ds(at, width)], target.at[here, :], sems.at[k]))
            continue
        for i, part in enumerate((section, 1 - section)):
            source = pl.ds(pl.multiple_of(at + part * half, LANES), half)
            copies.append(pltpu.make_async_copy(piece.at[:, source], target.at[here, pl.ds(i * half, half)], sems.at[2 * k + i]))
    for copy in copies:
        copy.start()
    return copies


def tall_product(left, right, stay, go, base, step):
    half = stay.shape[1]
    for i in range(left.shape[1] // step):
        cut, put = slice(i * step, (i + 1) * step), slice(base + i * step, base + (i + 1) * step)
        product = mm_tn(left[:, cut], right[...]).astype(low)
        stay[put, :] = product[:, :half]
        go[put, :] = product[:, half:]


def pair_grads_kernel(places, sc, *refs):
    count = len(places)
    outs, (a, b, sem) = refs[2 * GROUP * count : -3], refs[-3:]
    half = outs[0].shape[1]
    copies = []
    for i, (at_left, at_right) in enumerate(places):
        lefts, rights = refs[2 * GROUP * i :][:GROUP], refs[2 * GROUP * i + GROUP :][:GROUP]
        copies.append(
            gather_rows(lefts, at_left, a.at[i], None, None, sem.at[2 * i]) + gather_rows(rights, at_right, b.at[i], half, sc[0], sem.at[2 * i + 1])
        )
    for i in range(count):
        for copy in copies[i]:
            copy.wait()
        tall_product(a.at[i], b.at[i], outs[2 * i], outs[2 * i + 1], 0, WIDE)


def padding_place(lane):
    part, u = lane // WIDE, lane & (WIDE - 1)
    v = u & (LANES - 1)
    used, half = 3 * HALF, WIDE - HEAD_DIM
    turned = jnp.where(v >= used, part * HEAD_DIM + (u // LANES) * HALF + v - used, -1)
    plain = jnp.where(u >= half, 2 * HEAD_DIM + u - half, -1)
    return jnp.where(part < 2, turned, plain)


def attend_grads_kernel(at_att, fold, sc, n1, gmixed, m0, m1, m2, m3, g0, g1, g2, g3, stay, go, left, right, a, b, sem):
    width, half = b.shape[1], stay.shape[1]
    first = gather_rows((n1,), 0, left, None, None, sem.at[0]) + gather_rows((gmixed,), 0, right, half, sc[0], sem.at[1])
    second = gather_rows((m0, m1, m2, m3), at_att, a, None, None, sem.at[2])
    second += gather_rows((g0, g1, g2, g3), 0, b, None if fold else half, sc[0], sem.at[3])
    for copy in first:
        copy.wait()
    tall_product(left, right, stay, go, 0, WIDE)
    for copy in second:
        copy.wait()
    if not fold:
        product = mm_tn(a[...], b[...])[: stay.shape[0] - width, :].astype(low)
        stay[width:, :] = product[:, :half]
        go[width:, :] = product[:, half:]
        return
    mine_wide = 3 * HEAD_DIM
    product = mm_tn(a[...], b[...])[:mine_wide, :].astype(low)
    shape = (mine_wide, 2 * half)
    lane = lane_index(shape)
    lane = jnp.where(lane < half, lane + sc[0] * half, lane - sc[0] * half)
    spread = jnp.where(lax.broadcasted_iota(jnp.int32, shape, 0) == padding_place(lane), 1.0, 0.0).astype(low)
    few = mine_wide // GROUP
    for q in range(GROUP):
        put = mm(product[:, q * mine_wide : (q + 1) * mine_wide], spread).astype(low)
        for z in range(GROUP):
            at = slice(z * mine_wide + q * few, z * mine_wide + (q + 1) * few)
            stay[at, :] = stay[at, :] + put[z * few : (z + 1) * few, :half]
            go[at, :] = go[at, :] + put[z * few : (z + 1) * few, half:]


def add_kernel(sizes, *refs):
    count = len(sizes)
    mine, theirs = refs[:count], refs[count : 2 * count]
    norms = refs[2 * count] if len(refs) > 2 * count + 1 else None
    out = refs[-1]
    blocks, total, half = out.shape
    for b in range(blocks):
        at = 0
        for x, y, size in zip(mine, theirs, sizes):
            base = 0
            for part in size:
                step = part // blocks
                span = slice(base + b * step, base + (b + 1) * step)
                out[b, at : at + step, :] = (x[span, :].astype(full) + y[span, :].astype(full)).astype(low)
                at += step
                base += part
        if norms is not None:
            row = lax.broadcasted_iota(jnp.int32, (total - at, half), 0)
            lower, upper = norms[b : b + 1, :half], norms[b : b + 1, half:]
            out[b, at:, :] = jnp.where(row == 0, lower, jnp.where(row == 1, upper, 0.0)).astype(low)


def split_kernel(axis, sizes, sc, mine, theirs, stay, go):
    for out, flip in ((stay, 0), (go, 1)):
        for j in range(2):
            block = 2 * j + ((sc[axis] & 1) ^ flip)
            at, base = 0, 0
            for size in sizes:
                step = size // GROUP
                span = pl.ds(pl.multiple_of(base + block * step, 16), step)
                out[j, at : at + step, :] = (mine[span, :].astype(full) + theirs[span, :].astype(full)).astype(low)
                at += step
                base += size


def halve_kernel(axis, sc, held, got, stay, go):
    high = sc[axis] >> 1
    stay[...] = held[high].astype(full) + got[high].astype(full)
    go[...] = (held[1 - high].astype(full) + got[1 - high].astype(full)).astype(low)


def attend_pack_kernel(sc, att_0, grads_1, stay, go):
    first = sc[0] == 0
    zero, one = att_0[...], grads_1[0 : att_0.shape[0], :]
    stay[...] = jnp.where(first, zero, one)
    go[...] = jnp.where(first, one, zero)


def feed_pack_kernel(grads_1, down_1, down_1_got, out):
    split = down_1.shape[0]
    out[0:split, :] = grads_1[split:, :]
    out[split:, :] = (down_1[...] + down_1_got[...].astype(full)).astype(low)


def spread_rows(out, values, start, stride):
    for j in range(values.shape[1] // LANES):
        out[pl.ds(start + j, values.shape[0], stride=stride), :] = values[:, j * LANES : (j + 1) * LANES]


def join_halves(sc, whole, mine, theirs):
    half = mine.shape[1]
    whole[:, pl.ds(pl.multiple_of(sc[0] * half, LANES), half)] = mine[...].astype(full)
    whole[:, pl.ds(pl.multiple_of((1 - sc[0]) * half, LANES), half)] = theirs[...].astype(full)


def attend_finish_kernel(sc, mine, theirs, grad_out, v0, v1, v2, v3, whole, out):
    join_halves(sc, whole, mine, theirs)
    width = whole.shape[1]
    step = width // GROUP
    few = step // GROUP
    shape = (width, step)
    gather = jnp.where(padding_place(lax.broadcasted_iota(jnp.int32, shape, 0)) == lane_index(shape), 1.0, 0.0).astype(low)
    for q in range(GROUP):
        out[:, q * step : (q + 1) * step] = mm(whole[q * few : (q + 1) * few, :].astype(low), gather)
    spread_rows(grad_out, out[...], 0, width // LANES)
    for k, v in enumerate((v0, v1, v2, v3)):
        v[...] = whole[pl.ds(pl.multiple_of((sc[1] ^ k) * few, few), few), :].astype(low)


def qkv_place_kernel(heads, sc, v0, v1, v2, v3, grad_qkv, natural, whole):
    mine_wide = heads * HEAD_DIM
    shape = (WIDE, WIDE)
    source, out = lax.broadcasted_iota(jnp.int32, shape, 0), lane_index(shape)
    v = source & (LANES - 1)
    column = jnp.where(v < heads * HALF, (v // HALF) * HEAD_DIM + (source // LANES) * HALF + (v & (HALF - 1)), -1)
    back = jnp.where(out == column, 1.0, 0.0).astype(low)
    for k, piece in enumerate((v0, v1, v2, v3)):
        for part in range(3):
            values = piece[:, part * WIDE : (part + 1) * WIDE]
            natural[sc[1] ^ k, :, part * WIDE : (part + 1) * WIDE] = values.astype(full) if part == 2 else mm(values, back)
    for part in range(3):
        for c in range(GROUP):
            to = (part * GROUP + c) * mine_wide
            whole[:, to : to + mine_wide] = natural[c, :, part * WIDE : part * WIDE + mine_wide]
    spread_rows(grad_qkv, whole[...], 0, whole.shape[1] // LANES)


def feed_finish_kernel(sc, mine, theirs, feed_0, feed_0_got, grad_down, u0, u1, u2, u3, whole):
    join_halves(sc, whole, mine, theirs)
    half = mine.shape[1]
    width = 2 * half
    step = width // GROUP
    few = step // GROUP

    @pl.when(sc[0] == 0)
    def _():
        whole[:, 0:half] = feed_0[0 : 2 * step, :].astype(full)
        whole[:, half:] = feed_0_got[0 : 2 * step, :].astype(full)

    last = jnp.concatenate([feed_0[2 * step : 2 * step + 1, :], feed_0[2 * step + 1 : 2 * step + 2, :]], axis=1)
    shares = [last[:, c * step : (c + 1) * step] for c in range(GROUP)]
    for k, u in enumerate((u0, u1, u2, u3)):
        u[0:few, :] = whole[pl.ds(pl.multiple_of((sc[1] ^ k) * few, few), few), :].astype(low)
        share = jnp.zeros_like(shares[0])
        for c in range(GROUP):
            share = jnp.where((sc[1] ^ k) == c, shares[c], share)
        u[few:, :] = jnp.zeros((u.shape[0] - few, width), low)
        u[few : few + 1, :step] = share
    spread_rows(grad_down, whole[step:, :], 0, width // LANES)


def up_place_kernel(sc, u0, u1, u2, u3, grad_up, grad_norms):
    step = grad_norms.shape[1]
    few = step // GROUP
    per = u0.shape[1] // LANES
    norm = jnp.zeros((1, step), full)
    for k, u in enumerate((u0, u1, u2, u3)):
        spread_rows(grad_up, u[0:few, :].astype(full), (sc[1] ^ k) * per, GROUP * per)
        norm = norm + u[few : few + 1, :step].astype(full)
    grad_norms[...] = norm


class Late:
    def __init__(self, source, held, sem):
        self.copy, self.held, self.shape, self.here = pltpu.make_async_copy(source, held, sem), held, held.shape, False
        self.copy.start()

    def __getitem__(self, index):
        if not self.here:
            self.copy.wait()
            self.here = True
        return self.held[index]


def run(kernel, shapes, scratch, operands, spaces):
    place = {"s": pltpu.SMEM, "v": pltpu.VMEM, "a": pl.ANY, "h": pltpu.HBM}
    total = len(operands) + len(shapes) + len(scratch)
    late = [i for i, space in enumerate(spaces) if space == "h"]
    held = [pltpu.VMEM(operands[i].shape, operands[i].dtype) for i in late]

    def body(*refs):
        given = list(refs[:total])
        for n, i in enumerate(late):
            given[i] = Late(given[i], refs[total + n], refs[-1].at[n])
        kernel(*given)
        for i in late:
            given[i][...]

    return pl.pallas_call(
        body,
        out_shape=[jax.ShapeDtypeStruct(shape, kind) for shape, kind in shapes],
        in_specs=[pl.BlockSpec(memory_space=place[space]) for space in spaces],
        out_specs=[pl.BlockSpec(memory_space=pltpu.VMEM) for _ in shapes],
        scratch_shapes=[*scratch, *held, pltpu.SemaphoreType.DMA((len(held),))] if held else scratch,
        compiler_params=pltpu.CompilerParams(vmem_limit_bytes=52 * 2**20),
        cost_estimate=pl.CostEstimate(flops=1, bytes_accessed=1, transcendentals=0),
    )(*operands)


def exchange(value):
    values = value if isinstance(value, (list, tuple)) else [value] * GROUP
    return [values[0]] + [
        lax.ppermute(values[k], "ctx", [(i, i ^ k) for i in range(GROUP)]) for k in range(1, GROUP)
    ]


def towards(value, k):
    return lax.ppermute(value, "ctx", [(i, i ^ k) for i in range(GROUP)])


def along(value, k):
    count = lax.axis_size("dp")
    return lax.ppermute(value, "dp", [(i, i ^ k) for i in range(count)])


def swap(value):
    return lax.ppermute(value, "section", [(0, 1), (1, 0)])


def together(*values):
    return lax.optimization_barrier(values)


def on_device(tokens, cotangent, seq_bound, ln1_gain, ln1_shift, w_qkv, w_out, ln2_gain, ln2_shift, w_up, w_down):
    section = lax.axis_index("section")
    me = lax.axis_index("ctx")
    shards = lax.axis_size("dp")
    z = lax.axis_index("dp")
    rows, width = tokens.shape[1:]
    feed_width = w_up.shape[2]
    chunk = feed_width // GROUP
    heads = width // HEAD_DIM // GROUP
    mine_wide = heads * HEAD_DIM
    length = GROUP * rows
    few = width // (GROUP * shards)
    sc = jnp.stack([section, me, section, z]).astype(jnp.int32)

    dma = pltpu.SemaphoreType.DMA
    vm = pltpu.VMEM
    piece = ((rows, width), low)
    wide_piece = ((rows, width), full)
    pair = ((2, width), full)

    x = lax.dynamic_index_in_dim(tokens, section, 0, keepdims=False)
    gathered = exchange(x)
    wq_own, wo_own, up_own, dn_own = w_qkv[0], w_out[0], w_up[0], w_down[0]
    wq_oth, wo_oth = swap(wq_own), swap(wo_own)
    norms_own = jnp.concatenate([ln1_gain, ln1_shift, ln2_gain, ln2_shift], axis=0)
    wo_oth, later = together(wo_oth, norms_own)
    norms_oth = swap(later)
    wq_oth, norms_oth, later = together(wq_oth, norms_oth, up_own)
    up_oth = swap(later)
    *gathered, later = together(*gathered, dn_own)
    dn_oth = swap(later)

    def attend(layer, gathered, *tables):
        table = ((length, LANES), full)
        given = len(tables)
        return run(
            functools.partial(attend_kernel, layer, heads),
            [table] * (2 - given) + [((length, width), low), ((length, 3 * WIDE), low), ((heads, length, length), low)] + [((rows, mine_wide), low)] * GROUP,
            [vm((3, width, WIDE), low), vm((width, 3 * WIDE), low), vm((length, 3 * WIDE), full), vm((heads, length, length), full), dma((3,))],
            (sc, seq_bound, *gathered, norms_own, norms_oth, *tables, wq_own, wq_oth),
            "ssvvvvvv" + "v" * given + "aa",
        )

    def attend_back(layer, grads, qkv, probs):
        return run(
            functools.partial(attend_back_kernel, layer, heads),
            [((length, 3 * WIDE), low)] + [piece] * GROUP,
            [
                vm((mine_wide, width), low), vm((3, width, WIDE), low), vm((width, 3 * WIDE), low), vm((length, WIDE), low),
                vm((heads * length, length), low), vm((heads * length, WIDE), low), vm((heads * length, WIDE), low),
                vm((length, width), low), vm((heads, length, length), full), dma((4,)),
            ],
            (sc, *grads, qkv, probs, cos, sin, wo_own, wo_oth, wq_own, wq_oth),
            "svvvvvvvvaaaa",
        )

    half = width // 2
    small = shards == GROUP
    square, attend_size = (width,), (width,) if small else (width, mine_wide)

    def pair_grads(*products):
        out = ((width, half), low)
        operands = [piece for lefts, rights, _, _ in products for piece in (*lefts, *rights)]
        places = [(at_left, at_right) for _, _, at_left, at_right in products]
        return run(
            functools.partial(pair_grads_kernel, places),
            [out] * (2 * len(products)),
            [vm((len(products), length, width), low), vm((len(products), length, width), low), dma((2 * len(products), 2 * GROUP))],
            (sc, *operands), "s" + "a" * len(operands),
        )

    def attend_grads(n1, gmixed, fwd, ga, at_att):
        return run(
            functools.partial(attend_grads_kernel, at_att, small),
            [((sum(attend_size), half), low)] * 2,
            [vm((length, width), low), vm((length, 3 * WIDE), low), vm((length, WIDE), low), vm((length, width), low), dma((4, 2 * GROUP))],
            (sc, n1, gmixed, *fwd, *ga), "s" + "a" * (2 + 2 * GROUP),
        )


    def blocks_of(sizes, mine, theirs, *norms):
        total = sum(sum(size) for size in sizes) // shards + (16 if norms else 0)
        if small:
            (blocks,) = run(
                functools.partial(add_kernel, sizes), [((shards, total, half), low)], [], (*mine, *theirs, *norms),
                "v" * (2 * len(mine) + len(norms)),
            )
        else:
            parts = []
            for x, y, size in zip(mine, theirs, sizes):
                value = (x.astype(full) + y.astype(full)).astype(low)
                base = 0
                for part in size:
                    parts.append(value[base : base + part].reshape(shards, part // shards, half))
                    base += part
            blocks = jnp.concatenate(parts, axis=1)
        return blocks

    def over_dp(blocks):
        return lax.psum_scatter(blocks, "dp", scatter_dimension=0, tiled=False)

    def split(axis, sizes, mine, theirs):
        part = ((2, sum(sizes) // GROUP, half), low)
        return run(functools.partial(split_kernel, axis, sizes), [part, part], [], (sc, mine, theirs), "svv")

    def halve(axis, stay, got):
        part = stay.shape[1:]
        return run(functools.partial(halve_kernel, axis), [(part, full), (part, low)], [], (sc, stay, got), "svv")

    def level(token, *values):
        token, *values = together(token, *values)
        return together(swap(token), *values)[1:]

    feed_scratch = [vm((GROUP, width, chunk), low), vm((GROUP, chunk, width), low)]
    out_scratch = vm((GROUP, mine_wide, width), low)
    split_scratch = [vm((GROUP, rows, chunk), low), vm((GROUP, rows, WIDE), low)]
    owner, other_way = (3, along) if small else (1, towards)

    cos, sin, n1_0, qkv_0, probs_0, *att = attend(0, gathered)
    att = exchange(att)
    weights = (wo_own, wo_oth, up_own, up_oth, dn_own, dn_oth)
    cot = lax.dynamic_index_in_dim(cotangent, section, 0, keepdims=False)
    *att, cot = together(*att, cot)
    y0, hidden_0, slope_0, *fwd_0 = run(
        functools.partial(feed_kernel, 0, shards),
        [piece, wide_piece, ((rows, feed_width), low)] + [((rows, 2 * width + WIDE), low)] * GROUP,
        [out_scratch, *feed_scratch, *split_scratch, vm((16, width), low), dma, dma((3 * GROUP,))],
        (sc, x, *att, norms_own, norms_oth, *weights),
        "svvvvvvvaaaaaa",
    )
    gathered_1 = exchange(y0)
    cots = [cot, other_way(cot, 1), None, other_way(cot, 3)]
    *gathered_1, fwd_0[1], fwd_0[2], cots[1], cots[3] = together(*gathered_1, fwd_0[1], fwd_0[2], cots[1], cots[3])
    fwd_0[1], fwd_0[2] = towards(fwd_0[1], 1), towards(fwd_0[2], 2)
    n1_1, qkv_1, probs_1, *att = attend(1, gathered_1, cos, sin)
    att = exchange(att)
    *att, fwd_0[1], fwd_0[2], fwd_0[3] = together(*att, *fwd_0[1:])
    fwd_0[3] = towards(fwd_0[3], 3)
    y1, gh_1, dn2_1, *rest = run(
        functools.partial(feed_turn_kernel, 1, shards, owner),
        [piece, wide_piece, pair] + [((rows, width + WIDE), low)] * GROUP + [((rows, 2 * width), low)] * GROUP + [piece] * GROUP,
        [
            out_scratch, *feed_scratch, *split_scratch, vm((rows, width), full), vm((rows, feed_width), low),
            vm((GROUP, rows, chunk), low), dma((3 * GROUP,)),
        ],
        (sc, y0, *att, norms_own, norms_oth, cot, *weights),
        "svvvvvvvvaaaaaa",
    )
    ga, up_1, down_1 = rest[:GROUP], rest[GROUP : 2 * GROUP], rest[2 * GROUP :]
    *ga, fwd_0[3] = together(*ga, fwd_0[3])
    ga_1 = exchange(ga)
    *ga_1, cots[2], down_1[1], down_1[3], up_1[1], up_1[2] = together(*ga_1, cot, down_1[1], down_1[3], up_1[1], up_1[2])
    cots[2] = other_way(cots[2], 2)
    up_1[1], up_1[2] = towards(up_1[1], 1), towards(up_1[2], 2)
    gmixed_1, *back = attend_back(1, ga_1, qkv_1, probs_1)
    *back, up_1[1], up_1[2], up_1[3], down_1[1], down_1[3], cots[2] = together(*back, *up_1[1:], down_1[1], down_1[3], cots[2])
    back = exchange(back)
    down_1[1], down_1[3] = other_way(down_1[1], 1), other_way(down_1[3], 3)
    att_1, att_1_go = attend_grads(n1_1, gmixed_1, ga_1, ga_1, width)
    *back, down_1[1], down_1[2], down_1[3], up_1[3], att_1, att_1_go = together(*back, *down_1[1:], up_1[3], att_1, att_1_go)
    down_1[2] = other_way(down_1[2], 2)
    up_1[3] = towards(up_1[3], 3)
    att_1_got = swap(att_1_go)
    gx_1, dn1_1, ga, gh_0, dn2_0, *bwd_0 = run(
        functools.partial(turn_kernel, 0),
        [wide_piece, pair, piece, wide_piece, pair] + [((rows, 2 * width), low)] * GROUP,
        [*feed_scratch, vm((GROUP, rows, chunk), low), dma((2 * GROUP,))],
        (sc, *back, gh_1, y0, hidden_0, slope_0, norms_own, norms_oth, up_own, up_oth, dn_own, dn_oth),
        "svvvvvvvvvvaaaa",
    )
    gh_0, att_1_got, up_1[3], down_1[2] = together(gh_0, att_1_got, up_1[3], down_1[2])
    ga_0 = exchange(ga)
    up_1_stay, up_1_go = pair_grads((up_1, up_1, 0, width))
    up_1_got = swap(up_1_go)
    grads_1 = blocks_of([attend_size, square], [att_1, up_1_stay], [att_1_got, up_1_got])
    *ga_0, grads_1, bwd_0[1], bwd_0[2] = together(*ga_0, grads_1, bwd_0[1], bwd_0[2])
    sum_1 = over_dp(grads_1)
    bwd_0[1], bwd_0[2] = towards(bwd_0[1], 1), towards(bwd_0[2], 2)
    gmixed_0, *back = attend_back(0, ga_0, qkv_0, probs_0)
    gmixed_0, *back, bwd_0[1], bwd_0[2], bwd_0[3] = together(gmixed_0, *back, *bwd_0[1:])
    bwd_0[3] = towards(bwd_0[3], 3)
    att_0, att_0_go = attend_grads(n1_0, gmixed_0, fwd_0, ga_0, 2 * width)
    att_0_got = swap(att_0_go)
    *back, att_0, att_0_got = together(*back, att_0, att_0_got)
    back = exchange(back)
    sum_0 = over_dp(blocks_of([attend_size], [att_0], [att_0_got]))
    down_1_stay, down_1_go = pair_grads((down_1, cots, 0, 0))
    bwd_0[3], down_1_stay, down_1_go = together(bwd_0[3], down_1_stay, down_1_go)
    up_0, up_0_go, down_0, down_0_go = pair_grads((fwd_0, bwd_0, 0, 0), (fwd_0, bwd_0, width, width))
    *back, up_0, up_0_go, down_0, down_0_go = together(*back, up_0, up_0_go, down_0, down_0_go)
    up_0_got, down_0_got, down_1_got = swap(up_0_go), swap(down_0_go), swap(down_1_go)
    kept, sent, sums, sums_sent = run(
        last_kernel, [wide_piece, wide_piece, ((4, width), full), ((4, width), full)],
        [vm((rows, width), full), vm((2, width), full)],
        (sc, *back, gh_0, x, norms_own, norms_oth, gx_1, dn1_1, dn2_1, dn2_0), "svvvvvvvvvvvv",
    )
    y_own, y_got = jnp.where(section == 0, y0, y1), swap(jnp.where(section == 0, y1, y0))
    sums, sums_sent, up_0_got, down_0_got, down_1_got, sum_1, y_got = together(sums, sums_sent, up_0_got, down_0_got, down_1_got, sum_1, y_got)
    sums_got = swap(sums_sent)
    sums = sums + sums_got
    if small:
        grads_0 = blocks_of([square, square], [up_0, down_0], [up_0_got, down_0_got], sums)
        sum_feed_0 = over_dp(grads_0)
    if small:
        tall = width // shards
        lanes = width // LANES
        one, two = ((tall, half), low), ((2 * tall, half), low)
        down_1_stay, down_1_go = split(1, square, down_1_stay, down_1_got)
        down_1_got = towards(down_1_go, 1)
        att, att_go = run(attend_pack_kernel, [one, one], [], (sc, sum_0, sum_1), "shh")
        grad_out, *pieces = run(
            attend_finish_kernel, [((few * lanes, LANES), full)] + [((few, width), low)] * GROUP,
            [vm((tall, width), full), vm((few, width), full)], (sc, att, swap(att_go)), "svv",
        )
        down_1_got, grad_out, *pieces = together(down_1_got, grad_out, *pieces)
        down_1_stay, down_1_go = halve(1, down_1_stay, down_1_got)
        down_1_got = towards(down_1_go, 2)
        pieces = exchange(pieces)
        down_1_got, *pieces = together(down_1_got, *pieces)
        (feed,) = run(feed_pack_kernel, [two], [], (sum_1, down_1_stay, down_1_got), "hvv")
        feed_got = lax.ppermute(feed, "section", [(0, 1)])
        (grad_qkv,) = run(
            functools.partial(qkv_place_kernel, heads), [((few * 3 * lanes, LANES), full)],
            [vm((GROUP, few, 3 * WIDE), full), vm((few, 3 * width), full)], (sc, *pieces), "s" + "v" * GROUP,
        )
        sum_feed_0, grad_out, grad_qkv, feed_got = together(sum_feed_0, grad_out, grad_qkv, feed_got)
        grad_down, *pieces = run(
            feed_finish_kernel, [((tall * lanes, LANES), full)] + [((few + 16, width), low)] * GROUP, [vm((2 * tall, width), full)],
            (sc, feed, feed_got, sum_feed_0, lax.ppermute(sum_feed_0, "section", [(1, 0)])), "svvvv",
        )
        grad_up, grad_norms = run(
            up_place_kernel, [((few * GROUP * lanes, LANES), full), ((1, mine_wide), full)], [], (sc, *exchange(pieces)), "s" + "v" * GROUP,
        )
    else:
        sum_feed_0 = over_dp(blocks_of([square, square], [up_0, down_0], [up_0_got, down_0_got]))
        sum_down_1 = over_dp(blocks_of([square], [down_1_stay], [down_1_got]))
        grad_up, grad_down, grad_out, grad_qkv = many_shards(
            me, section, heads, few, jnp.concatenate([sum_0, sum_feed_0]), jnp.concatenate([sum_1, sum_down_1])
        )
        grad_norms = lax.psum_scatter(sums.reshape(shards * GROUP, -1), ("dp", "ctx"), scatter_dimension=0, tiled=True)

    def by_section(own, got):
        return jnp.where(section == 0, jnp.stack([own, got]), jnp.stack([got, own]))[None]

    return (
        by_section(y_own, y_got),
        by_section(kept, swap(sent)),
        grad_qkv.reshape(1, -1),
        grad_out.reshape(1, -1),
        grad_up.reshape(1, -1),
        grad_down.reshape(1, -1),
        grad_norms.reshape(1, -1),
    )


def many_shards(me, section, heads, few, first, second):
    own, other = jnp.where(section == 0, first, second), jnp.where(section == 0, second, first)
    got = swap(other)
    whole = jnp.where(section == 0, jnp.concatenate([own, got], axis=1), jnp.concatenate([got, own], axis=1))
    width = whole.shape[1]
    chunk, tall = width, GROUP * few
    t_qkv, t_out, t_up, t_down = whole[:tall], whole[tall : tall + few], whole[tall + few : 2 * tall + few], whole[2 * tall + few :]
    slim = jnp.concatenate([t_up, t_qkv], axis=1)
    slim = slim.reshape(GROUP, slim.shape[0] // GROUP, slim.shape[1])
    gets = jnp.stack(exchange([lax.dynamic_index_in_dim(slim, me ^ k, 0, keepdims=False) for k in range(GROUP)]))
    gets = jnp.stack([lax.dynamic_index_in_dim(gets, me ^ k, 0, keepdims=False) for k in range(GROUP)]).astype(full)
    few = gets.shape[1]
    grad_up = jnp.transpose(gets[:, :, :chunk], (1, 0, 2))
    cols = gets[:, :, chunk:].reshape(GROUP, few, 3, WIDE)
    turned = cols[:, :, :2].reshape(GROUP, few, 2, 2, LANES)[..., : heads * HALF]
    turned = turned.reshape(GROUP, few, 2, 2, heads, HALF).transpose(1, 2, 0, 4, 3, 5).reshape(few, 2 * width)
    plain = cols[:, :, 2, : heads * HEAD_DIM].transpose(1, 0, 2).reshape(few, width)
    return grad_up, t_down.astype(full), t_out.astype(full), jnp.concatenate([turned, plain], axis=1)


def solution(mesh):
    in_specs = (
        P(None, ("dp", "ctx"), None),
        P(None, ("dp", "ctx"), None),
        P("dp", None),
        P("section", None),
        P("section", None),
        P("section", None, None),
        P("section", None, None),
        P("section", None),
        P("section", None),
        P("section", None, None),
        P("section", None, None),
    )
    out_specs = (
        P("section", None, ("dp", "ctx"), None),
        P("section", None, ("dp", "ctx"), None),
        P("section", ("dp", "ctx")),
        P("section", ("dp", "ctx")),
        P("section", ("dp", "ctx")),
        P("section", ("dp", "ctx")),
        P("section", ("dp", "ctx")),
    )
    return jax.shard_map(
        on_device, mesh=mesh, in_specs=in_specs, out_specs=out_specs, check_vma=False
    )
```
